32 devices in a mesh: elem: 4 (over z), clus: 8 (over y, x, core).
Axes of the slice: x: 2, y: 2, z: 4, core: 2. Of those that a mesh axis runs over, the one named last changes fastest.
Arguments:
- nodal: float32 [512, 8192], P(None, ('elem', 'clus')), may hold values from -6 to 6
- metric: bfloat16 [3, 512, 8192], P(None, None, ('elem', 'clus')), may hold values from 0.25 to 2.5
- derivative: float32 [8, 8], replicated, may hold values from -2 to 2
- interp: float32 [2, 8, 8], replicated, may hold values from -2 to 2
- face_level: int32 [49152], P(('elem', 'clus')), may hold values from 0 to 4
- face_target: int32 [49152], P(('elem', 'clus')), may hold values from 0 to 895, as said below
- slot_mortar: int32 [12288], P(('elem', 'clus')), may hold values from 0 to 511
- vertex_ids: int32 [8, 8192], P(None, ('elem', 'clus')), may hold values from 0 to 1023, as said below
Outputs:
- applied: float32 [512, 8192], P(None, ('elem', 'clus'))
The draws below stay inside these ranges and needn't reach their ends.
Inputs may be any that keep to these rules, and one draw needn't show every extreme that they name: `face_target`: A value below 512 names a mortar of the face's own device; a value 512 + s names slot s of that device's outgoing buffer, laid out as in the reference program. No two faces of one device name the same slot, and on some device every slot is named. `vertex_ids`: the coarse vertices of the elements on elem index e lie in e * 256 to e * 256 + 2 * 256 - 1, taken modulo 1024.
All inputs are finite; a program needn't handle non-finite values.
Results may differ from the reference program's by a relative error of at most 0.0003.
Values sent between devices are 32-bit elements; how exact they have to be, the bound alone decides.
No kernel may reach another device: no remote copies, remote signals or barrier semaphores. Data moves between devices by JAX's collectives and lax.ppermute only.
A program may use at most 64 MiB of HBM per device.

```python
import math
import jax
import jax.numpy as jnp
from jax import lax

POINTS = 8
E_DEV = 256
CAP_E = 128
CAP_C = 16
GROUP = 8
SLOTS = 384
M_DEV = 512
NV_DEV = 256
NV = 1024
ELEMENTS = 8192
FACES = 49152
SLOTS_ALL = 12288
N_ELEM = 4
N_CLUS = 8


def one_device(key, fill_level):
    key_used, key_order, key_local = jax.random.split(key, 3)
    slot_used = jax.random.randint(key_used, (SLOTS,), 0, 4) < fill_level
    slot_order = jnp.argsort(jnp.where(slot_used, 0, SLOTS) + jnp.arange(SLOTS))
    used_count = jnp.sum(slot_used.astype(jnp.int32))
    face_order = jax.random.permutation(key_order, 6 * E_DEV)
    face_rank = jnp.argsort(face_order)
    local_mortar = jax.random.randint(key_local, (6 * E_DEV,), 0, M_DEV)
    sent_slot = M_DEV + slot_order[jnp.minimum(face_rank, SLOTS - 1)]
    return jnp.where(face_rank < used_count, sent_slot, local_mortar).astype(jnp.int32)


def draw_face_target(key, part):
    devices = ELEMENTS // E_DEV
    key_fill, key_full, key_each = jax.random.split(key, 3)
    fill_level = jax.random.randint(key_fill, (devices,), 1, 5)
    full_device = jax.random.randint(key_full, (), 0, devices)
    fill_level = jnp.where(jnp.arange(devices) == full_device, 4, fill_level)
    return jax.vmap(one_device)(jax.random.split(key_each, devices), fill_level).reshape(-1)


def draw_vertex_ids(key, part):
    positions = jnp.arange(ELEMENTS)
    elem_of = positions // E_DEV // GROUP
    offsets = jax.random.randint(key, (8, ELEMENTS), 0, 2 * NV_DEV)
    first_one = positions % E_DEV == 0
    offsets = offsets.at[0].set(jnp.where(first_one, 2 * NV_DEV - 1, offsets[0]))
    offsets = offsets.at[1].set(jnp.where(first_one, 0, offsets[1]))
    return jnp.mod(elem_of[None, :] * NV_DEV + offsets, NV).astype(jnp.int32)


def plant(values, key, least, high):
    extent = values.shape
    spot = [jax.random.randint(jax.random.fold_in(key, axis), (), 0, extent[axis]) for axis in range(len(extent))]
    values = values.at[tuple(spot)].set(least)
    longest = extent.index(max(extent))
    spot[longest] = (spot[longest] + 1) % extent[longest]
    return values.at[tuple(spot)].set(high)


def level_of(own_key, dims, pieces, least, top_value):
    def one(position, blocks):
        steps = jax.random.uniform(jax.random.fold_in(jax.random.fold_in(own_key, 6), position), (blocks,), jnp.float32, least / len(pieces), top_value / len(pieces))
        return jnp.repeat(jnp.exp(steps), dims[position] // blocks).reshape((-1,) + (1,) * (len(dims) - position - 1))

    gain = one(*pieces[0])
    for cut in pieces[1:]:
        gain = gain * one(*cut)
    return gain


def scatter_about(key, extent, scale, bound, cuts=(), kind=jnp.bfloat16):
    values = jax.random.normal(key, extent, jnp.float32) * scale
    if len(cuts) > 0:
        values = level_of(key, extent, cuts, -0.22, 0.18) * values
    return jnp.clip(values, min=-bound, max=bound).astype(kind)


def setup_inputs(seed: int = 0) -> dict:
    streams_of = jax.random.split(jax.random.key(seed), 9)
    nodal = scatter_about(streams_of[0], (POINTS ** 3, ELEMENTS), 1.0, 6.0, ((1, 32),), jnp.float32)
    metric = jnp.clip(jnp.exp(math.log(2.5) - 2.3025851 * jax.random.uniform(streams_of[1], (3, POINTS ** 3, ELEMENTS), jnp.float32) ** level_of(streams_of[1], (3, POINTS ** 3, ELEMENTS), ((2, 32),), -0.2, 0.2)), 0.25, 2.5).astype(jnp.bfloat16)
    derivative = scatter_about(streams_of[2], (POINTS, POINTS), POINTS ** -0.5, 2.0, (), jnp.float32)
    interp = scatter_about(streams_of[3], (2, POINTS, POINTS), POINTS ** -0.5, 2.0, (), jnp.float32)
    face_level = plant(jax.random.randint(streams_of[4], (FACES,), 0, 5), jax.random.fold_in(streams_of[4], 1), 0, 4).astype(jnp.int32)
    face_target = draw_face_target(jax.random.fold_in(streams_of[8], 71), 0)
    slot_mortar = plant(jax.random.randint(streams_of[6], (SLOTS_ALL,), 0, M_DEV), jax.random.fold_in(streams_of[6], 1), 0, M_DEV - 1).astype(jnp.int32)
    vertex_ids = draw_vertex_ids(jax.random.fold_in(streams_of[8], 71), 0)
    return {"nodal": nodal, "metric": metric, "derivative": derivative, "interp": interp, "face_level": face_level, "face_target": face_target, "slot_mortar": slot_mortar, "vertex_ids": vertex_ids}


highest = lax.Precision.HIGHEST


def face_traces(nodal_block, points):
    element_cube = nodal_block.reshape(points, points, points, -1)
    far_index = points - 1
    slab_list = [element_cube[0], element_cube[far_index], element_cube[:, 0], element_cube[:, far_index], element_cube[:, :, 0], element_cube[:, :, far_index]]
    return jnp.concatenate(slab_list, axis=2)


def face_maps(interp, face_level, points):
    identity = jnp.eye(points, dtype=jnp.float32)[:, :, None]
    first_one = interp[0][:, :, None]
    second_one = interp[1][:, :, None]
    level_row = face_level[None, None, :]
    left_map = jnp.where(level_row == 0, identity, jnp.where(level_row <= 2, first_one, second_one))
    right_map = jnp.where(level_row == 0, identity, jnp.where(level_row % 2 == 1, first_one, second_one))
    return left_map, right_map


def project_traces(traces, left_map, right_map):
    partial_rows = jnp.einsum('xaf,abf->xbf', left_map, traces, precision=highest)
    return jnp.einsum('ybf,xbf->xyf', right_map, partial_rows, precision=highest)


def back_project(values, left_map, right_map):
    partial_rows = jnp.einsum('xaf,xyf->ayf', left_map, values, precision=highest)
    return jnp.einsum('ybf,ayf->abf', right_map, partial_rows, precision=highest)


def stiffness_apply(nodal_block, metric_block, derivative, points):
    element_cube = nodal_block.reshape(points, points, points, -1)
    metric_cube = metric_block.astype(jnp.float32).reshape(3, points, points, points, -1)
    grad_first = jnp.einsum('ai,ijke->ajke', derivative, element_cube, precision=highest)
    grad_second = jnp.einsum('bj,ijke->ibke', derivative, element_cube, precision=highest)
    grad_third = jnp.einsum('ck,ijke->ijce', derivative, element_cube, precision=highest)
    result = jnp.einsum('ai,ajke->ijke', derivative, metric_cube[0] * grad_first, precision=highest)
    result = result + jnp.einsum('bj,ibke->ijke', derivative, metric_cube[1] * grad_second, precision=highest)
    result = result + jnp.einsum('ck,ijce->ijke', derivative, metric_cube[2] * grad_third, precision=highest)
    return result


def corner_values(nodal_block, points):
    element_cube = nodal_block.reshape(points, points, points, -1)
    far_index = points - 1
    return jnp.stack([element_cube[(corner // 4) * far_index, ((corner // 2) % 2) * far_index, (corner % 2) * far_index] for corner in range(8)])


def finish_block(result_cube, back_faces, corner_fix, points):
    far_index = points - 1
    count_elems = result_cube.shape[-1]
    face_parts = back_faces.reshape(points, points, 6, count_elems)
    result_cube = result_cube.at[0].add(face_parts[:, :, 0])
    result_cube = result_cube.at[far_index].add(face_parts[:, :, 1])
    result_cube = result_cube.at[:, 0].add(face_parts[:, :, 2])
    result_cube = result_cube.at[:, far_index].add(face_parts[:, :, 3])
    result_cube = result_cube.at[:, :, 0].add(face_parts[:, :, 4])
    result_cube = result_cube.at[:, :, far_index].add(face_parts[:, :, 5])
    for corner in range(8):
        result_cube = result_cube.at[(corner // 4) * far_index, ((corner // 2) % 2) * far_index, (corner % 2) * far_index].add(corner_fix[corner])
    return result_cube.reshape(points ** 3, count_elems)


def regroup(blocks, width_sq):
    shaped = blocks.reshape(N_ELEM, N_CLUS, width_sq, N_CLUS, CAP_C)
    return shaped.transpose(0, 3, 2, 1, 4).reshape(N_ELEM, N_CLUS, width_sq, N_CLUS * CAP_C)


def assemble(local_cols, incoming_cols, slot_row):
    mortar = local_cols.at[:, slot_row].add(incoming_cols)
    return mortar, mortar[:, slot_row]


def reference(nodal, metric, derivative, interp, face_level, face_target, slot_mortar, vertex_ids):
    devices = N_ELEM * N_CLUS
    points = POINTS
    width_sq = points * points
    per_face = 6 * E_DEV

    def send_one(device_index):
        first_col = (device_index * E_DEV).astype(jnp.int32)
        first_face = (device_index * per_face).astype(jnp.int32)
        nodal_block = lax.dynamic_slice_in_dim(nodal, first_col, E_DEV, axis=1)
        level_row = lax.dynamic_slice_in_dim(face_level, first_face, per_face)
        target_row = lax.dynamic_slice_in_dim(face_target, first_face, per_face)
        left_map, right_map = face_maps(interp, level_row, points)
        projected = project_traces(face_traces(nodal_block, points), left_map, right_map)
        return jnp.zeros((width_sq, M_DEV + SLOTS), jnp.float32).at[:, target_row].add(projected.reshape(width_sq, -1))

    outgoing = lax.map(send_one, jnp.arange(devices, dtype=jnp.int32))
    grid = outgoing.reshape(N_ELEM, N_CLUS, width_sq, M_DEV + SLOTS)
    local_part = grid[..., :M_DEV]
    to_prev = grid[..., M_DEV:M_DEV + CAP_E]
    to_next = grid[..., M_DEV + CAP_E:M_DEV + 2 * CAP_E]
    to_group = grid[..., M_DEV + 2 * CAP_E:]
    incoming = jnp.concatenate([jnp.roll(to_next, 1, axis=0), jnp.roll(to_prev, -1, axis=0), regroup(to_group, width_sq)], axis=3)
    slot_grid = slot_mortar.reshape(N_ELEM, N_CLUS, SLOTS)
    mortar, answers = jax.vmap(jax.vmap(assemble))(local_part, incoming, slot_grid)
    returned = jnp.concatenate([mortar, jnp.roll(answers[..., CAP_E:2 * CAP_E], 1, axis=0), jnp.roll(answers[..., :CAP_E], -1, axis=0), regroup(answers[..., 2 * CAP_E:], width_sq)], axis=3)
    returned_dev = returned.reshape(devices, width_sq, M_DEV + SLOTS)

    corners_all = corner_values(nodal, points)
    flat_ids = vertex_ids.reshape(-1)
    totals = jnp.zeros((NV,), jnp.float32).at[flat_ids].add(corners_all.reshape(-1))
    counts = jnp.zeros((NV,), jnp.float32).at[flat_ids].add(jnp.ones(flat_ids.shape, jnp.float32))
    coarse = totals / (1.0 + counts)
    corner_fix = coarse[vertex_ids]

    def finish_one(device_index):
        first_col = (device_index * E_DEV).astype(jnp.int32)
        first_face = (device_index * per_face).astype(jnp.int32)
        nodal_block = lax.dynamic_slice_in_dim(nodal, first_col, E_DEV, axis=1)
        metric_block = lax.dynamic_slice_in_dim(metric, first_col, E_DEV, axis=2)
        fix_block = lax.dynamic_slice_in_dim(corner_fix, first_col, E_DEV, axis=1)
        level_row = lax.dynamic_slice_in_dim(face_level, first_face, per_face)
        target_row = lax.dynamic_slice_in_dim(face_target, first_face, per_face)
        left_map, right_map = face_maps(interp, level_row, points)
        picked = returned_dev[device_index][:, target_row].reshape(points, points, -1)
        back_faces = back_project(picked, left_map, right_map)
        result_cube = stiffness_apply(nodal_block, metric_block, derivative, points)
        return finish_block(result_cube, back_faces, fix_block, points)

    blocks = lax.map(finish_one, jnp.arange(devices, dtype=jnp.int32))
    return blocks.transpose(1, 0, 2).reshape(points ** 3, devices * E_DEV)
```

```python
import functools

import jax
import jax.numpy as jnp
from jax import lax
from jax.experimental import pallas as pl
from jax.experimental.pallas import tpu as pltpu
from jax.sharding import PartitionSpec as P

POINTS = 8
SQ = POINTS * POINTS
CAP_E = 128
CAP_C = 16
M_DEV = 512
NV_DEV = 256
HALF = 64
LANES = 128
MIB = 1 << 20

f32 = jnp.float32
bf16 = jnp.bfloat16
highest = lax.Precision.HIGHEST


def split(x):
    hi = x.astype(bf16)
    lo = (x - hi.astype(f32)).astype(bf16)
    return hi, lo


def stack3(x, axis=0):
    hi, lo = split(x)
    return jnp.concatenate([hi, lo, hi], axis=axis)


def stack2(x):
    hi, lo = split(x)
    return jnp.concatenate([hi, lo], axis=0)


def mm(a, b):
    return lax.dot_general(a, b, (((1,), (0,)), ((), ())), preferred_element_type=f32)


def mm_nt(a, b):
    return lax.dot_general(a, b, (((1,), (1,)), ((), ())), preferred_element_type=f32)


def iota(shape, dim):
    return lax.broadcasted_iota(jnp.int32, shape, dim)


def expand(matrix, copies):
    width = SQ * copies
    lane = iota((POINTS, width), 1) % SQ
    row = iota((POINTS, width), 0)
    to_first = (lane // POINTS == row).astype(f32)
    to_second = (lane % POINTS == row).astype(f32)
    first = jnp.dot(matrix, to_first, precision=highest, preferred_element_type=f32)
    second = jnp.dot(matrix, to_second, precision=highest, preferred_element_type=f32)
    first = jnp.broadcast_to(first[:, None, :], (POINTS, POINTS, width)).reshape(SQ, width)
    second = jnp.concatenate([second] * POINTS, axis=0)
    return first, second


def hi_hi_lo(matrix):
    hi = matrix.astype(bf16).astype(f32)
    lane = iota(matrix.shape, 1)
    return jnp.where(lane < 2 * SQ, hi, matrix - hi).astype(bf16)


def kron_four(low, high):
    low_first, low_second = expand(low, 3)
    high_first, high_second = expand(high, 3)
    maps = [
        low_first * low_second,
        low_first * high_second,
        high_first * low_second,
        high_first * high_second,
    ]
    return hi_hi_lo(jnp.concatenate(maps, axis=0))


def load_rows(ref, rows):
    return jnp.concatenate([ref[h, rows, :] for h in range(ref.shape[0])], axis=1)


def load_comb(ref, j):
    return jnp.concatenate([load_rows(ref, pl.ds(a * SQ + j * 8, 8)) for a in range(8)], axis=0)


def store_rows(ref, rows, value):
    for h in range(ref.shape[0]):
        ref[h, rows, :] = value[:, h * LANES : (h + 1) * LANES]


def add_rows(ref, rows, value):
    for h in range(ref.shape[0]):
        ref[h, rows, :] += value[:, h * LANES : (h + 1) * LANES]


def lane_copies(hbm, blocks, sems, outward):
    copies = []
    for h in range(blocks.shape[0]):
        outer = hbm.at[:, pl.ds(h * LANES, LANES)]
        ends = (blocks.at[h], outer) if outward else (outer, blocks.at[h])
        copies.append(pltpu.make_async_copy(*ends, sems.at[h]))
    return copies


def pick_level(plain, mapped, level):
    out = plain
    for number in range(1, 5):
        out = jnp.where(level == number, mapped[(number - 1) * SQ : number * SQ], out)
    return out


def one_hot_rows(ids, first, count):
    return (iota((count, ids.shape[1]), 0) + first == ids).astype(f32).astype(bf16)


def window_ids(vertex_ids, elem_index, total):
    shifted = vertex_ids - elem_index * NV_DEV
    return jnp.where(shifted < 0, shifted + total, shifted)


def corner_row(corner):
    last = POINTS - 1
    return corner // 4 * last * SQ + corner // 2 % 2 * last * POINTS + corner % 2 * last


def send_kernel(
    total_vertices,
    elem_ref,
    nodal_hbm,
    metric_hbm,
    level_ref,
    target_ref,
    interp_ref,
    vertex_ref,
    down_ref,
    up_ref,
    group_ref,
    nodal_ref,
    metric_ref,
    traces_ref,
    remote_ref,
    slot_level_ref,
    maps_ref,
    low_ids_ref,
    sems,
):
    nodal_copies = lane_copies(nodal_hbm, nodal_ref, sems, False)
    metric_copy = pltpu.make_async_copy(metric_hbm, metric_ref, sems.at[len(nodal_copies)])
    for copy in nodal_copies:
        copy.start()
    metric_copy.start()
    slots = remote_ref.shape[0]
    elems = nodal_hbm.shape[1]
    level = level_ref[...]
    remote_ref[...] = one_hot_rows(target_ref[...], M_DEV, slots)
    maps = kron_four(interp_ref[0], interp_ref[1])
    maps_ref[...] = maps
    window = window_ids(vertex_ref[...], elem_ref[0], total_vertices)
    high_id = window // HALF
    low_id = window % HALF
    zeros = jnp.zeros((HALF, elems), bf16)
    low_hot = []
    for corner in range(8):
        hot = one_hot_rows(low_id[corner : corner + 1], 0, HALF)
        low_hot.append(jnp.concatenate([zeros, hot], axis=0))
    low_hot = jnp.concatenate(low_hot, axis=1)
    low_ids_ref[...] = low_hot

    for copy in nodal_copies:
        copy.wait()
    faces = [
        load_rows(nodal_ref, pl.ds(0, SQ)),
        load_rows(nodal_ref, pl.ds(7 * SQ, SQ)),
        load_comb(nodal_ref, 0),
        load_comb(nodal_ref, 7),
        load_rows(nodal_ref, pl.ds(0, SQ, stride=8)),
        load_rows(nodal_ref, pl.ds(7, SQ, stride=8)),
    ]
    trace = jnp.concatenate(faces, axis=1)
    hi, lo = split(trace)
    traces_ref[0:SQ, :] = hi
    traces_ref[SQ : 2 * SQ, :] = lo
    traces_ref[2 * SQ :, :] = jnp.broadcast_to(level, (16, level.shape[1])).astype(f32).astype(bf16)

    picked = mm_nt(traces_ref[...], remote_ref[...])
    plain = picked[0:SQ] + picked[SQ : 2 * SQ]
    slot_level = picked[2 * SQ : 2 * SQ + 8]
    slot_level_ref[...] = slot_level
    mapped = mm(maps, stack3(plain))
    sent = pick_level(plain, mapped, slot_level[0:1])
    down_ref[...] = sent[:, 0:CAP_E]
    up_ref[...] = sent[:, CAP_E : 2 * CAP_E]

    row = iota((16, elems), 0)
    row_high = row % 4 + 4 * (row // 8)
    is_count = row // 4 % 2 == 1
    weighted = []
    for corner in range(8):
        value = load_rows(nodal_ref, pl.ds(corner_row(corner), 1))
        value_hi = value.astype(bf16).astype(f32)
        value_lo = value - value_hi
        mine = high_id[corner : corner + 1] == row_high
        first = jnp.where(mine, jnp.where(is_count, 1.0, value_hi), 0.0)
        second = jnp.where(mine & ~is_count, value_lo, 0.0)
        weighted.append(jnp.concatenate([first, second], axis=0).astype(bf16))
    sums = mm_nt(jnp.concatenate(weighted, axis=1), low_hot)
    sums = sums[0:16] + sums[16:32]
    group = sent[:, 2 * CAP_E :]
    group = jnp.concatenate([group, jnp.zeros_like(group)], axis=0).T
    group_ref[...] = group + jnp.concatenate([sums] * (group.shape[0] // 16), axis=0)
    metric_copy.wait()


def local_kernel(
    traces_ref,
    maps_ref,
    level_ref,
    target_ref,
    slot_mortar_ref,
    nodal_ref,
    metric_ref,
    derivative_ref,
    mortar_ref,
    answers_ref,
    equal_ref,
    local_ref,
    slot_hot_ref,
    stiff_ref,
    by_row,
    by_col,
):
    hi = traces_ref[0:SQ, :]
    lo = traces_ref[SQ : 2 * SQ, :]
    plain = hi.astype(f32) + lo.astype(f32)
    mapped = mm(maps_ref[...], jnp.concatenate([hi, lo, hi], axis=0))
    projected = pick_level(plain, mapped, level_ref[...])
    local_ref[...] = one_hot_rows(target_ref[...], 0, M_DEV)
    mortar = mm_nt(stack2(projected), local_ref[...])
    mortar = mortar[0:SQ] + mortar[SQ:]
    mortar_ref[...] = mortar
    slot_row = slot_mortar_ref[...]
    slots = slot_row.shape[1]
    slot_hot_t = one_hot_rows(slot_row, 0, M_DEV)
    answers = mm(stack2(mortar), slot_hot_t)
    answers_ref[...] = answers[0:SQ] + answers[SQ:]
    slot_col = jnp.broadcast_to(slot_row, (128, slots)).T[:, 0:1]
    equal_ref[...] = (slot_col == slot_row).astype(f32).astype(bf16)
    slot_hot_ref[...] = (slot_col == iota((slots, M_DEV), 1)).astype(f32).astype(bf16)
    stiffness(nodal_ref, metric_ref, derivative_ref, stiff_ref, by_row, by_col)


def stiffness(nodal_ref, metric_ref, derivative_ref, stiff_ref, by_row, by_col):
    derivative = derivative_ref[...]
    row = iota((SQ, 3 * SQ), 0)
    lane = iota((SQ, 3 * SQ), 1) % SQ

    def pair(matrix):
        first, second = expand(matrix, 3)
        outer = jnp.where(row % 8 == lane % 8, first, 0.0)
        inner = jnp.where(row // 8 == lane // 8, second, 0.0)
        return hi_hi_lo(outer), hi_hi_lo(inner)

    outer, inner = pair(derivative)
    outer_t, inner_t = pair(derivative.T)
    both = jnp.concatenate([outer, inner], axis=0)
    for i in range(8):
        slab = load_rows(nodal_ref, pl.ds(i * SQ, SQ))
        grad = mm(outer, stack3(slab))
        weighted = grad * metric_ref[1, i * SQ : (i + 1) * SQ, :].astype(f32)
        stiff_ref[i * SQ : (i + 1) * SQ, :] = mm(outer_t, stack3(weighted))
        by_row[i * SQ : (i + 1) * SQ, :] = metric_ref[0, i * SQ : (i + 1) * SQ, :].astype(f32)
        by_col[i * SQ : (i + 1) * SQ, :] = metric_ref[2, i * SQ : (i + 1) * SQ, :].astype(f32)

    def comb(ref, j):
        return jnp.concatenate([ref[i * SQ + j * 8 : i * SQ + j * 8 + 8, :] for i in range(8)], axis=0)

    for j in range(8):
        grad = mm(both, stack3(load_comb(nodal_ref, j)))
        out = mm(outer_t, stack3(grad[0:SQ] * comb(by_row, j)))
        out = out + mm(inner_t, stack3(grad[SQ:] * comb(by_col, j)))
        for i in range(8):
            stiff_ref[i * SQ + j * 8 : i * SQ + j * 8 + 8, :] += out[i * 8 : i * 8 + 8]


def answer_kernel(
    from_up_ref,
    from_down_ref,
    group_ref,
    equal_ref,
    local_answers_ref,
    down_ref,
    up_ref,
    group_out_ref,
    incoming_ref,
    sums_ref,
):
    group_in = group_ref[...]
    incoming = jnp.concatenate([from_up_ref[...], from_down_ref[...], group_in.T[0:SQ]], axis=1)
    incoming_ref[...] = incoming
    added = mm(stack2(incoming), equal_ref[...])
    answers = local_answers_ref[...] + added[0:SQ] + added[SQ:]
    sums = group_in[0:16]
    for block in range(1, group_in.shape[0] // 16):
        sums = sums + group_in[block * 16 : block * 16 + 16]
    sums_ref[...] = sums
    down_ref[0:SQ, :] = answers[:, 0:CAP_E]
    up_ref[0:SQ, :] = answers[:, CAP_E : 2 * CAP_E]
    down_ref[SQ:, :] = sums[0:8]
    up_ref[SQ:, :] = sums[8:16]
    group = answers[:, 2 * CAP_E :]
    group_out_ref[...] = jnp.concatenate([group, jnp.zeros_like(group)], axis=0).T


def gather_kernel(
    mortar_ref,
    incoming_ref,
    slot_hot_ref,
    local_ref,
    level_ref,
    interp_ref,
    stiff_ref,
    result_ref,
    maps_ref,
):
    added = mm(stack2(incoming_ref[...]), slot_hot_ref[...])
    mortar = mortar_ref[...] + added[0:SQ] + added[SQ:]
    picked = mm(stack2(mortar), local_ref[...])
    picked = picked[0:SQ] + picked[SQ:]
    maps = kron_four(interp_ref[0].T, interp_ref[1].T)
    maps_ref[...] = maps
    back = pick_level(picked, mm(maps, stack3(picked)), level_ref[...])
    store_rows(result_ref, slice(None), stiff_ref[...])
    add_faces(result_ref, back)


def add_faces(ref, back):
    elems = ref.shape[0] * LANES
    parts = [back[:, f * elems : (f + 1) * elems] for f in range(6)]
    add_rows(ref, pl.ds(0, SQ), parts[0])
    add_rows(ref, pl.ds(7 * SQ, SQ), parts[1])
    for a in range(8):
        add_rows(ref, pl.ds(a * SQ, 8), parts[2][a * 8 : a * 8 + 8])
        add_rows(ref, pl.ds(a * SQ + 56, 8), parts[3][a * 8 : a * 8 + 8])
    add_rows(ref, pl.ds(0, SQ, stride=8), parts[4])
    add_rows(ref, pl.ds(7, SQ, stride=8), parts[5])


def final_kernel(
    total_vertices,
    elem_ref,
    from_up_ref,
    from_down_ref,
    group_ref,
    slot_level_ref,
    maps_ref,
    remote_ref,
    sums_ref,
    vertex_ref,
    low_ids_ref,
    result_ref,
    out_hbm,
    out_ref,
    sems,
):
    arrived = jnp.concatenate(
        [from_up_ref[0:SQ, :], from_down_ref[0:SQ, :], group_ref[...].T[0:SQ]], axis=1
    )
    slot_back = pick_level(arrived, mm(maps_ref[...], stack3(arrived)), slot_level_ref[0:1, :])
    back = mm(stack2(slot_back), remote_ref[...])
    back = back[0:SQ] + back[SQ:]

    first = sums_ref[0:8, :] + from_up_ref[SQ:, :]
    second = sums_ref[8:16, :] + from_down_ref[SQ:, :]
    totals = jnp.concatenate([first[0:4], second[0:4]], axis=0)
    counts = jnp.concatenate([first[4:8], second[4:8]], axis=0)
    coarse = jnp.where(iota(totals.shape, 1) < HALF, 0.0, totals / (1.0 + counts))
    coarse_hi = coarse.astype(bf16).astype(f32)
    table = jnp.concatenate([coarse_hi, coarse - coarse_hi], axis=0).astype(bf16)
    found = mm(table, low_ids_ref[...])
    found = found[0:8] + found[8:16]
    high_id = window_ids(vertex_ref[...], elem_ref[0], total_vertices) // HALF

    out_ref[...] = result_ref[...]
    add_faces(out_ref, back)
    elems = out_hbm.shape[1]
    row = iota((8, elems), 0)
    for corner in range(8):
        mine = row == high_id[corner : corner + 1]
        fix = jnp.where(mine, found[:, corner * elems : (corner + 1) * elems], 0.0)
        at = corner_row(corner)
        add_rows(out_ref, pl.ds(at, 1), jnp.sum(fix, axis=0, keepdims=True))
    copies = lane_copies(out_hbm, out_ref, sems, True)
    for copy in copies:
        copy.start()
    for copy in copies:
        copy.wait()


VMEM = pl.BlockSpec(memory_space=pltpu.VMEM)
SMEM = pl.BlockSpec(memory_space=pltpu.SMEM)
HBM = pl.BlockSpec(memory_space=pltpu.HBM)


def params(mib):
    return pltpu.CompilerParams(vmem_limit_bytes=mib * MIB)


def cost(us):
    return pl.CostEstimate(flops=int(us * 5e8), bytes_accessed=int(us * 2e6), transcendentals=0)


def neighbours(axis):
    peers = lax.axis_size(axis)
    up = [(i, (i + 1) % peers) for i in range(peers)]
    return up, [(j, i) for i, j in up]


def exchange(down, up, group):
    up_pairs, down_pairs = neighbours("elem")
    group = lax.all_to_all(group, "clus", split_axis=0, concat_axis=0, tiled=True)
    return lax.ppermute(up, "elem", up_pairs), lax.ppermute(down, "elem", down_pairs), group


def on_device(nodal, metric, derivative, interp, face_level, face_target, slot_mortar, vertex_ids):
    elems = nodal.shape[1]
    faces = face_level.shape[0]
    slots = slot_mortar.shape[0]
    total_vertices = NV_DEV * lax.axis_size("elem")
    elem_index = lax.axis_index("elem").astype(jnp.int32).reshape(1)
    level = face_level.reshape(1, faces)
    target = face_target.reshape(1, faces)
    slot_row = slot_mortar.reshape(1, slots)
    blocked = (elems // LANES, nodal.shape[0], LANES)
    group_slots = slots - 2 * CAP_E

    down, up, group, nodal_in, metric_in, traces, remote, slot_level, maps, low_ids = pl.pallas_call(
        functools.partial(send_kernel, total_vertices),
        in_specs=[SMEM, HBM, HBM] + [VMEM] * 4,
        out_specs=[VMEM] * 10,
        out_shape=[
            pltpu.VMEM((SQ, CAP_E), f32),
            pltpu.VMEM((SQ, CAP_E), f32),
            pltpu.VMEM((group_slots, 128), f32),
            pltpu.VMEM(blocked, f32),
            pltpu.VMEM(metric.shape, bf16),
            pltpu.VMEM((2 * SQ + 16, faces), bf16),
            pltpu.VMEM((slots, faces), bf16),
            pltpu.VMEM((8, slots), f32),
            pltpu.VMEM((4 * SQ, 3 * SQ), bf16),
            pltpu.VMEM((2 * HALF, 8 * elems), bf16),
        ],
        scratch_shapes=[pltpu.SemaphoreType.DMA((blocked[0] + 1,))],
        compiler_params=params(16),
        name="send",
    )(elem_index, nodal, metric, level, target, interp, vertex_ids)

    from_up, from_down, group_in = exchange(down, up, group)

    mortar, local_answers, equal, local, slot_hot, stiff = pl.pallas_call(
        local_kernel,
        in_specs=[VMEM] * 8,
        out_specs=[VMEM] * 6,
        out_shape=[
            pltpu.VMEM((SQ, M_DEV), f32),
            pltpu.VMEM((SQ, slots), f32),
            pltpu.VMEM((slots, slots), bf16),
            pltpu.VMEM((M_DEV, faces), bf16),
            pltpu.VMEM((slots, M_DEV), bf16),
            pltpu.VMEM(nodal.shape, f32),
        ],
        scratch_shapes=[pltpu.VMEM(nodal.shape, f32), pltpu.VMEM(nodal.shape, f32)],
        compiler_params=params(16),
        cost_estimate=cost(3),
        name="local",
    )(traces, maps, level, target, slot_row, nodal_in, metric_in, derivative)

    down, up, group, incoming, sums = pl.pallas_call(
        answer_kernel,
        in_specs=[VMEM] * 5,
        out_specs=[VMEM] * 5,
        out_shape=[
            pltpu.VMEM((SQ + 8, CAP_E), f32),
            pltpu.VMEM((SQ + 8, CAP_E), f32),
            pltpu.VMEM((group_slots, 128), f32),
            pltpu.VMEM((SQ, slots), f32),
            pltpu.VMEM((16, 128), f32),
        ],
        compiler_params=params(16),
        name="answer",
    )(from_up, from_down, group_in, equal, local_answers)

    from_up, from_down, group_in = exchange(down, up, group)

    result, back_maps = pl.pallas_call(
        gather_kernel,
        in_specs=[VMEM] * 7,
        out_specs=[VMEM] * 2,
        out_shape=[pltpu.VMEM(blocked, f32), pltpu.VMEM((4 * SQ, 3 * SQ), bf16)],
        compiler_params=params(16),
        cost_estimate=cost(2),
        name="gather",
    )(mortar, incoming, slot_hot, local, level, interp, stiff)

    return pl.pallas_call(
        functools.partial(final_kernel, total_vertices),
        in_specs=[SMEM] + [VMEM] * 10,
        out_specs=HBM,
        out_shape=jax.ShapeDtypeStruct(nodal.shape, f32),
        scratch_shapes=[pltpu.VMEM(blocked, f32), pltpu.SemaphoreType.DMA((blocked[0],))],
        compiler_params=params(16),
        name="final",
    )(
        elem_index,
        from_up,
        from_down,
        group_in,
        slot_level,
        back_maps,
        remote,
        sums,
        vertex_ids,
        low_ids,
        result,
    )


def solution(mesh):
    in_specs = (
        P(None, ("elem", "clus")),
        P(None, None, ("elem", "clus")),
        P(),
        P(),
        P(("elem", "clus")),
        P(("elem", "clus")),
        P(("elem", "clus")),
        P(None, ("elem", "clus")),
    )
    out_specs = P(None, ("elem", "clus"))
    return jax.shard_map(
        on_device, mesh=mesh, in_specs=in_specs, out_specs=out_specs, check_vma=False
    )
```

```python
import functools

import jax
import jax.numpy as jnp
from jax import lax
from jax.experimental import pallas as pl
from jax.experimental.pallas import tpu as pltpu
from jax.sharding import PartitionSpec as P

POINTS = 8
SQ = POINTS * POINTS
CAP_E = 128
CAP_C = 16
M_DEV = 512
NV_DEV = 256
HALF = 64
LANES = 128
MIB = 1 << 20

f32 = jnp.float32
bf16 = jnp.bfloat16
highest = lax.Precision.HIGHEST


def split(x):
    hi = x.astype(bf16)
    lo = (x - hi.astype(f32)).astype(bf16)
    return hi, lo


def stack3(x, axis=0):
    hi, lo = split(x)
    return jnp.concatenate([hi, lo, hi], axis=axis)


def stack2(x):
    hi, lo = split(x)
    return jnp.concatenate([hi, lo], axis=0)


def mm(a, b):
    return lax.dot_general(a, b, (((1,), (0,)), ((), ())), preferred_element_type=f32)


def mm_nt(a, b):
    return lax.dot_general(a, b, (((1,), (1,)), ((), ())), preferred_element_type=f32)


def iota(shape, dim):
    return lax.broadcasted_iota(jnp.int32, shape, dim)


def expand(matrix, copies):
    width = SQ * copies
    lane = iota((POINTS, width), 1) % SQ
    row = iota((POINTS, width), 0)
    to_first = (lane // POINTS == row).astype(f32)
    to_second = (lane % POINTS == row).astype(f32)
    first = jnp.dot(matrix, to_first, precision=highest, preferred_element_type=f32)
    second = jnp.dot(matrix, to_second, precision=highest, preferred_element_type=f32)
    first = jnp.broadcast_to(first[:, None, :], (POINTS, POINTS, width)).reshape(SQ, width)
    second = jnp.concatenate([second] * POINTS, axis=0)
    return first, second


def hi_hi_lo(matrix):
    hi = matrix.astype(bf16).astype(f32)
    lane = iota(matrix.shape, 1)
    return jnp.where(lane < 2 * SQ, hi, matrix - hi).astype(bf16)


def kron_four(low, high):
    low_first, low_second = expand(low, 3)
    high_first, high_second = expand(high, 3)
    maps = [
        low_first * low_second,
        low_first * high_second,
        high_first * low_second,
        high_first * high_second,
    ]
    return hi_hi_lo(jnp.concatenate(maps, axis=0))


def load_rows(ref, rows):
    return jnp.concatenate([ref[h, rows, :] for h in range(ref.shape[0])], axis=1)


def load_comb(ref, j):
    return jnp.concatenate([load_rows(ref, pl.ds(a * SQ + j * 8, 8)) for a in range(8)], axis=0)


def store_rows(ref, rows, value):
    for h in range(ref.shape[0]):
        ref[h, rows, :] = value[:, h * LANES : (h + 1) * LANES]


def add_rows(ref, rows, value):
    for h in range(ref.shape[0]):
        ref[h, rows, :] += value[:, h * LANES : (h + 1) * LANES]


def lane_copies(hbm, blocks, sems, outward):
    copies = []
    for h in range(blocks.shape[0]):
        outer = hbm.at[:, pl.ds(h * LANES, LANES)]
        ends = (blocks.at[h], outer) if outward else (outer, blocks.at[h])
        copies.append(pltpu.make_async_copy(*ends, sems.at[h]))
    return copies


def pick_level(plain, mapped, level):
    out = plain
    for number in range(1, 5):
        out = jnp.where(level == number, mapped[(number - 1) * SQ : number * SQ], out)
    return out


def one_hot_rows(ids, first, count):
    return (iota((count, ids.shape[1]), 0) + first == ids).astype(f32).astype(bf16)


def columns_of(row):
    return jnp.broadcast_to(row, (LANES, row.shape[1])).T


def one_hot_lanes(columns, first, count):
    lane = iota((columns.shape[0], LANES), 1) + first
    blocks = [columns == lane + start for start in range(0, count, LANES)]
    return jnp.concatenate([block.astype(f32).astype(bf16) for block in blocks], axis=1)


def window_ids(vertex_ids, elem_index, total):
    shifted = vertex_ids - elem_index * NV_DEV
    window = jnp.where(shifted < 0, shifted + total, shifted)
    return window // HALF, window % HALF


def low_one_hot(low_id):
    parts = []
    for corner in range(8):
        hot = one_hot_rows(low_id[corner : corner + 1], 0, HALF)
        parts.append(jnp.concatenate([jnp.zeros_like(hot), hot], axis=0))
    return jnp.concatenate(parts, axis=1)


def corner_row(corner):
    last = POINTS - 1
    return corner // 4 * last * SQ + corner // 2 % 2 * last * POINTS + corner % 2 * last


def send_kernel(
    total_vertices,
    elem_ref,
    nodal_hbm,
    level_hbm,
    target_hbm,
    slot_hbm,
    interp_hbm,
    derivative_hbm,
    vertex_hbm,
    down_ref,
    up_ref,
    group_hbm,
    traces_ref,
    columns_ref,
    slot_level_ref,
    maps_ref,
    level_ref,
    target_ref,
    slot_mortar_ref,
    interp_ref,
    derivative_ref,
    vertex_ref,
    nodal_ref,
    group_ref,
    nodal_sems,
    sems,
):
    target_copy = pltpu.make_async_copy(target_hbm, target_ref.at[0], sems.at[0])
    level_copy = pltpu.make_async_copy(level_hbm, level_ref.at[0], sems.at[1])
    interp_copy = pltpu.make_async_copy(interp_hbm, interp_ref, sems.at[2])
    vertex_copy = pltpu.make_async_copy(vertex_hbm, vertex_ref, sems.at[3])
    slot_copy = pltpu.make_async_copy(slot_hbm, slot_mortar_ref.at[0], sems.at[4])
    derivative_copy = pltpu.make_async_copy(derivative_hbm, derivative_ref, sems.at[5])
    nodal_copies = lane_copies(nodal_hbm, nodal_ref, nodal_sems, False)
    target_copy.start()
    interp_copy.start()
    for copy in nodal_copies:
        copy.start()
    for copy in (level_copy, vertex_copy, slot_copy, derivative_copy):
        copy.start()
    slots = slot_level_ref.shape[1]
    elems = nodal_hbm.shape[1]
    target_copy.wait()
    columns = columns_of(target_ref[...])
    columns_ref[...] = columns
    remote = one_hot_lanes(columns, M_DEV, -(-slots // 256) * 256)
    interp_copy.wait()
    maps = kron_four(interp_ref[0], interp_ref[1])
    maps_ref[...] = maps
    vertex_copy.wait()
    high_id, low_id = window_ids(vertex_ref[...], elem_ref[0], total_vertices)
    low_hot = low_one_hot(low_id)

    for copy in nodal_copies:
        copy.wait()
    level_copy.wait()
    level = level_ref[...]
    faces = [
        load_rows(nodal_ref, pl.ds(0, SQ)),
        load_rows(nodal_ref, pl.ds(7 * SQ, SQ)),
        load_comb(nodal_ref, 0),
        load_comb(nodal_ref, 7),
        load_rows(nodal_ref, pl.ds(0, SQ, stride=8)),
        load_rows(nodal_ref, pl.ds(7, SQ, stride=8)),
    ]
    trace = jnp.concatenate(faces, axis=1)
    hi, lo = split(trace)
    traces_ref[0:SQ, :] = hi
    traces_ref[SQ : 2 * SQ, :] = lo
    traces_ref[2 * SQ :, :] = jnp.broadcast_to(level, (16, level.shape[1])).astype(f32).astype(bf16)

    picked = mm(traces_ref[...], remote)[:, 0:slots]
    plain = picked[0:SQ] + picked[SQ : 2 * SQ]
    slot_level = picked[2 * SQ : 2 * SQ + 8]
    slot_level_ref[...] = slot_level
    mapped = mm(maps, stack3(plain))
    sent = pick_level(plain, mapped, slot_level[0:1])
    row = iota((16, elems), 0)
    row_high = row % 4 + 4 * (row // 8)
    is_count = row // 4 % 2 == 1
    weighted = []
    for corner in range(8):
        value = load_rows(nodal_ref, pl.ds(corner_row(corner), 1))
        value_hi = value.astype(bf16).astype(f32)
        value_lo = value - value_hi
        mine = high_id[corner : corner + 1] == row_high
        first = jnp.where(mine, jnp.where(is_count, 1.0, value_hi), 0.0)
        second = jnp.where(mine & ~is_count, value_lo, 0.0)
        weighted.append(jnp.concatenate([first, second], axis=0).astype(bf16))
    sums = mm_nt(jnp.concatenate(weighted, axis=1), low_hot)
    sums = sums[0:16] + sums[16:32]
    group = sent[:, 2 * CAP_E :]
    group = jnp.concatenate([group, jnp.zeros_like(group)], axis=0).T
    group_ref[...] = group + jnp.concatenate([sums] * (group.shape[0] // 16), axis=0)
    group_copy = pltpu.make_async_copy(group_ref, group_hbm, sems.at[6])
    group_copy.start()
    down_ref[...] = sent[:, 0:CAP_E]
    up_ref[...] = sent[:, CAP_E : 2 * CAP_E]
    slot_copy.wait()
    derivative_copy.wait()
    group_copy.wait()


def stiffness_maps(matrix):
    row = iota((SQ, 3 * SQ), 0)
    lane = iota((SQ, 3 * SQ), 1) % SQ
    first, second = expand(matrix, 3)
    outer = jnp.where(row % 8 == lane % 8, first, 0.0)
    inner = jnp.where(row // 8 == lane // 8, second, 0.0)
    return hi_hi_lo(outer), hi_hi_lo(inner)


def local_kernel(
    nodal_hbm,
    metric_hbm,
    traces_ref,
    maps_ref,
    level_ref,
    columns_ref,
    slot_mortar_ref,
    interp_ref,
    derivative_ref,
    mortar_ref,
    answers_ref,
    equal_ref,
    stiff_ref,
    back_maps_ref,
    grad_map_ref,
    div_map_ref,
    nodal_ref,
    metric_ref,
    by_row,
    nodal_sems,
    sem,
):
    nodal_copies = lane_copies(nodal_hbm, nodal_ref, nodal_sems, False)
    metric_copy = pltpu.make_async_copy(metric_hbm.at[0], metric_ref, sem)
    for copy in nodal_copies:
        copy.start()
    metric_copy.start()
    hi = traces_ref[0:SQ, :]
    lo = traces_ref[SQ : 2 * SQ, :]
    plain = hi.astype(f32) + lo.astype(f32)
    mapped = mm(maps_ref[...], jnp.concatenate([hi, lo, hi], axis=0))
    projected = pick_level(plain, mapped, level_ref[...])
    mortar = mm(stack2(projected), one_hot_lanes(columns_ref[...], 0, M_DEV))
    mortar = mortar[0:SQ] + mortar[SQ:]
    mortar_ref[...] = mortar
    slot_row = slot_mortar_ref[...]
    answers = mm(stack2(mortar), one_hot_rows(slot_row, 0, M_DEV))
    answers_ref[...] = answers[0:SQ] + answers[SQ:]
    equal_ref[...] = (columns_of(slot_row)[:, 0:1] == slot_row).astype(f32).astype(bf16)

    back_maps_ref[...] = kron_four(interp_ref[0].T, interp_ref[1].T)
    outer, inner = stiffness_maps(derivative_ref[...])
    outer_t, inner_t = stiffness_maps(derivative_ref[...].T)
    grad_map_ref[0:SQ, :] = outer
    grad_map_ref[SQ:, :] = inner
    div_map_ref[...] = jnp.concatenate([outer_t, inner_t], axis=1)
    for copy in nodal_copies:
        copy.wait()
    metric_copy.wait()
    first_direction(nodal_ref, metric_ref, outer, outer_t, stiff_ref, by_row)


def first_direction(nodal_ref, metric_ref, outer, outer_t, stiff_ref, by_row):
    for i in range(8):
        by_row[i * SQ : (i + 1) * SQ, :] = metric_ref[i * SQ : (i + 1) * SQ, :].astype(f32)
    grads = [mm(outer, stack3(load_comb(nodal_ref, j))) for j in range(8)]
    weighted = []
    for j in range(8):
        factor = [by_row[i * SQ + j * 8 : i * SQ + j * 8 + 8, :] for i in range(8)]
        weighted.append(stack3(grads[j] * jnp.concatenate(factor, axis=0)))
    for j in range(8):
        out = mm(outer_t, weighted[j])
        for i in range(8):
            stiff_ref[i * SQ + j * 8 : i * SQ + j * 8 + 8, :] = out[i * 8 : i * 8 + 8]


def other_directions(nodal_ref, metric_ref, grad_map, div_map, stiff_ref, result_ref):
    slabs = [pl.ds(i * SQ, SQ) for i in range(8)]
    grads = [mm(grad_map, stack3(load_rows(nodal_ref, slab))) for slab in slabs]
    weighted = []
    for slab, grad in zip(slabs, grads):
        second = stack3(grad[0:SQ] * metric_ref[0, slab, :].astype(f32))
        third = stack3(grad[SQ:] * metric_ref[1, slab, :].astype(f32))
        weighted.append(jnp.concatenate([second, third], axis=0))
    for slab, part in zip(slabs, weighted):
        store_rows(result_ref, slab, stiff_ref[slab, :] + mm(div_map, part))


def answer_kernel(
    from_up_ref,
    from_down_ref,
    group_ref,
    equal_ref,
    local_answers_ref,
    down_ref,
    up_ref,
    group_hbm,
    incoming_ref,
    sums_ref,
    group_out_ref,
    sem,
):
    group_in = group_ref[...]
    incoming = jnp.concatenate([from_up_ref[...], from_down_ref[...], group_in.T[0:SQ]], axis=1)
    incoming_ref[...] = incoming
    added = mm(stack2(incoming), equal_ref[...])
    answers = local_answers_ref[...] + added[0:SQ] + added[SQ:]
    group = answers[:, 2 * CAP_E :]
    group_out_ref[...] = jnp.concatenate([group, jnp.zeros_like(group)], axis=0).T
    group_copy = pltpu.make_async_copy(group_out_ref, group_hbm, sem)
    group_copy.start()
    sums = group_in[0:16]
    for block in range(1, group_in.shape[0] // 16):
        sums = sums + group_in[block * 16 : block * 16 + 16]
    sums_ref[...] = sums
    down_ref[0:SQ, :] = answers[:, 0:CAP_E]
    up_ref[0:SQ, :] = answers[:, CAP_E : 2 * CAP_E]
    down_ref[SQ:, :] = sums[0:8]
    up_ref[SQ:, :] = sums[8:16]
    group_copy.wait()


def gather_kernel(
    total_vertices,
    elem_ref,
    nodal_hbm,
    metric_hbm,
    mortar_ref,
    incoming_ref,
    slot_mortar_ref,
    target_ref,
    level_ref,
    back_maps_ref,
    grad_map_ref,
    div_map_ref,
    vertex_ref,
    stiff_ref,
    result_ref,
    remote_ref,
    low_ids_ref,
    high_ids_ref,
    nodal_ref,
    metric_ref,
    nodal_sems,
    sem,
):
    nodal_copies = lane_copies(nodal_hbm, nodal_ref, nodal_sems, False)
    metric_copy = pltpu.make_async_copy(metric_hbm.at[1:3], metric_ref, sem)
    for copy in nodal_copies:
        copy.start()
    metric_copy.start()
    slot_hot = one_hot_lanes(columns_of(slot_mortar_ref[...]), 0, M_DEV)
    added = mm(stack2(incoming_ref[...]), slot_hot)
    mortar = mortar_ref[...] + added[0:SQ] + added[SQ:]
    target = target_ref[...]
    picked = mm(stack2(mortar), one_hot_rows(target, 0, M_DEV))
    picked = picked[0:SQ] + picked[SQ:]
    back = pick_level(picked, mm(back_maps_ref[...], stack3(picked)), level_ref[...])
    remote_ref[...] = one_hot_rows(target, M_DEV, remote_ref.shape[0])
    high_id, low_id = window_ids(vertex_ref[...], elem_ref[0], total_vertices)
    high_ids_ref[...] = high_id
    low_ids_ref[...] = low_one_hot(low_id)
    for copy in nodal_copies:
        copy.wait()
    metric_copy.wait()
    other_directions(
        nodal_ref, metric_ref, grad_map_ref[...], div_map_ref[...], stiff_ref, result_ref
    )
    add_faces(result_ref, back)


def add_faces(ref, back):
    elems = ref.shape[0] * LANES
    parts = [back[:, f * elems : (f + 1) * elems] for f in range(6)]
    add_rows(ref, pl.ds(0, SQ), parts[0])
    add_rows(ref, pl.ds(7 * SQ, SQ), parts[1])
    for a in range(8):
        add_rows(ref, pl.ds(a * SQ, 8), parts[2][a * 8 : a * 8 + 8])
        add_rows(ref, pl.ds(a * SQ + 56, 8), parts[3][a * 8 : a * 8 + 8])
    add_rows(ref, pl.ds(0, SQ, stride=8), parts[4])
    add_rows(ref, pl.ds(7, SQ, stride=8), parts[5])


def final_kernel(
    from_up_ref,
    from_down_ref,
    group_ref,
    slot_level_ref,
    maps_ref,
    remote_ref,
    sums_ref,
    high_ids_ref,
    low_ids_ref,
    result_ref,
    out_hbm,
    out_ref,
    sems,
):
    arrived = jnp.concatenate(
        [from_up_ref[0:SQ, :], from_down_ref[0:SQ, :], group_ref[...].T[0:SQ]], axis=1
    )
    slot_back = pick_level(arrived, mm(maps_ref[...], stack3(arrived)), slot_level_ref[0:1, :])
    back = mm(stack2(slot_back), remote_ref[...])
    back = back[0:SQ] + back[SQ:]

    first = sums_ref[0:8, :] + from_up_ref[SQ:, :]
    second = sums_ref[8:16, :] + from_down_ref[SQ:, :]
    totals = jnp.concatenate([first[0:4], second[0:4]], axis=0)
    counts = jnp.concatenate([first[4:8], second[4:8]], axis=0)
    coarse = jnp.where(iota(totals.shape, 1) < HALF, 0.0, totals / (1.0 + counts))
    coarse_hi = coarse.astype(bf16).astype(f32)
    table = jnp.concatenate([coarse_hi, coarse - coarse_hi], axis=0).astype(bf16)
    found = mm(table, low_ids_ref[...])
    found = found[0:8] + found[8:16]
    high_id = high_ids_ref[...]

    out_ref[...] = result_ref[...]
    add_faces(out_ref, back)
    elems = out_hbm.shape[1]
    row = iota((8, elems), 0)
    for corner in range(8):
        mine = row == high_id[corner : corner + 1]
        fix = jnp.where(mine, found[:, corner * elems : (corner + 1) * elems], 0.0)
        at = corner_row(corner)
        add_rows(out_ref, pl.ds(at, 1), jnp.sum(fix, axis=0, keepdims=True))
    copies = lane_copies(out_hbm, out_ref, sems, True)
    for copy in copies:
        copy.start()
    for copy in copies:
        copy.wait()


VMEM = pl.BlockSpec(memory_space=pltpu.VMEM)
SMEM = pl.BlockSpec(memory_space=pltpu.SMEM)
HBM = pl.BlockSpec(memory_space=pltpu.HBM)


def params(mib):
    return pltpu.CompilerParams(vmem_limit_bytes=mib * MIB)


def cost(us):
    return pl.CostEstimate(flops=int(us * 5e8), bytes_accessed=int(us * 2e6), transcendentals=0)


def neighbours(axis):
    peers = lax.axis_size(axis)
    up = [(i, (i + 1) % peers) for i in range(peers)]
    return up, [(j, i) for i, j in up]


def exchange(down, up, group):
    up_pairs, down_pairs = neighbours("elem")
    group = lax.all_to_all(group, "clus", split_axis=0, concat_axis=0, tiled=True)
    return lax.ppermute(up, "elem", up_pairs), lax.ppermute(down, "elem", down_pairs), group


def on_device(nodal, metric, derivative, interp, face_level, face_target, slot_mortar, vertex_ids):
    elems = nodal.shape[1]
    faces = face_level.shape[0]
    slots = slot_mortar.shape[0]
    blocked = (elems // LANES, nodal.shape[0], LANES)
    total_vertices = NV_DEV * lax.axis_size("elem")
    elem_index = lax.axis_index("elem").astype(jnp.int32).reshape(1)
    group_slots = slots - 2 * CAP_E
    nodal, metric, derivative, interp, face_level, face_target, slot_mortar, vertex_ids = (
        pltpu.with_memory_space_constraint(array, pltpu.HBM)
        for array in (
            nodal, metric, derivative, interp, face_level, face_target, slot_mortar, vertex_ids
        )
    )
    maps_shape = pltpu.VMEM((4 * SQ, 3 * SQ), bf16)

    (
        down, up, group, traces, columns, slot_level, maps,
        level, target, slot_row, interp_in, derivative_in, vertex_in,
    ) = pl.pallas_call(
        functools.partial(send_kernel, total_vertices),
        in_specs=[SMEM] + [HBM] * 7,
        out_specs=[VMEM, VMEM, HBM] + [VMEM] * 10,
        out_shape=[
            pltpu.VMEM((SQ, CAP_E), f32),
            pltpu.VMEM((SQ, CAP_E), f32),
            jax.ShapeDtypeStruct((group_slots, LANES), f32),
            pltpu.VMEM((2 * SQ + 16, faces), bf16),
            pltpu.VMEM((faces, LANES), jnp.int32),
            pltpu.VMEM((8, slots), f32),
            maps_shape,
            pltpu.VMEM((1, faces), jnp.int32),
            pltpu.VMEM((1, faces), jnp.int32),
            pltpu.VMEM((1, slots), jnp.int32),
            pltpu.VMEM(interp.shape, f32),
            pltpu.VMEM(derivative.shape, f32),
            pltpu.VMEM(vertex_ids.shape, jnp.int32),
        ],
        scratch_shapes=[
            pltpu.VMEM(blocked, f32),
            pltpu.VMEM((group_slots, LANES), f32),
            pltpu.SemaphoreType.DMA((blocked[0],)),
            pltpu.SemaphoreType.DMA((7,)),
        ],
        compiler_params=params(16),
        name="send",
    )(elem_index, nodal, face_level, face_target, slot_mortar, interp, derivative, vertex_ids)

    from_up, from_down, group_in = exchange(down, up, group)

    mortar, local_answers, equal, stiff, back_maps, grad_map, div_map = pl.pallas_call(
        local_kernel,
        in_specs=[HBM, HBM] + [VMEM] * 7,
        out_specs=[VMEM] * 7,
        out_shape=[
            pltpu.VMEM((SQ, M_DEV), f32),
            pltpu.VMEM((SQ, slots), f32),
            pltpu.VMEM((slots, slots), bf16),
            pltpu.VMEM(nodal.shape, f32),
            maps_shape,
            pltpu.VMEM((2 * SQ, 3 * SQ), bf16),
            pltpu.VMEM((SQ, 6 * SQ), bf16),
        ],
        scratch_shapes=[
            pltpu.VMEM(blocked, f32),
            pltpu.VMEM(nodal.shape, bf16),
            pltpu.VMEM(nodal.shape, f32),
            pltpu.SemaphoreType.DMA((blocked[0],)),
            pltpu.SemaphoreType.DMA,
        ],
        compiler_params=params(16),
        cost_estimate=cost(3),
        name="local",
    )(nodal, metric, traces, maps, level, columns, slot_row, interp_in, derivative_in)

    down, up, group, incoming, sums = pl.pallas_call(
        answer_kernel,
        in_specs=[VMEM] * 5,
        out_specs=[VMEM, VMEM, HBM, VMEM, VMEM],
        out_shape=[
            pltpu.VMEM((SQ + 8, CAP_E), f32),
            pltpu.VMEM((SQ + 8, CAP_E), f32),
            jax.ShapeDtypeStruct((group_slots, LANES), f32),
            pltpu.VMEM((SQ, slots), f32),
            pltpu.VMEM((16, LANES), f32),
        ],
        scratch_shapes=[pltpu.VMEM((group_slots, LANES), f32), pltpu.SemaphoreType.DMA],
        compiler_params=params(16),
        name="answer",
    )(from_up, from_down, group_in, equal, local_answers)

    from_up, from_down, group_in = exchange(down, up, group)

    result, remote, low_ids, high_ids = pl.pallas_call(
        functools.partial(gather_kernel, total_vertices),
        in_specs=[SMEM, HBM, HBM] + [VMEM] * 10,
        out_specs=[VMEM] * 4,
        out_shape=[
            pltpu.VMEM(blocked, f32),
            pltpu.VMEM((slots, faces), bf16),
            pltpu.VMEM((2 * HALF, 8 * elems), bf16),
            pltpu.VMEM((8, elems), jnp.int32),
        ],
        scratch_shapes=[
            pltpu.VMEM(blocked, f32),
            pltpu.VMEM((2,) + nodal.shape, bf16),
            pltpu.SemaphoreType.DMA((blocked[0],)),
            pltpu.SemaphoreType.DMA,
        ],
        compiler_params=params(16),
        cost_estimate=cost(3),
        name="gather",
    )(
        elem_index, nodal, metric, mortar, incoming, slot_row, target, level, back_maps,
        grad_map, div_map, vertex_in, stiff,
    )

    return pl.pallas_call(
        final_kernel,
        in_specs=[VMEM] * 10,
        out_specs=HBM,
        out_shape=jax.ShapeDtypeStruct(nodal.shape, f32),
        scratch_shapes=[pltpu.VMEM(blocked, f32), pltpu.SemaphoreType.DMA((blocked[0],))],
        compiler_params=params(16),
        name="final",
    )(
        from_up, from_down, group_in, slot_level, back_maps, remote, sums, high_ids, low_ids, result
    )


def solution(mesh):
    in_specs = (
        P(None, ("elem", "clus")),
        P(None, None, ("elem", "clus")),
        P(),
        P(),
        P(("elem", "clus")),
        P(("elem", "clus")),
        P(("elem", "clus")),
        P(None, ("elem", "clus")),
    )
    out_specs = P(None, ("elem", "clus"))
    return jax.shard_map(
        on_device, mesh=mesh, in_specs=in_specs, out_specs=out_specs, check_vma=False
    )
```

```python
import functools

import jax
import jax.numpy as jnp
from jax import lax
from jax.experimental import pallas as pl
from jax.experimental.pallas import tpu as pltpu
from jax.sharding import PartitionSpec as P

POINTS = 8
SQ = POINTS * POINTS
CAP_E = 128
CAP_C = 16
M_DEV = 512
NV_DEV = 256
HALF = 64
LANES = 128
MIB = 1 << 20

f32 = jnp.float32
bf16 = jnp.bfloat16
highest = lax.Precision.HIGHEST


def split(x):
    hi = x.astype(bf16)
    lo = (x - hi.astype(f32)).astype(bf16)
    return hi, lo


def stack3(x, axis=0):
    hi, lo = split(x)
    return jnp.concatenate([hi, lo, hi], axis=axis)


def stack2(x):
    hi, lo = split(x)
    return jnp.concatenate([hi, lo], axis=0)


def mm(a, b):
    return lax.dot_general(a, b, (((1,), (0,)), ((), ())), preferred_element_type=f32)


def mm_nt(a, b):
    return lax.dot_general(a, b, (((1,), (1,)), ((), ())), preferred_element_type=f32)


def iota(shape, dim):
    return lax.broadcasted_iota(jnp.int32, shape, dim)


def expand(matrix, copies):
    width = SQ * copies
    lane = iota((POINTS, width), 1) % SQ
    row = iota((POINTS, width), 0)
    to_first = (lane // POINTS == row).astype(f32)
    to_second = (lane % POINTS == row).astype(f32)
    first = jnp.dot(matrix, to_first, precision=highest, preferred_element_type=f32)
    second = jnp.dot(matrix, to_second, precision=highest, preferred_element_type=f32)
    first = jnp.broadcast_to(first[:, None, :], (POINTS, POINTS, width)).reshape(SQ, width)
    second = jnp.concatenate([second] * POINTS, axis=0)
    return first, second


def hi_hi_lo(matrix):
    hi = matrix.astype(bf16).astype(f32)
    lane = iota(matrix.shape, 1)
    return jnp.where(lane < 2 * SQ, hi, matrix - hi).astype(bf16)


def kron_four(low, high):
    low_first, low_second = expand(low, 3)
    high_first, high_second = expand(high, 3)
    maps = [
        low_first * low_second,
        low_first * high_second,
        high_first * low_second,
        high_first * high_second,
    ]
    return hi_hi_lo(jnp.concatenate(maps, axis=0))


def load_rows(ref, rows):
    return jnp.concatenate([ref[h, rows, :] for h in range(ref.shape[0])], axis=1)


def load_comb(ref, j):
    return jnp.concatenate([load_rows(ref, pl.ds(a * SQ + j * 8, 8)) for a in range(8)], axis=0)


def store_rows(ref, rows, value):
    for h in range(ref.shape[0]):
        ref[h, rows, :] = value[:, h * LANES : (h + 1) * LANES]


def add_rows(ref, rows, value):
    for h in range(ref.shape[0]):
        ref[h, rows, :] += value[:, h * LANES : (h + 1) * LANES]


def lane_copies(hbm, blocks, sems, outward):
    copies = []
    for h in range(blocks.shape[0]):
        outer = hbm.at[:, pl.ds(h * LANES, LANES)]
        ends = (blocks.at[h], outer) if outward else (outer, blocks.at[h])
        copies.append(pltpu.make_async_copy(*ends, sems.at[h]))
    return copies


def pick_level(plain, mapped, level):
    out = plain
    for number in range(1, 5):
        out = jnp.where(level == number, mapped[(number - 1) * SQ : number * SQ], out)
    return out


def one_hot_rows(ids, first, count):
    return (iota((count, ids.shape[1]), 0) + first == ids).astype(f32).astype(bf16)


def columns_of(row):
    return jnp.broadcast_to(row, (LANES, row.shape[1])).T


def one_hot_lanes(columns, first, count):
    lane = iota((columns.shape[0], LANES), 1) + first
    blocks = [columns == lane + start for start in range(0, count, LANES)]
    return jnp.concatenate([block.astype(f32).astype(bf16) for block in blocks], axis=1)


def window_ids(vertex_ids, elem_index, total):
    shifted = vertex_ids - elem_index * NV_DEV
    window = jnp.where(shifted < 0, shifted + total, shifted)
    return window // HALF, window % HALF


def low_one_hot(low_id):
    parts = []
    for corner in range(8):
        hot = one_hot_rows(low_id[corner : corner + 1], 0, HALF)
        parts.append(jnp.concatenate([jnp.zeros_like(hot), hot], axis=0))
    return jnp.concatenate(parts, axis=1)


def corner_row(corner):
    last = POINTS - 1
    return corner // 4 * last * SQ + corner // 2 % 2 * last * POINTS + corner % 2 * last


def up_goes_near(paired):
    return lax.axis_index("elem") % 2 == 0 if paired else lax.axis_index("elem") >= 0


def up_came_near(paired):
    return lax.axis_index("elem") % 2 == 1 if paired else lax.axis_index("elem") >= 0


def swap_if(flag, first, second):
    return jnp.where(flag, first, second), jnp.where(flag, second, first)


def member_rows(mask):
    member = lax.axis_index("clus")
    same = jnp.bitwise_xor(member, 2 * mask)
    other = jnp.bitwise_xor(same, 1)
    return pl.ds(pl.multiple_of(same * 16, 16), 16), pl.ds(pl.multiple_of(other * 16, 16), 16)


def part_group(group_ref, keep_ref, cross_ref):
    for mask in range(group_ref.shape[0] // 32):
        same, other = member_rows(mask)
        keep_ref[mask * 16 : mask * 16 + 16, :] = group_ref[same, :]
        cross_ref[mask * 16 : mask * 16 + 16, :] = group_ref[other, :]


def join_group(message_refs, group_ref):
    for mask, message_ref in enumerate(message_refs):
        same, other = member_rows(mask)
        group_ref[same, :] = message_ref[0:16, :]
        group_ref[other, :] = message_ref[16:32, :]


def merge_kernel(keep_ref, cross_ref, *message_refs):
    upper = iota((16, LANES), 1) >= HALF
    sums = jnp.where(upper, keep_ref[0:16, :] + cross_ref[0:16, :], 0.0)
    for mask, message_ref in enumerate(message_refs):
        block = keep_ref[mask * 16 : mask * 16 + 16, :]
        message_ref[0:16, :] = jnp.where(upper, sums, block)
        message_ref[16:32, :] = cross_ref[mask * 16 : mask * 16 + 16, :]


def send_kernel(
    total_vertices,
    paired,
    nodal_hbm,
    level_hbm,
    target_hbm,
    slot_hbm,
    interp_hbm,
    derivative_hbm,
    vertex_hbm,
    near_ref,
    far_ref,
    keep_ref,
    cross_ref,
    traces_ref,
    columns_ref,
    slot_level_ref,
    maps_ref,
    level_ref,
    target_ref,
    slot_mortar_ref,
    interp_ref,
    derivative_ref,
    vertex_ref,
    nodal_ref,
    group_ref,
    nodal_sems,
    sems,
):
    target_copy = pltpu.make_async_copy(target_hbm, target_ref.at[0], sems.at[0])
    level_copy = pltpu.make_async_copy(level_hbm, level_ref.at[0], sems.at[1])
    interp_copy = pltpu.make_async_copy(interp_hbm, interp_ref, sems.at[2])
    vertex_copy = pltpu.make_async_copy(vertex_hbm, vertex_ref, sems.at[3])
    slot_copy = pltpu.make_async_copy(slot_hbm, slot_mortar_ref.at[0], sems.at[4])
    derivative_copy = pltpu.make_async_copy(derivative_hbm, derivative_ref, sems.at[5])
    nodal_copies = lane_copies(nodal_hbm, nodal_ref, nodal_sems, False)
    target_copy.start()
    interp_copy.start()
    for copy in nodal_copies:
        copy.start()
    for copy in (level_copy, vertex_copy, slot_copy, derivative_copy):
        copy.start()
    slots = slot_level_ref.shape[1]
    elems = nodal_hbm.shape[1]
    target_copy.wait()
    columns = columns_of(target_ref[...])
    columns_ref[...] = columns
    remote = one_hot_lanes(columns, M_DEV, -(-slots // 256) * 256)
    interp_copy.wait()
    maps = kron_four(interp_ref[0], interp_ref[1])
    maps_ref[...] = maps
    vertex_copy.wait()
    high_id, low_id = window_ids(vertex_ref[...], lax.axis_index("elem"), total_vertices)
    low_hot = low_one_hot(low_id)

    for copy in nodal_copies:
        copy.wait()
    level_copy.wait()
    level = level_ref[...]
    faces = [
        load_rows(nodal_ref, pl.ds(0, SQ)),
        load_rows(nodal_ref, pl.ds(7 * SQ, SQ)),
        load_comb(nodal_ref, 0),
        load_comb(nodal_ref, 7),
        load_rows(nodal_ref, pl.ds(0, SQ, stride=8)),
        load_rows(nodal_ref, pl.ds(7, SQ, stride=8)),
    ]
    trace = jnp.concatenate(faces, axis=1)
    hi, lo = split(trace)
    traces_ref[0:SQ, :] = hi
    traces_ref[SQ : 2 * SQ, :] = lo
    traces_ref[2 * SQ :, :] = jnp.broadcast_to(level, (16, level.shape[1])).astype(f32).astype(bf16)

    picked = mm(traces_ref[...], remote)[:, 0:slots]
    plain = picked[0:SQ] + picked[SQ : 2 * SQ]
    slot_level = picked[2 * SQ : 2 * SQ + 8]
    slot_level_ref[...] = slot_level
    mapped = mm(maps, stack3(plain))
    sent = pick_level(plain, mapped, slot_level[0:1])
    row = iota((16, elems), 0)
    row_high = row % 4 + 4 * (row // 8)
    is_count = row // 4 % 2 == 1
    weighted = []
    for corner in range(8):
        value = load_rows(nodal_ref, pl.ds(corner_row(corner), 1))
        value_hi = value.astype(bf16).astype(f32)
        value_lo = value - value_hi
        mine = high_id[corner : corner + 1] == row_high
        first = jnp.where(mine, jnp.where(is_count, 1.0, value_hi), 0.0)
        second = jnp.where(mine & ~is_count, value_lo, 0.0)
        weighted.append(jnp.concatenate([first, second], axis=0).astype(bf16))
    sums = mm_nt(jnp.concatenate(weighted, axis=1), low_hot)
    sums = sums[0:16] + sums[16:32]
    group = sent[:, 2 * CAP_E :]
    group = jnp.concatenate([group, jnp.zeros_like(group)], axis=0).T
    group_ref[...] = group
    part_group(group_ref, keep_ref, cross_ref)
    keep_ref[0:16, :] += sums
    cross_ref[0:16, :] += sums
    near_ref[...], far_ref[...] = swap_if(
        up_goes_near(paired), sent[:, CAP_E : 2 * CAP_E], sent[:, 0:CAP_E]
    )
    slot_copy.wait()
    derivative_copy.wait()


def stiffness_maps(matrix):
    row = iota((SQ, 3 * SQ), 0)
    lane = iota((SQ, 3 * SQ), 1) % SQ
    first, second = expand(matrix, 3)
    outer = jnp.where(row % 8 == lane % 8, first, 0.0)
    inner = jnp.where(row // 8 == lane // 8, second, 0.0)
    return hi_hi_lo(outer), hi_hi_lo(inner)


def local_kernel(
    nodal_hbm,
    metric_hbm,
    traces_ref,
    maps_ref,
    level_ref,
    columns_ref,
    slot_mortar_ref,
    interp_ref,
    derivative_ref,
    mortar_ref,
    answers_ref,
    equal_ref,
    stiff_ref,
    back_maps_ref,
    grad_map_ref,
    div_map_ref,
    nodal_ref,
    metric_ref,
    by_row,
    nodal_sems,
    sem,
):
    nodal_copies = lane_copies(nodal_hbm, nodal_ref, nodal_sems, False)
    metric_copy = pltpu.make_async_copy(metric_hbm.at[0], metric_ref, sem)
    for copy in nodal_copies:
        copy.start()
    metric_copy.start()
    hi = traces_ref[0:SQ, :]
    lo = traces_ref[SQ : 2 * SQ, :]
    plain = hi.astype(f32) + lo.astype(f32)
    mapped = mm(maps_ref[...], jnp.concatenate([hi, lo, hi], axis=0))
    projected = pick_level(plain, mapped, level_ref[...])
    mortar = mm(stack2(projected), one_hot_lanes(columns_ref[...], 0, M_DEV))
    mortar = mortar[0:SQ] + mortar[SQ:]
    mortar_ref[...] = mortar
    slot_row = slot_mortar_ref[...]
    answers = mm(stack2(mortar), one_hot_rows(slot_row, 0, M_DEV))
    answers_ref[...] = answers[0:SQ] + answers[SQ:]
    equal_ref[...] = (columns_of(slot_row)[:, 0:1] == slot_row).astype(f32).astype(bf16)

    back_maps_ref[...] = kron_four(interp_ref[0].T, interp_ref[1].T)
    outer, inner = stiffness_maps(derivative_ref[...])
    outer_t, inner_t = stiffness_maps(derivative_ref[...].T)
    grad_map_ref[0:SQ, :] = outer
    grad_map_ref[SQ:, :] = inner
    div_map_ref[...] = jnp.concatenate([outer_t, inner_t], axis=1)
    for copy in nodal_copies:
        copy.wait()
    metric_copy.wait()
    first_direction(nodal_ref, metric_ref, outer, outer_t, stiff_ref, by_row)


def first_direction(nodal_ref, metric_ref, outer, outer_t, stiff_ref, by_row):
    for i in range(8):
        by_row[i * SQ : (i + 1) * SQ, :] = metric_ref[i * SQ : (i + 1) * SQ, :].astype(f32)
    grads = [mm(outer, stack3(load_comb(nodal_ref, j))) for j in range(8)]
    weighted = []
    for j in range(8):
        factor = [by_row[i * SQ + j * 8 : i * SQ + j * 8 + 8, :] for i in range(8)]
        weighted.append(stack3(grads[j] * jnp.concatenate(factor, axis=0)))
    for j in range(8):
        out = mm(outer_t, weighted[j])
        for i in range(8):
            stiff_ref[i * SQ + j * 8 : i * SQ + j * 8 + 8, :] = out[i * 8 : i * 8 + 8]


def other_directions(nodal_ref, metric_ref, grad_map, div_map, stiff_ref, result_ref):
    slabs = [pl.ds(i * SQ, SQ) for i in range(8)]
    grads = [mm(grad_map, stack3(load_rows(nodal_ref, slab))) for slab in slabs]
    weighted = []
    for slab, grad in zip(slabs, grads):
        second = stack3(grad[0:SQ] * metric_ref[0, slab, :].astype(f32))
        third = stack3(grad[SQ:] * metric_ref[1, slab, :].astype(f32))
        weighted.append(jnp.concatenate([second, third], axis=0))
    for slab, part in zip(slabs, weighted):
        store_rows(result_ref, slab, stiff_ref[slab, :] + mm(div_map, part))


def answer_kernel(
    paired,
    near_in_ref,
    far_in_ref,
    equal_ref,
    local_answers_ref,
    *refs,
):
    *message_refs, near_ref, far_ref, keep_ref, cross_ref, incoming_ref, sums_ref, group_ref = refs
    join_group(message_refs, group_ref)
    from_up, from_down = swap_if(
        up_came_near(paired), near_in_ref[...], far_in_ref[...]
    )
    incoming = jnp.concatenate([from_up, from_down, group_ref[...].T[0:SQ]], axis=1)
    incoming_ref[...] = incoming
    added = mm(stack2(incoming), equal_ref[...])
    answers = local_answers_ref[...] + added[0:SQ] + added[SQ:]
    group = answers[:, 2 * CAP_E :]
    group_ref[...] = jnp.concatenate([group, jnp.zeros_like(group)], axis=0).T
    part_group(group_ref, keep_ref, cross_ref)
    sums = message_refs[0][0:16, :]
    for message_ref in message_refs[1:]:
        sums = sums + message_ref[0:16, :]
    sums_ref[...] = sums
    down = jnp.concatenate([answers[:, 0:CAP_E], sums[0:8]], axis=0)
    up = jnp.concatenate([answers[:, CAP_E : 2 * CAP_E], sums[8:16]], axis=0)
    near_ref[...], far_ref[...] = swap_if(up_goes_near(paired), up, down)


def gather_kernel(
    total_vertices,
    nodal_hbm,
    metric_hbm,
    mortar_ref,
    incoming_ref,
    slot_mortar_ref,
    target_ref,
    level_ref,
    back_maps_ref,
    grad_map_ref,
    div_map_ref,
    vertex_ref,
    stiff_ref,
    result_ref,
    remote_ref,
    low_ids_ref,
    high_ids_ref,
    nodal_ref,
    metric_ref,
    nodal_sems,
    sem,
):
    nodal_copies = lane_copies(nodal_hbm, nodal_ref, nodal_sems, False)
    metric_copy = pltpu.make_async_copy(metric_hbm.at[1:3], metric_ref, sem)
    for copy in nodal_copies:
        copy.start()
    metric_copy.start()
    slot_hot = one_hot_lanes(columns_of(slot_mortar_ref[...]), 0, M_DEV)
    added = mm(stack2(incoming_ref[...]), slot_hot)
    mortar = mortar_ref[...] + added[0:SQ] + added[SQ:]
    target = target_ref[...]
    picked = mm(stack2(mortar), one_hot_rows(target, 0, M_DEV))
    picked = picked[0:SQ] + picked[SQ:]
    back = pick_level(picked, mm(back_maps_ref[...], stack3(picked)), level_ref[...])
    remote_ref[...] = one_hot_rows(target, M_DEV, remote_ref.shape[0])
    high_id, low_id = window_ids(vertex_ref[...], lax.axis_index("elem"), total_vertices)
    high_ids_ref[...] = high_id
    low_ids_ref[...] = low_one_hot(low_id)
    for copy in nodal_copies:
        copy.wait()
    metric_copy.wait()
    other_directions(
        nodal_ref, metric_ref, grad_map_ref[...], div_map_ref[...], stiff_ref, result_ref
    )
    add_faces(result_ref, back)


def add_faces(ref, back):
    elems = ref.shape[0] * LANES
    parts = [back[:, f * elems : (f + 1) * elems] for f in range(6)]
    add_rows(ref, pl.ds(0, SQ), parts[0])
    add_rows(ref, pl.ds(7 * SQ, SQ), parts[1])
    for a in range(8):
        add_rows(ref, pl.ds(a * SQ, 8), parts[2][a * 8 : a * 8 + 8])
        add_rows(ref, pl.ds(a * SQ + 56, 8), parts[3][a * 8 : a * 8 + 8])
    add_rows(ref, pl.ds(0, SQ, stride=8), parts[4])
    add_rows(ref, pl.ds(7, SQ, stride=8), parts[5])


def final_kernel(
    paired,
    near_in_ref,
    far_in_ref,
    slot_level_ref,
    maps_ref,
    remote_ref,
    sums_ref,
    high_ids_ref,
    low_ids_ref,
    result_ref,
    *refs,
):
    *message_refs, out_hbm, out_ref, group_ref, sems = refs
    join_group(message_refs, group_ref)
    from_up, from_down = swap_if(
        up_came_near(paired), near_in_ref[...], far_in_ref[...]
    )
    arrived = jnp.concatenate([from_up[0:SQ], from_down[0:SQ], group_ref[...].T[0:SQ]], axis=1)
    slot_back = pick_level(arrived, mm(maps_ref[...], stack3(arrived)), slot_level_ref[0:1, :])
    back = mm(stack2(slot_back), remote_ref[...])
    back = back[0:SQ] + back[SQ:]

    first = sums_ref[0:8, :] + from_up[SQ:]
    second = sums_ref[8:16, :] + from_down[SQ:]
    totals = jnp.concatenate([first[0:4], second[0:4]], axis=0)
    counts = jnp.concatenate([first[4:8], second[4:8]], axis=0)
    coarse = jnp.where(iota(totals.shape, 1) < HALF, 0.0, totals / (1.0 + counts))
    coarse_hi = coarse.astype(bf16).astype(f32)
    table = jnp.concatenate([coarse_hi, coarse - coarse_hi], axis=0).astype(bf16)
    found = mm(table, low_ids_ref[...])
    found = found[0:8] + found[8:16]
    high_id = high_ids_ref[...]

    out_ref[...] = result_ref[...]
    add_faces(out_ref, back)
    elems = out_hbm.shape[1]
    row = iota((8, elems), 0)
    for corner in range(8):
        mine = row == high_id[corner : corner + 1]
        fix = jnp.where(mine, found[:, corner * elems : (corner + 1) * elems], 0.0)
        at = corner_row(corner)
        add_rows(out_ref, pl.ds(at, 1), jnp.sum(fix, axis=0, keepdims=True))
    copies = lane_copies(out_hbm, out_ref, sems, True)
    for copy in copies:
        copy.start()
    for copy in copies:
        copy.wait()


VMEM = pl.BlockSpec(memory_space=pltpu.VMEM)
HBM = pl.BlockSpec(memory_space=pltpu.HBM)


def params(mib):
    return pltpu.CompilerParams(vmem_limit_bytes=mib * MIB)


def cost(us):
    return pl.CostEstimate(flops=int(us * 5e8), bytes_accessed=int(us * 2e6), transcendentals=0)


def curve_swap(near, far):
    peers = lax.axis_size("elem")
    up = [(i, (i + 1) % peers) for i in range(peers)]
    near_pairs, far_pairs = up, [(j, i) for i, j in up]
    if peers % 2 == 0:
        near_pairs = [(i, i ^ 1) for i in range(peers)]
        far_pairs = [(i, (i + 1 if i % 2 else i - 1) % peers) for i in range(peers)]
    return lax.ppermute(near, "elem", near_pairs), lax.ppermute(far, "elem", far_pairs)


def group_swap(keep, cross):
    members = lax.axis_size("clus")
    chips = members // 2
    cross = lax.ppermute(cross, "clus", [(i, i ^ 1) for i in range(members)])
    messages = pl.pallas_call(
        merge_kernel,
        in_specs=[VMEM] * 2,
        out_specs=[VMEM] * chips,
        out_shape=[pltpu.VMEM((32, LANES), f32)] * chips,
        compiler_params=params(16),
        name="merge",
    )(keep, cross)
    return [messages[0]] + [
        lax.ppermute(messages[mask], "clus", [(i, i ^ (2 * mask)) for i in range(members)])
        for mask in range(1, chips)
    ]


def on_device(nodal, metric, derivative, interp, face_level, face_target, slot_mortar, vertex_ids):
    elems = nodal.shape[1]
    faces = face_level.shape[0]
    slots = slot_mortar.shape[0]
    blocked = (elems // LANES, nodal.shape[0], LANES)
    total_vertices = NV_DEV * lax.axis_size("elem")
    paired = lax.axis_size("elem") % 2 == 0
    group_slots = slots - 2 * CAP_E
    half_group = pltpu.VMEM((group_slots // 2, LANES), f32)
    nodal, metric, derivative, interp, face_level, face_target, slot_mortar, vertex_ids = (
        pltpu.with_memory_space_constraint(array, pltpu.HBM)
        for array in (
            nodal, metric, derivative, interp, face_level, face_target, slot_mortar, vertex_ids
        )
    )
    maps_shape = pltpu.VMEM((4 * SQ, 3 * SQ), bf16)

    (
        near, far, keep, cross, traces, columns, slot_level, maps,
        level, target, slot_row, interp_in, derivative_in, vertex_in,
    ) = pl.pallas_call(
        functools.partial(send_kernel, total_vertices, paired),
        in_specs=[HBM] * 7,
        out_specs=[VMEM] * 14,
        out_shape=[
            pltpu.VMEM((SQ, CAP_E), f32),
            pltpu.VMEM((SQ, CAP_E), f32),
            half_group,
            half_group,
            pltpu.VMEM((2 * SQ + 16, faces), bf16),
            pltpu.VMEM((faces, LANES), jnp.int32),
            pltpu.VMEM((8, slots), f32),
            maps_shape,
            pltpu.VMEM((1, faces), jnp.int32),
            pltpu.VMEM((1, faces), jnp.int32),
            pltpu.VMEM((1, slots), jnp.int32),
            pltpu.VMEM(interp.shape, f32),
            pltpu.VMEM(derivative.shape, f32),
            pltpu.VMEM(vertex_ids.shape, jnp.int32),
        ],
        scratch_shapes=[
            pltpu.VMEM(blocked, f32),
            pltpu.VMEM((group_slots, LANES), f32),
            pltpu.SemaphoreType.DMA((blocked[0],)),
            pltpu.SemaphoreType.DMA((6,)),
        ],
        compiler_params=params(16),
        name="send",
    )(nodal, face_level, face_target, slot_mortar, interp, derivative, vertex_ids)

    near, far = curve_swap(near, far)
    messages = group_swap(keep, cross)

    mortar, local_answers, equal, stiff, back_maps, grad_map, div_map = pl.pallas_call(
        local_kernel,
        in_specs=[HBM, HBM] + [VMEM] * 7,
        out_specs=[VMEM] * 7,
        out_shape=[
            pltpu.VMEM((SQ, M_DEV), f32),
            pltpu.VMEM((SQ, slots), f32),
            pltpu.VMEM((slots, slots), bf16),
            pltpu.VMEM(nodal.shape, f32),
            maps_shape,
            pltpu.VMEM((2 * SQ, 3 * SQ), bf16),
            pltpu.VMEM((SQ, 6 * SQ), bf16),
        ],
        scratch_shapes=[
            pltpu.VMEM(blocked, f32),
            pltpu.VMEM(nodal.shape, bf16),
            pltpu.VMEM(nodal.shape, f32),
            pltpu.SemaphoreType.DMA((blocked[0],)),
            pltpu.SemaphoreType.DMA,
        ],
        compiler_params=params(16),
        cost_estimate=cost(3),
        name="local",
    )(nodal, metric, traces, maps, level, columns, slot_row, interp_in, derivative_in)

    near, far, keep, cross, incoming, sums = pl.pallas_call(
        functools.partial(answer_kernel, paired),
        in_specs=[VMEM] * (4 + len(messages)),
        out_specs=[VMEM] * 6,
        out_shape=[
            pltpu.VMEM((SQ + 8, CAP_E), f32),
            pltpu.VMEM((SQ + 8, CAP_E), f32),
            half_group,
            half_group,
            pltpu.VMEM((SQ, slots), f32),
            pltpu.VMEM((16, LANES), f32),
        ],
        scratch_shapes=[pltpu.VMEM((group_slots, LANES), f32)],
        compiler_params=params(16),
        name="answer",
    )(near, far, equal, local_answers, *messages)

    near, far = curve_swap(near, far)
    messages = group_swap(keep, cross)

    result, remote, low_ids, high_ids = pl.pallas_call(
        functools.partial(gather_kernel, total_vertices),
        in_specs=[HBM, HBM] + [VMEM] * 10,
        out_specs=[VMEM] * 4,
        out_shape=[
            pltpu.VMEM(blocked, f32),
            pltpu.VMEM((slots, faces), bf16),
            pltpu.VMEM((2 * HALF, 8 * elems), bf16),
            pltpu.VMEM((8, elems), jnp.int32),
        ],
        scratch_shapes=[
            pltpu.VMEM(blocked, f32),
            pltpu.VMEM((2,) + nodal.shape, bf16),
            pltpu.SemaphoreType.DMA((blocked[0],)),
            pltpu.SemaphoreType.DMA,
        ],
        compiler_params=params(16),
        cost_estimate=cost(3),
        name="gather",
    )(
        nodal, metric, mortar, incoming, slot_row, target, level, back_maps,
        grad_map, div_map, vertex_in, stiff,
    )

    return pl.pallas_call(
        functools.partial(final_kernel, paired),
        in_specs=[VMEM] * (9 + len(messages)),
        out_specs=HBM,
        out_shape=jax.ShapeDtypeStruct(nodal.shape, f32),
        scratch_shapes=[
            pltpu.VMEM(blocked, f32),
            pltpu.VMEM((group_slots, LANES), f32),
            pltpu.SemaphoreType.DMA((blocked[0],)),
        ],
        compiler_params=params(16),
        name="final",
    )(
        near, far, slot_level, back_maps, remote, sums, high_ids, low_ids, result, *messages
    )


def solution(mesh):
    in_specs = (
        P(None, ("elem", "clus")),
        P(None, None, ("elem", "clus")),
        P(),
        P(),
        P(("elem", "clus")),
        P(("elem", "clus")),
        P(("elem", "clus")),
        P(None, ("elem", "clus")),
    )
    out_specs = P(None, ("elem", "clus"))
    return jax.shard_map(
        on_device, mesh=mesh, in_specs=in_specs, out_specs=out_specs, check_vma=False
    )
```

```python
import functools

import jax
import jax.numpy as jnp
from jax import lax
from jax.experimental import pallas as pl
from jax.experimental.pallas import tpu as pltpu
from jax.sharding import PartitionSpec as P

POINTS = 8
SQ = POINTS * POINTS
CAP_E = 128
CAP_C = 16
M_DEV = 512
NV_DEV = 256
HALF = 64
LANES = 128
MIB = 1 << 20

f32 = jnp.float32
bf16 = jnp.bfloat16
highest = lax.Precision.HIGHEST


def split(x):
    hi = x.astype(bf16)
    lo = (x - hi.astype(f32)).astype(bf16)
    return hi, lo


def stack3(x, axis=0):
    hi, lo = split(x)
    return jnp.concatenate([hi, lo, hi], axis=axis)


def stack2(x):
    hi, lo = split(x)
    return jnp.concatenate([hi, lo], axis=0)


def mm(a, b):
    return lax.dot_general(a, b, (((1,), (0,)), ((), ())), preferred_element_type=f32)


def mm_nt(a, b):
    return lax.dot_general(a, b, (((1,), (1,)), ((), ())), preferred_element_type=f32)


def iota(shape, dim):
    return lax.broadcasted_iota(jnp.int32, shape, dim)


def expand(matrix, copies):
    width = SQ * copies
    lane = iota((POINTS, width), 1) % SQ
    row = iota((POINTS, width), 0)
    to_first = (lane // POINTS == row).astype(f32)
    to_second = (lane % POINTS == row).astype(f32)
    first = jnp.dot(matrix, to_first, precision=highest, preferred_element_type=f32)
    second = jnp.dot(matrix, to_second, precision=highest, preferred_element_type=f32)
    first = jnp.broadcast_to(first[:, None, :], (POINTS, POINTS, width)).reshape(SQ, width)
    second = jnp.concatenate([second] * POINTS, axis=0)
    return first, second


def hi_hi_lo(matrix):
    hi = matrix.astype(bf16).astype(f32)
    lane = iota(matrix.shape, 1)
    return jnp.where(lane < 2 * SQ, hi, matrix - hi).astype(bf16)


def kron_four(low, high):
    low_first, low_second = expand(low, 3)
    high_first, high_second = expand(high, 3)
    maps = [
        low_first * low_second,
        low_first * high_second,
        high_first * low_second,
        high_first * high_second,
    ]
    return hi_hi_lo(jnp.concatenate(maps, axis=0))


def load_rows(ref, rows):
    return jnp.concatenate([ref[h, rows, :] for h in range(ref.shape[0])], axis=1)


def load_comb(ref, j):
    return jnp.concatenate([load_rows(ref, pl.ds(a * SQ + j * 8, 8)) for a in range(8)], axis=0)


def store_rows(ref, rows, value):
    for h in range(ref.shape[0]):
        ref[h, rows, :] = value[:, h * LANES : (h + 1) * LANES]


def add_rows(ref, rows, value):
    for h in range(ref.shape[0]):
        ref[h, rows, :] += value[:, h * LANES : (h + 1) * LANES]


def lane_copies(hbm, blocks, sems):
    return [
        pltpu.make_async_copy(hbm.at[:, pl.ds(h * LANES, LANES)], blocks.at[h], sems.at[h])
        for h in range(blocks.shape[0])
    ]


def pick_level(plain, mapped, level):
    out = plain
    for number in range(1, 5):
        out = jnp.where(level == number, mapped[(number - 1) * SQ : number * SQ], out)
    return out


def one_hot_rows(ids, first, count):
    return (iota((count, ids.shape[1]), 0) + first == ids).astype(f32).astype(bf16)


def columns_of(row):
    return jnp.broadcast_to(row, (LANES, row.shape[1])).T


def one_hot_lanes(columns, first, count):
    lane = iota((columns.shape[0], LANES), 1) + first
    blocks = [columns == lane + start for start in range(0, count, LANES)]
    return jnp.concatenate([block.astype(f32).astype(bf16) for block in blocks], axis=1)


def window_ids(vertex_ids, elem_index, total):
    shifted = vertex_ids - elem_index * NV_DEV
    window = jnp.where(shifted < 0, shifted + total, shifted)
    return window // HALF, window % HALF


def low_one_hot(low_id):
    parts = []
    for corner in range(8):
        hot = one_hot_rows(low_id[corner : corner + 1], 0, HALF)
        parts.append(jnp.concatenate([jnp.zeros_like(hot), hot], axis=0))
    return jnp.concatenate(parts, axis=1)


def corner_row(corner):
    last = POINTS - 1
    return corner // 4 * last * SQ + corner // 2 % 2 * last * POINTS + corner % 2 * last


def up_goes_near(paired):
    return lax.axis_index("elem") % 2 == 0 if paired else lax.axis_index("elem") >= 0


def up_came_near(paired):
    return lax.axis_index("elem") % 2 == 1 if paired else lax.axis_index("elem") >= 0


def swap_if(flag, first, second):
    return jnp.where(flag, first, second), jnp.where(flag, second, first)


def member_rows(mask):
    member = lax.axis_index("clus")
    same = jnp.bitwise_xor(member, 2 * mask)
    other = jnp.bitwise_xor(same, 1)
    return pl.ds(pl.multiple_of(same * 16, 16), 16), pl.ds(pl.multiple_of(other * 16, 16), 16)


def chip_masks(chips):
    return [0] + list(range(chips - 1, 0, -1))


def part_group(group_ref, keep_ref, cross_ref):
    for mask in range(group_ref.shape[0] // 32):
        same, other = member_rows(mask)
        keep_ref[mask * 16 : mask * 16 + 16, :] = group_ref[same, :]
        cross_ref[mask * 16 : mask * 16 + 16, :] = group_ref[other, :]


def join_group(message_refs, group_ref):
    for mask, message_ref in zip(chip_masks(len(message_refs)), message_refs):
        same, other = member_rows(mask)
        group_ref[same, :] = message_ref[0:16, :]
        group_ref[other, :] = message_ref[16:32, :]


def merge_kernel(keep_ref, cross_ref, *message_refs):
    upper = iota((16, LANES), 1) >= HALF
    sums = jnp.where(upper, keep_ref[0:16, :] + cross_ref[0:16, :], 0.0)
    for mask, message_ref in enumerate(message_refs):
        block = keep_ref[mask * 16 : mask * 16 + 16, :]
        message_ref[0:16, :] = jnp.where(upper, sums, block)
        message_ref[16:32, :] = cross_ref[mask * 16 : mask * 16 + 16, :]


def send_kernel(
    total_vertices,
    paired,
    nodal_hbm,
    level_hbm,
    target_hbm,
    slot_hbm,
    interp_hbm,
    derivative_hbm,
    vertex_hbm,
    near_ref,
    far_ref,
    keep_ref,
    cross_ref,
    traces_ref,
    columns_ref,
    slot_level_ref,
    maps_ref,
    level_ref,
    target_ref,
    slot_mortar_ref,
    interp_ref,
    derivative_ref,
    vertex_ref,
    nodal_ref,
    group_ref,
    nodal_sems,
    sems,
):
    target_copy = pltpu.make_async_copy(target_hbm, target_ref.at[0], sems.at[0])
    level_copy = pltpu.make_async_copy(level_hbm, level_ref.at[0], sems.at[1])
    interp_copy = pltpu.make_async_copy(interp_hbm, interp_ref, sems.at[2])
    vertex_copy = pltpu.make_async_copy(vertex_hbm, vertex_ref, sems.at[3])
    slot_copy = pltpu.make_async_copy(slot_hbm, slot_mortar_ref.at[0], sems.at[4])
    derivative_copy = pltpu.make_async_copy(derivative_hbm, derivative_ref, sems.at[5])
    nodal_copies = lane_copies(nodal_hbm, nodal_ref, nodal_sems)
    target_copy.start()
    interp_copy.start()
    for copy in nodal_copies:
        copy.start()
    for copy in (level_copy, vertex_copy, slot_copy, derivative_copy):
        copy.start()
    slots = slot_level_ref.shape[1]
    elems = nodal_hbm.shape[1]
    target_copy.wait()
    columns = columns_of(target_ref[...])
    columns_ref[...] = columns
    remote = one_hot_lanes(columns, M_DEV, -(-slots // 256) * 256)
    interp_copy.wait()
    maps = kron_four(interp_ref[0], interp_ref[1])
    maps_ref[...] = maps
    vertex_copy.wait()
    high_id, low_id = window_ids(vertex_ref[...], lax.axis_index("elem"), total_vertices)
    low_hot = low_one_hot(low_id)

    for copy in nodal_copies:
        copy.wait()
    level_copy.wait()
    level = level_ref[...]
    faces = [
        load_rows(nodal_ref, pl.ds(0, SQ)),
        load_rows(nodal_ref, pl.ds(7 * SQ, SQ)),
        load_comb(nodal_ref, 0),
        load_comb(nodal_ref, 7),
        load_rows(nodal_ref, pl.ds(0, SQ, stride=8)),
        load_rows(nodal_ref, pl.ds(7, SQ, stride=8)),
    ]
    trace = jnp.concatenate(faces, axis=1)
    hi, lo = split(trace)
    traces_ref[0:SQ, :] = hi
    traces_ref[SQ : 2 * SQ, :] = lo
    traces_ref[2 * SQ :, :] = jnp.broadcast_to(level, (16, level.shape[1])).astype(f32).astype(bf16)

    picked = mm(traces_ref[...], remote)[:, 0:slots]
    plain = picked[0:SQ] + picked[SQ : 2 * SQ]
    slot_level = picked[2 * SQ : 2 * SQ + 8]
    slot_level_ref[...] = slot_level
    sent = pick_level(plain, mm(maps, stack3(plain)), slot_level[0:1])

    row = iota((16, elems), 0)
    row_high = row % 4 + 4 * (row // 8)
    is_count = row // 4 % 2 == 1
    weighted = []
    for corner in range(8):
        value = load_rows(nodal_ref, pl.ds(corner_row(corner), 1))
        value_hi = value.astype(bf16).astype(f32)
        value_lo = value - value_hi
        mine = high_id[corner : corner + 1] == row_high
        first = jnp.where(mine, jnp.where(is_count, 1.0, value_hi), 0.0)
        second = jnp.where(mine & ~is_count, value_lo, 0.0)
        weighted.append(jnp.concatenate([first, second], axis=0).astype(bf16))
    sums = mm_nt(jnp.concatenate(weighted, axis=1), low_hot)
    sums = sums[0:16] + sums[16:32]
    group = sent[:, 2 * CAP_E :]
    group_ref[...] = jnp.concatenate([group, jnp.zeros_like(group)], axis=0).T
    part_group(group_ref, keep_ref, cross_ref)
    keep_ref[0:16, :] += sums
    cross_ref[0:16, :] += sums
    near_ref[...], far_ref[...] = swap_if(
        up_goes_near(paired), sent[:, CAP_E : 2 * CAP_E], sent[:, 0:CAP_E]
    )
    slot_copy.wait()
    derivative_copy.wait()


def stiffness_maps(matrix):
    row = iota((SQ, 3 * SQ), 0)
    lane = iota((SQ, 3 * SQ), 1) % SQ
    first, second = expand(matrix, 3)
    outer = jnp.where(row % 8 == lane % 8, first, 0.0)
    inner = jnp.where(row // 8 == lane // 8, second, 0.0)
    return hi_hi_lo(outer), hi_hi_lo(inner)


def local_kernel(
    traces_ref,
    maps_ref,
    level_ref,
    columns_ref,
    slot_mortar_ref,
    interp_ref,
    derivative_ref,
    mortar_ref,
    answers_ref,
    equal_ref,
    back_maps_ref,
    grad_map_ref,
    div_map_ref,
):
    back_maps_ref[...] = kron_four(interp_ref[0].T, interp_ref[1].T)
    slot_row = slot_mortar_ref[...]
    equal_ref[...] = (columns_of(slot_row)[:, 0:1] == slot_row).astype(f32).astype(bf16)
    hi = traces_ref[0:SQ, :]
    lo = traces_ref[SQ : 2 * SQ, :]
    plain = hi.astype(f32) + lo.astype(f32)
    mapped = mm(maps_ref[...], jnp.concatenate([hi, lo, hi], axis=0))
    projected = pick_level(plain, mapped, level_ref[...])
    mortar = mm(stack2(projected), one_hot_lanes(columns_ref[...], 0, M_DEV))
    mortar = mortar[0:SQ] + mortar[SQ:]
    mortar_ref[...] = mortar
    answers = mm(stack2(mortar), one_hot_rows(slot_row, 0, M_DEV))
    answers_ref[...] = answers[0:SQ] + answers[SQ:]
    outer, inner = stiffness_maps(derivative_ref[...])
    outer_t, inner_t = stiffness_maps(derivative_ref[...].T)
    grad_map_ref[0:SQ, :] = outer
    grad_map_ref[SQ:, :] = inner
    div_map_ref[...] = jnp.concatenate([outer_t, inner_t], axis=1)


def first_direction(nodal_ref, metric_ref, outer, outer_t, stiff_ref, by_row):
    for i in range(8):
        by_row[i * SQ : (i + 1) * SQ, :] = metric_ref[i * SQ : (i + 1) * SQ, :].astype(f32)
    grads = [mm(outer, stack3(load_comb(nodal_ref, j))) for j in range(8)]
    weighted = []
    for j in range(8):
        factor = [by_row[i * SQ + j * 8 : i * SQ + j * 8 + 8, :] for i in range(8)]
        weighted.append(stack3(grads[j] * jnp.concatenate(factor, axis=0)))
    for j in range(8):
        out = mm(outer_t, weighted[j])
        for i in range(8):
            stiff_ref[i * SQ + j * 8 : i * SQ + j * 8 + 8, :] = out[i * 8 : i * 8 + 8]


def other_directions(nodal_ref, metric_ref, grad_map, div_map, stiff_ref, result_ref):
    slabs = [pl.ds(i * SQ, SQ) for i in range(8)]
    grads = [mm(grad_map, stack3(load_rows(nodal_ref, slab))) for slab in slabs]
    weighted = []
    for slab, grad in zip(slabs, grads):
        second = stack3(grad[0:SQ] * metric_ref[0, slab, :].astype(f32))
        third = stack3(grad[SQ:] * metric_ref[1, slab, :].astype(f32))
        weighted.append(jnp.concatenate([second, third], axis=0))
    for slab, part in zip(slabs, weighted):
        store_rows(result_ref, slab, stiff_ref[slab, :] + mm(div_map, part))


def answer_kernel(
    paired,
    near_in_ref,
    far_in_ref,
    equal_ref,
    local_answers_ref,
    *refs,
):
    *message_refs, near_ref, far_ref, keep_ref, cross_ref, incoming_ref, sums_ref, group_ref = refs
    join_group(message_refs, group_ref)
    from_up, from_down = swap_if(
        up_came_near(paired), near_in_ref[...], far_in_ref[...]
    )
    incoming = jnp.concatenate([from_up, from_down, group_ref[...].T[0:SQ]], axis=1)
    incoming_ref[...] = incoming
    added = mm(stack2(incoming), equal_ref[...])
    answers = local_answers_ref[...] + added[0:SQ] + added[SQ:]
    group = answers[:, 2 * CAP_E :]
    group_ref[...] = jnp.concatenate([group, jnp.zeros_like(group)], axis=0).T
    part_group(group_ref, keep_ref, cross_ref)
    sums = message_refs[0][0:16, :]
    for message_ref in message_refs[1:]:
        sums = sums + message_ref[0:16, :]
    sums_ref[...] = sums
    down = jnp.concatenate([answers[:, 0:CAP_E], sums[0:8]], axis=0)
    up = jnp.concatenate([answers[:, CAP_E : 2 * CAP_E], sums[8:16]], axis=0)
    near_ref[...], far_ref[...] = swap_if(up_goes_near(paired), up, down)


def gather_kernel(
    total_vertices,
    nodal_hbm,
    metric_hbm,
    mortar_ref,
    incoming_ref,
    slot_mortar_ref,
    target_ref,
    level_ref,
    back_maps_ref,
    grad_map_ref,
    div_map_ref,
    vertex_ref,
    result_ref,
    remote_ref,
    low_ids_ref,
    high_ids_ref,
    nodal_ref,
    metric_ref,
    stiff_ref,
    by_row,
    nodal_sems,
    sem,
):
    nodal_copies = lane_copies(nodal_hbm, nodal_ref, nodal_sems)
    metric_copy = pltpu.make_async_copy(metric_hbm, metric_ref, sem)
    for copy in nodal_copies:
        copy.start()
    metric_copy.start()
    slot_hot = one_hot_lanes(columns_of(slot_mortar_ref[...]), 0, M_DEV)
    added = mm(stack2(incoming_ref[...]), slot_hot)
    mortar = mortar_ref[...] + added[0:SQ] + added[SQ:]
    target = target_ref[...]
    picked = mm(stack2(mortar), one_hot_rows(target, 0, M_DEV))
    picked = picked[0:SQ] + picked[SQ:]
    back = pick_level(picked, mm(back_maps_ref[...], stack3(picked)), level_ref[...])
    remote_ref[...] = one_hot_rows(target, M_DEV, remote_ref.shape[0])
    high_id, low_id = window_ids(vertex_ref[...], lax.axis_index("elem"), total_vertices)
    high_ids_ref[...] = high_id
    low_ids_ref[...] = low_one_hot(low_id)
    for copy in nodal_copies:
        copy.wait()
    metric_copy.wait()
    first_direction(nodal_ref, metric_ref.at[0], grad_map_ref[0:SQ, :], div_map_ref[:, 0:3 * SQ], stiff_ref, by_row)
    other_directions(
        nodal_ref, metric_ref.at[1:3], grad_map_ref[...], div_map_ref[...], stiff_ref, result_ref
    )
    add_faces(result_ref, back)


def add_faces(ref, back):
    elems = ref.shape[0] * LANES
    parts = [back[:, f * elems : (f + 1) * elems] for f in range(6)]
    add_rows(ref, pl.ds(0, SQ), parts[0])
    add_rows(ref, pl.ds(7 * SQ, SQ), parts[1])
    for a in range(8):
        add_rows(ref, pl.ds(a * SQ, 8), parts[2][a * 8 : a * 8 + 8])
        add_rows(ref, pl.ds(a * SQ + 56, 8), parts[3][a * 8 : a * 8 + 8])
    add_rows(ref, pl.ds(0, SQ, stride=8), parts[4])
    add_rows(ref, pl.ds(7, SQ, stride=8), parts[5])


def final_kernel(
    paired,
    near_in_ref,
    far_in_ref,
    slot_level_ref,
    maps_ref,
    remote_ref,
    sums_ref,
    high_ids_ref,
    low_ids_ref,
    result_ref,
    *refs,
):
    *message_refs, out_hbm, out_ref, group_ref, sems = refs
    join_group(message_refs, group_ref)
    from_up, from_down = swap_if(
        up_came_near(paired), near_in_ref[...], far_in_ref[...]
    )
    arrived = jnp.concatenate([from_up[0:SQ], from_down[0:SQ], group_ref[...].T[0:SQ]], axis=1)
    slot_back = pick_level(arrived, mm(maps_ref[...], stack3(arrived)), slot_level_ref[0:1, :])
    back = mm(stack2(slot_back), remote_ref[...])
    back = back[0:SQ] + back[SQ:]

    first = sums_ref[0:8, :] + from_up[SQ:]
    second = sums_ref[8:16, :] + from_down[SQ:]
    totals = jnp.concatenate([first[0:4], second[0:4]], axis=0)
    counts = jnp.concatenate([first[4:8], second[4:8]], axis=0)
    coarse = jnp.where(iota(totals.shape, 1) < HALF, 0.0, totals / (1.0 + counts))
    coarse_hi = coarse.astype(bf16).astype(f32)
    table = jnp.concatenate([coarse_hi, coarse - coarse_hi], axis=0).astype(bf16)
    found = mm(table, low_ids_ref[...])
    found = found[0:8] + found[8:16]
    high_id = high_ids_ref[...]

    elems = out_hbm.shape[1]
    row = iota((8, elems), 0)
    fixes = []
    for corner in range(8):
        mine = row == high_id[corner : corner + 1]
        fix = jnp.where(mine, found[:, corner * elems : (corner + 1) * elems], 0.0)
        fixes.append(jnp.sum(fix, axis=0, keepdims=True))
    parts = [back[:, f * elems : (f + 1) * elems] for f in range(6)]
    copies = []
    for i in range(POINTS):
        rows = slice(i * POINTS, (i + 1) * POINTS)
        slab = load_rows(result_ref, pl.ds(i * SQ, SQ))
        if i in (0, POINTS - 1):
            slab = slab + parts[min(i, 1)]
        pieces = [slab[0:8] + parts[2][rows], slab[8:56], slab[56:64] + parts[3][rows]]
        store_rows(out_ref, pl.ds(i * SQ, SQ), jnp.concatenate(pieces, axis=0))
        add_rows(out_ref, pl.ds(i * SQ, 8, stride=8), parts[4][rows])
        add_rows(out_ref, pl.ds(i * SQ + 7, 8, stride=8), parts[5][rows])
        for corner in range(8):
            if corner_row(corner) // SQ == i:
                add_rows(out_ref, pl.ds(corner_row(corner), 1), fixes[corner])
        if i % 2:
            rows = pl.ds((i - 1) * SQ, 2 * SQ)
            for h in range(out_ref.shape[0]):
                lanes = pl.ds(h * LANES, LANES)
                copies.append(
                    pltpu.make_async_copy(
                        out_ref.at[h, rows], out_hbm.at[rows, lanes], sems.at[len(copies)]
                    )
                )
                copies[-1].start()
    for copy in copies:
        copy.wait()


VMEM = pl.BlockSpec(memory_space=pltpu.VMEM)
HBM = pl.BlockSpec(memory_space=pltpu.HBM)


def params(mib):
    return pltpu.CompilerParams(vmem_limit_bytes=mib * MIB)


def cost(us):
    return pl.CostEstimate(flops=int(us * 5e8), bytes_accessed=int(us * 2e6), transcendentals=0)


def curve_swap(near, far):
    peers = lax.axis_size("elem")
    up = [(i, (i + 1) % peers) for i in range(peers)]
    near_pairs, far_pairs = up, [(j, i) for i, j in up]
    if peers % 2 == 0:
        near_pairs = [(i, i ^ 1) for i in range(peers)]
        far_pairs = [(i, (i + 1 if i % 2 else i - 1) % peers) for i in range(peers)]
    return lax.ppermute(near, "elem", near_pairs), lax.ppermute(far, "elem", far_pairs)


def group_swap(keep, cross):
    members = lax.axis_size("clus")
    chips = members // 2
    cross = lax.ppermute(cross, "clus", [(i, i ^ 1) for i in range(members)])
    messages = pl.pallas_call(
        merge_kernel,
        in_specs=[VMEM] * 2,
        out_specs=[VMEM] * chips,
        out_shape=[pltpu.VMEM((32, LANES), f32)] * chips,
        compiler_params=params(16),
        name="merge",
    )(keep, cross)
    return [messages[0]] + [
        lax.ppermute(messages[mask], "clus", [(i, i ^ (2 * mask)) for i in range(members)])
        for mask in chip_masks(chips)[1:]
    ]


def on_device(nodal, metric, derivative, interp, face_level, face_target, slot_mortar, vertex_ids):
    elems = nodal.shape[1]
    faces = face_level.shape[0]
    slots = slot_mortar.shape[0]
    blocked = (elems // LANES, nodal.shape[0], LANES)
    total_vertices = NV_DEV * lax.axis_size("elem")
    paired = lax.axis_size("elem") % 2 == 0
    group_slots = slots - 2 * CAP_E
    half_group = pltpu.VMEM((group_slots // 2, LANES), f32)
    nodal, metric, derivative, interp, face_level, face_target, slot_mortar, vertex_ids = (
        pltpu.with_memory_space_constraint(array, pltpu.HBM)
        for array in (
            nodal, metric, derivative, interp, face_level, face_target, slot_mortar, vertex_ids
        )
    )
    maps_shape = pltpu.VMEM((4 * SQ, 3 * SQ), bf16)

    (
        near, far, keep, cross, traces, columns, slot_level, maps,
        level, target, slot_row, interp_in, derivative_in, vertex_in,
    ) = pl.pallas_call(
        functools.partial(send_kernel, total_vertices, paired),
        in_specs=[HBM] * 7,
        out_specs=[VMEM] * 14,
        out_shape=[
            pltpu.VMEM((SQ, CAP_E), f32),
            pltpu.VMEM((SQ, CAP_E), f32),
            half_group,
            half_group,
            pltpu.VMEM((2 * SQ + 16, faces), bf16),
            pltpu.VMEM((faces, LANES), jnp.int32),
            pltpu.VMEM((8, slots), f32),
            maps_shape,
            pltpu.VMEM((1, faces), jnp.int32),
            pltpu.VMEM((1, faces), jnp.int32),
            pltpu.VMEM((1, slots), jnp.int32),
            pltpu.VMEM(interp.shape, f32),
            pltpu.VMEM(derivative.shape, f32),
            pltpu.VMEM(vertex_ids.shape, jnp.int32),
        ],
        scratch_shapes=[
            pltpu.VMEM(blocked, f32),
            pltpu.VMEM((group_slots, LANES), f32),
            pltpu.SemaphoreType.DMA((blocked[0],)),
            pltpu.SemaphoreType.DMA((6,)),
        ],
        compiler_params=params(16),
        name="send",
    )(nodal, face_level, face_target, slot_mortar, interp, derivative, vertex_ids)

    near, far = curve_swap(near, far)
    messages = group_swap(keep, cross)

    mortar, local_answers, equal, back_maps, grad_map, div_map = pl.pallas_call(
        local_kernel,
        in_specs=[VMEM] * 7,
        out_specs=[VMEM] * 6,
        out_shape=[
            pltpu.VMEM((SQ, M_DEV), f32),
            pltpu.VMEM((SQ, slots), f32),
            pltpu.VMEM((slots, slots), bf16),
            maps_shape,
            pltpu.VMEM((2 * SQ, 3 * SQ), bf16),
            pltpu.VMEM((SQ, 6 * SQ), bf16),
        ],
        compiler_params=params(16),
        cost_estimate=cost(3),
        name="local",
    )(traces, maps, level, columns, slot_row, interp_in, derivative_in)

    near, far, keep, cross, incoming, sums = pl.pallas_call(
        functools.partial(answer_kernel, paired),
        in_specs=[VMEM] * (4 + len(messages)),
        out_specs=[VMEM] * 6,
        out_shape=[
            pltpu.VMEM((SQ + 8, CAP_E), f32),
            pltpu.VMEM((SQ + 8, CAP_E), f32),
            half_group,
            half_group,
            pltpu.VMEM((SQ, slots), f32),
            pltpu.VMEM((16, LANES), f32),
        ],
        scratch_shapes=[pltpu.VMEM((group_slots, LANES), f32)],
        compiler_params=params(16),
        name="answer",
    )(near, far, equal, local_answers, *messages)

    near, far = curve_swap(near, far)
    messages = group_swap(keep, cross)

    result, remote, low_ids, high_ids = pl.pallas_call(
        functools.partial(gather_kernel, total_vertices),
        in_specs=[HBM, HBM] + [VMEM] * 9,
        out_specs=[VMEM] * 4,
        out_shape=[
            pltpu.VMEM(blocked, f32),
            pltpu.VMEM((slots, faces), bf16),
            pltpu.VMEM((2 * HALF, 8 * elems), bf16),
            pltpu.VMEM((8, elems), jnp.int32),
        ],
        scratch_shapes=[
            pltpu.VMEM(blocked, f32),
            pltpu.VMEM(metric.shape, bf16),
            pltpu.VMEM(nodal.shape, f32),
            pltpu.VMEM(nodal.shape, f32),
            pltpu.SemaphoreType.DMA((blocked[0],)),
            pltpu.SemaphoreType.DMA,
        ],
        compiler_params=params(16),
        cost_estimate=cost(3),
        name="gather",
    )(
        nodal, metric, mortar, incoming, slot_row, target, level, back_maps,
        grad_map, div_map, vertex_in,
    )

    return pl.pallas_call(
        functools.partial(final_kernel, paired),
        in_specs=[VMEM] * (9 + len(messages)),
        out_specs=HBM,
        out_shape=jax.ShapeDtypeStruct(nodal.shape, f32),
        scratch_shapes=[
            pltpu.VMEM(blocked, f32),
            pltpu.VMEM((group_slots, LANES), f32),
            pltpu.SemaphoreType.DMA((POINTS // 2 * blocked[0],)),
        ],
        compiler_params=params(16),
        name="final",
    )(
        near, far, slot_level, back_maps, remote, sums, high_ids, low_ids, result, *messages
    )


def solution(mesh):
    in_specs = (
        P(None, ("elem", "clus")),
        P(None, None, ("elem", "clus")),
        P(),
        P(),
        P(("elem", "clus")),
        P(("elem", "clus")),
        P(("elem", "clus")),
        P(None, ("elem", "clus")),
    )
    out_specs = P(None, ("elem", "clus"))
    return jax.shard_map(
        on_device, mesh=mesh, in_specs=in_specs, out_specs=out_specs, check_vma=False
    )
```

```python
import functools

import jax
import jax.numpy as jnp
from jax import lax
from jax.experimental import pallas as pl
from jax.experimental.pallas import tpu as pltpu
from jax.sharding import PartitionSpec as P

POINTS = 8
SQ = POINTS * POINTS
CAP_E = 128
CAP_C = 16
M_DEV = 512
NV_DEV = 256
HALF = 64
LANES = 128
MIB = 1 << 20

f32 = jnp.float32
bf16 = jnp.bfloat16
highest = lax.Precision.HIGHEST


def split(x):
    hi = x.astype(bf16)
    lo = (x - hi.astype(f32)).astype(bf16)
    return hi, lo


def stack3(x, axis=0):
    hi, lo = split(x)
    return jnp.concatenate([hi, lo, hi], axis=axis)


def stack2(x):
    hi, lo = split(x)
    return jnp.concatenate([hi, lo], axis=0)


def mm(a, b):
    return lax.dot_general(a, b, (((1,), (0,)), ((), ())), preferred_element_type=f32)


def mm_nt(a, b):
    return lax.dot_general(a, b, (((1,), (1,)), ((), ())), preferred_element_type=f32)


def iota(shape, dim):
    return lax.broadcasted_iota(jnp.int32, shape, dim)


def expand(matrix, copies):
    width = SQ * copies
    lane = iota((POINTS, width), 1) % SQ
    row = iota((POINTS, width), 0)
    to_first = (lane // POINTS == row).astype(f32)
    to_second = (lane % POINTS == row).astype(f32)
    first = jnp.dot(matrix, to_first, precision=highest, preferred_element_type=f32)
    second = jnp.dot(matrix, to_second, precision=highest, preferred_element_type=f32)
    first = jnp.broadcast_to(first[:, None, :], (POINTS, POINTS, width)).reshape(SQ, width)
    second = jnp.concatenate([second] * POINTS, axis=0)
    return first, second


def hi_hi_lo(matrix):
    hi = matrix.astype(bf16).astype(f32)
    lane = iota(matrix.shape, 1)
    return jnp.where(lane < 2 * SQ, hi, matrix - hi).astype(bf16)


def kron_four(low, high):
    low_first, low_second = expand(low, 3)
    high_first, high_second = expand(high, 3)
    maps = [
        low_first * low_second,
        low_first * high_second,
        high_first * low_second,
        high_first * high_second,
    ]
    return hi_hi_lo(jnp.concatenate(maps, axis=0))


def load_rows(ref, rows):
    return jnp.concatenate([ref[h, rows, :] for h in range(ref.shape[0])], axis=1)


def load_comb(ref, j):
    return jnp.concatenate([load_rows(ref, pl.ds(a * SQ + j * 8, 8)) for a in range(8)], axis=0)


def store_rows(ref, rows, value):
    for h in range(ref.shape[0]):
        ref[h, rows, :] = value[:, h * LANES : (h + 1) * LANES]


def add_rows(ref, rows, value):
    for h in range(ref.shape[0]):
        ref[h, rows, :] += value[:, h * LANES : (h + 1) * LANES]


def lane_copies(hbm, blocks, sems):
    return [
        pltpu.make_async_copy(hbm.at[:, pl.ds(h * LANES, LANES)], blocks.at[h], sems.at[h])
        for h in range(blocks.shape[0])
    ]


def pick_level(plain, mapped, level):
    out = plain
    for number in range(1, 5):
        out = jnp.where(level == number, mapped[(number - 1) * SQ : number * SQ], out)
    return out


def one_hot_rows(ids, first, count):
    return (iota((count, ids.shape[1]), 0) + first == ids).astype(f32).astype(bf16)


def columns_of(row):
    return jnp.broadcast_to(row, (LANES, row.shape[1])).T


def one_hot_lanes(columns, first, count):
    lane = iota((columns.shape[0], LANES), 1) + first
    blocks = [columns == lane + start for start in range(0, count, LANES)]
    return jnp.concatenate([block.astype(f32).astype(bf16) for block in blocks], axis=1)


def window_ids(vertex_ids, elem_index, total):
    shifted = vertex_ids - elem_index * NV_DEV
    window = jnp.where(shifted < 0, shifted + total, shifted)
    return window // HALF, window % HALF


def low_one_hot(low_id):
    parts = []
    for corner in range(8):
        hot = one_hot_rows(low_id[corner : corner + 1], 0, HALF)
        parts.append(jnp.concatenate([jnp.zeros_like(hot), hot], axis=0))
    return jnp.concatenate(parts, axis=1)


def corner_row(corner):
    last = POINTS - 1
    return corner // 4 * last * SQ + corner // 2 % 2 * last * POINTS + corner % 2 * last


def up_goes_near(paired):
    return lax.axis_index("elem") % 2 == 0 if paired else lax.axis_index("elem") >= 0


def up_came_near(paired):
    return lax.axis_index("elem") % 2 == 1 if paired else lax.axis_index("elem") >= 0


def swap_if(flag, first, second):
    return jnp.where(flag, first, second), jnp.where(flag, second, first)


def member_rows(mask):
    member = lax.axis_index("clus")
    same = jnp.bitwise_xor(member, 2 * mask + (mask > 0))
    other = jnp.bitwise_xor(same, 1)
    return pl.ds(pl.multiple_of(same * 16, 16), 16), pl.ds(pl.multiple_of(other * 16, 16), 16)


def chip_masks(chips):
    return [0] + list(range(chips - 1, 0, -1))


def part_group(group_ref, keep_ref, cross_ref):
    for mask in range(group_ref.shape[0] // 32):
        same, other = member_rows(mask)
        keep_ref[mask * 16 : mask * 16 + 16, :] = group_ref[same, :]
        cross_ref[mask * 16 : mask * 16 + 16, :] = group_ref[other, :]


def join_group(message_refs, group_ref):
    for mask, message_ref in zip(chip_masks(len(message_refs)), message_refs):
        same, other = member_rows(mask)
        group_ref[same, :] = message_ref[0:16, :]
        group_ref[other, :] = message_ref[16:32, :]


def merge_kernel(keep_ref, cross_ref, *message_refs):
    upper = iota((16, LANES), 1) >= HALF
    sums = jnp.where(upper, keep_ref[0:16, :] + cross_ref[0:16, :], 0.0)
    for mask, message_ref in enumerate(message_refs):
        block = keep_ref[mask * 16 : mask * 16 + 16, :]
        message_ref[0:16, :] = jnp.where(upper, sums, block)
        message_ref[16:32, :] = cross_ref[mask * 16 : mask * 16 + 16, :]


def send_kernel(
    total_vertices,
    paired,
    nodal_hbm,
    level_hbm,
    target_hbm,
    slot_hbm,
    interp_hbm,
    derivative_hbm,
    vertex_hbm,
    near_ref,
    far_ref,
    keep_ref,
    cross_ref,
    traces_ref,
    columns_ref,
    slot_level_ref,
    maps_ref,
    level_ref,
    target_ref,
    slot_mortar_ref,
    interp_ref,
    derivative_ref,
    vertex_ref,
    nodal_ref,
    group_ref,
    nodal_sems,
    sems,
):
    target_copy = pltpu.make_async_copy(target_hbm, target_ref.at[0], sems.at[0])
    level_copy = pltpu.make_async_copy(level_hbm, level_ref.at[0], sems.at[1])
    interp_copy = pltpu.make_async_copy(interp_hbm, interp_ref, sems.at[2])
    vertex_copy = pltpu.make_async_copy(vertex_hbm, vertex_ref, sems.at[3])
    slot_copy = pltpu.make_async_copy(slot_hbm, slot_mortar_ref.at[0], sems.at[4])
    derivative_copy = pltpu.make_async_copy(derivative_hbm, derivative_ref, sems.at[5])
    nodal_copies = lane_copies(nodal_hbm, nodal_ref, nodal_sems)
    target_copy.start()
    interp_copy.start()
    for copy in nodal_copies:
        copy.start()
    for copy in (level_copy, vertex_copy, slot_copy, derivative_copy):
        copy.start()
    slots = slot_level_ref.shape[1]
    elems = nodal_hbm.shape[1]
    target_copy.wait()
    columns = columns_of(target_ref[...])
    columns_ref[...] = columns
    remote = one_hot_lanes(columns, M_DEV, -(-slots // 256) * 256)
    interp_copy.wait()
    maps = kron_four(interp_ref[0], interp_ref[1])
    maps_ref[...] = maps
    vertex_copy.wait()
    high_id, low_id = window_ids(vertex_ref[...], lax.axis_index("elem"), total_vertices)
    low_hot = low_one_hot(low_id)

    for copy in nodal_copies:
        copy.wait()
    level_copy.wait()
    level = level_ref[...]
    faces = [
        load_rows(nodal_ref, pl.ds(0, SQ)),
        load_rows(nodal_ref, pl.ds(7 * SQ, SQ)),
        load_comb(nodal_ref, 0),
        load_comb(nodal_ref, 7),
        load_rows(nodal_ref, pl.ds(0, SQ, stride=8)),
        load_rows(nodal_ref, pl.ds(7, SQ, stride=8)),
    ]
    trace = jnp.concatenate(faces, axis=1)
    hi, lo = split(trace)
    traces_ref[0:SQ, :] = hi
    traces_ref[SQ : 2 * SQ, :] = lo
    traces_ref[2 * SQ :, :] = jnp.broadcast_to(level, (16, level.shape[1])).astype(f32).astype(bf16)

    picked = mm(traces_ref[...], remote)[:, 0:slots]
    plain = picked[0:SQ] + picked[SQ : 2 * SQ]
    slot_level = picked[2 * SQ : 2 * SQ + 8]
    slot_level_ref[...] = slot_level
    sent = pick_level(plain, mm(maps, stack3(plain)), slot_level[0:1])

    row = iota((16, elems), 0)
    row_high = row % 4 + 4 * (row // 8)
    is_count = row // 4 % 2 == 1
    weighted = []
    for corner in range(8):
        value = load_rows(nodal_ref, pl.ds(corner_row(corner), 1))
        value_hi = value.astype(bf16).astype(f32)
        value_lo = value - value_hi
        mine = high_id[corner : corner + 1] == row_high
        first = jnp.where(mine, jnp.where(is_count, 1.0, value_hi), 0.0)
        second = jnp.where(mine & ~is_count, value_lo, 0.0)
        weighted.append(jnp.concatenate([first, second], axis=0).astype(bf16))
    sums = mm_nt(jnp.concatenate(weighted, axis=1), low_hot)
    sums = sums[0:16] + sums[16:32]
    group = sent[:, 2 * CAP_E :]
    group_ref[...] = jnp.concatenate([group, jnp.zeros_like(group)], axis=0).T
    part_group(group_ref, keep_ref, cross_ref)
    keep_ref[0:16, :] += sums
    cross_ref[0:16, :] += sums
    near_ref[...], far_ref[...] = swap_if(
        up_goes_near(paired), sent[:, CAP_E : 2 * CAP_E], sent[:, 0:CAP_E]
    )
    slot_copy.wait()
    derivative_copy.wait()


def stiffness_maps(matrix):
    row = iota((SQ, 3 * SQ), 0)
    lane = iota((SQ, 3 * SQ), 1) % SQ
    first, second = expand(matrix, 3)
    outer = jnp.where(row % 8 == lane % 8, first, 0.0)
    inner = jnp.where(row // 8 == lane // 8, second, 0.0)
    return hi_hi_lo(outer), hi_hi_lo(inner)


def local_kernel(
    traces_ref,
    maps_ref,
    level_ref,
    columns_ref,
    slot_mortar_ref,
    interp_ref,
    derivative_ref,
    mortar_ref,
    answers_ref,
    equal_ref,
    back_maps_ref,
    grad_map_ref,
    div_map_ref,
):
    back_maps_ref[...] = kron_four(interp_ref[0].T, interp_ref[1].T)
    slot_row = slot_mortar_ref[...]
    equal_ref[...] = (columns_of(slot_row)[:, 0:1] == slot_row).astype(f32).astype(bf16)
    hi = traces_ref[0:SQ, :]
    lo = traces_ref[SQ : 2 * SQ, :]
    plain = hi.astype(f32) + lo.astype(f32)
    mapped = mm(maps_ref[...], jnp.concatenate([hi, lo, hi], axis=0))
    projected = pick_level(plain, mapped, level_ref[...])
    mortar = mm(stack2(projected), one_hot_lanes(columns_ref[...], 0, M_DEV))
    mortar = mortar[0:SQ] + mortar[SQ:]
    mortar_ref[...] = mortar
    answers = mm(stack2(mortar), one_hot_rows(slot_row, 0, M_DEV))
    answers_ref[...] = answers[0:SQ] + answers[SQ:]
    outer, inner = stiffness_maps(derivative_ref[...])
    outer_t, inner_t = stiffness_maps(derivative_ref[...].T)
    grad_map_ref[0:SQ, :] = outer
    grad_map_ref[SQ:, :] = inner
    div_map_ref[...] = jnp.concatenate([outer_t, inner_t], axis=1)


def first_direction(nodal_ref, metric_ref, outer, outer_t, stiff_ref, by_row):
    for i in range(8):
        by_row[i * SQ : (i + 1) * SQ, :] = metric_ref[i * SQ : (i + 1) * SQ, :].astype(f32)
    grads = [mm(outer, stack3(load_comb(nodal_ref, j))) for j in range(8)]
    weighted = []
    for j in range(8):
        factor = [by_row[i * SQ + j * 8 : i * SQ + j * 8 + 8, :] for i in range(8)]
        weighted.append(stack3(grads[j] * jnp.concatenate(factor, axis=0)))
    for j in range(8):
        out = mm(outer_t, weighted[j])
        for i in range(8):
            stiff_ref[i * SQ + j * 8 : i * SQ + j * 8 + 8, :] = out[i * 8 : i * 8 + 8]


def other_directions(nodal_ref, metric_ref, grad_map, div_map, stiff_ref, result_ref):
    slabs = [pl.ds(i * SQ, SQ) for i in range(8)]
    grads = [mm(grad_map, stack3(load_rows(nodal_ref, slab))) for slab in slabs]
    weighted = []
    for slab, grad in zip(slabs, grads):
        second = stack3(grad[0:SQ] * metric_ref[0, slab, :].astype(f32))
        third = stack3(grad[SQ:] * metric_ref[1, slab, :].astype(f32))
        weighted.append(jnp.concatenate([second, third], axis=0))
    for slab, part in zip(slabs, weighted):
        store_rows(result_ref, slab, stiff_ref[slab, :] + mm(div_map, part))


def answer_kernel(
    paired,
    near_in_ref,
    far_in_ref,
    equal_ref,
    local_answers_ref,
    *refs,
):
    *message_refs, near_ref, far_ref, keep_ref, cross_ref, incoming_ref, sums_ref, group_ref = refs
    join_group(message_refs, group_ref)
    from_up, from_down = swap_if(
        up_came_near(paired), near_in_ref[...], far_in_ref[...]
    )
    incoming = jnp.concatenate([from_up, from_down, group_ref[...].T[0:SQ]], axis=1)
    incoming_ref[...] = incoming
    added = mm(stack2(incoming), equal_ref[...])
    answers = local_answers_ref[...] + added[0:SQ] + added[SQ:]
    group = answers[:, 2 * CAP_E :]
    group_ref[...] = jnp.concatenate([group, jnp.zeros_like(group)], axis=0).T
    part_group(group_ref, keep_ref, cross_ref)
    sums = message_refs[0][0:16, :]
    for message_ref in message_refs[1:]:
        sums = sums + message_ref[0:16, :]
    sums_ref[...] = sums
    down = jnp.concatenate([answers[:, 0:CAP_E], sums[0:8]], axis=0)
    up = jnp.concatenate([answers[:, CAP_E : 2 * CAP_E], sums[8:16]], axis=0)
    near_ref[...], far_ref[...] = swap_if(up_goes_near(paired), up, down)


def gather_kernel(
    total_vertices,
    nodal_hbm,
    metric_hbm,
    mortar_ref,
    incoming_ref,
    slot_mortar_ref,
    target_ref,
    level_ref,
    back_maps_ref,
    grad_map_ref,
    div_map_ref,
    vertex_ref,
    result_ref,
    remote_ref,
    low_ids_ref,
    high_ids_ref,
    nodal_ref,
    metric_ref,
    stiff_ref,
    by_row,
    nodal_sems,
    sem,
):
    nodal_copies = lane_copies(nodal_hbm, nodal_ref, nodal_sems)
    metric_copy = pltpu.make_async_copy(metric_hbm, metric_ref, sem)
    for copy in nodal_copies:
        copy.start()
    metric_copy.start()
    slot_hot = one_hot_lanes(columns_of(slot_mortar_ref[...]), 0, M_DEV)
    added = mm(stack2(incoming_ref[...]), slot_hot)
    mortar = mortar_ref[...] + added[0:SQ] + added[SQ:]
    target = target_ref[...]
    picked = mm(stack2(mortar), one_hot_rows(target, 0, M_DEV))
    picked = picked[0:SQ] + picked[SQ:]
    back = pick_level(picked, mm(back_maps_ref[...], stack3(picked)), level_ref[...])
    remote_ref[...] = one_hot_rows(target, M_DEV, remote_ref.shape[0])
    high_id, low_id = window_ids(vertex_ref[...], lax.axis_index("elem"), total_vertices)
    high_ids_ref[...] = high_id
    low_ids_ref[...] = low_one_hot(low_id)
    for copy in nodal_copies:
        copy.wait()
    metric_copy.wait()
    first_direction(nodal_ref, metric_ref.at[0], grad_map_ref[0:SQ, :], div_map_ref[:, 0:3 * SQ], stiff_ref, by_row)
    other_directions(
        nodal_ref, metric_ref.at[1:3], grad_map_ref[...], div_map_ref[...], stiff_ref, result_ref
    )
    add_faces(result_ref, back)


def add_faces(ref, back):
    elems = ref.shape[0] * LANES
    parts = [back[:, f * elems : (f + 1) * elems] for f in range(6)]
    add_rows(ref, pl.ds(0, SQ), parts[0])
    add_rows(ref, pl.ds(7 * SQ, SQ), parts[1])
    for a in range(8):
        add_rows(ref, pl.ds(a * SQ, 8), parts[2][a * 8 : a * 8 + 8])
        add_rows(ref, pl.ds(a * SQ + 56, 8), parts[3][a * 8 : a * 8 + 8])
    add_rows(ref, pl.ds(0, SQ, stride=8), parts[4])
    add_rows(ref, pl.ds(7, SQ, stride=8), parts[5])


def final_kernel(
    paired,
    near_in_ref,
    far_in_ref,
    slot_level_ref,
    maps_ref,
    remote_ref,
    sums_ref,
    high_ids_ref,
    low_ids_ref,
    result_ref,
    *refs,
):
    *message_refs, out_hbm, out_ref, group_ref, sems = refs
    join_group(message_refs, group_ref)
    from_up, from_down = swap_if(
        up_came_near(paired), near_in_ref[...], far_in_ref[...]
    )
    arrived = jnp.concatenate([from_up[0:SQ], from_down[0:SQ], group_ref[...].T[0:SQ]], axis=1)
    slot_back = pick_level(arrived, mm(maps_ref[...], stack3(arrived)), slot_level_ref[0:1, :])
    back = mm(stack2(slot_back), remote_ref[...])
    back = back[0:SQ] + back[SQ:]

    first = sums_ref[0:8, :] + from_up[SQ:]
    second = sums_ref[8:16, :] + from_down[SQ:]
    totals = jnp.concatenate([first[0:4], second[0:4]], axis=0)
    counts = jnp.concatenate([first[4:8], second[4:8]], axis=0)
    coarse = jnp.where(iota(totals.shape, 1) < HALF, 0.0, totals / (1.0 + counts))
    coarse_hi = coarse.astype(bf16).astype(f32)
    table = jnp.concatenate([coarse_hi, coarse - coarse_hi], axis=0).astype(bf16)
    found = mm(table, low_ids_ref[...])
    found = found[0:8] + found[8:16]
    high_id = high_ids_ref[...]

    elems = out_hbm.shape[1]
    row = iota((8, elems), 0)
    fixes = []
    for corner in range(8):
        mine = row == high_id[corner : corner + 1]
        fix = jnp.where(mine, found[:, corner * elems : (corner + 1) * elems], 0.0)
        fixes.append(jnp.sum(fix, axis=0, keepdims=True))
    parts = [back[:, f * elems : (f + 1) * elems] for f in range(6)]
    copies = []
    for i in range(POINTS):
        rows = slice(i * POINTS, (i + 1) * POINTS)
        slab = load_rows(result_ref, pl.ds(i * SQ, SQ))
        if i in (0, POINTS - 1):
            slab = slab + parts[min(i, 1)]
        pieces = [slab[0:8] + parts[2][rows], slab[8:56], slab[56:64] + parts[3][rows]]
        store_rows(out_ref, pl.ds(i * SQ, SQ), jnp.concatenate(pieces, axis=0))
        add_rows(out_ref, pl.ds(i * SQ, 8, stride=8), parts[4][rows])
        add_rows(out_ref, pl.ds(i * SQ + 7, 8, stride=8), parts[5][rows])
        for corner in range(8):
            if corner_row(corner) // SQ == i:
                add_rows(out_ref, pl.ds(corner_row(corner), 1), fixes[corner])
        if i % 2:
            rows = pl.ds((i - 1) * SQ, 2 * SQ)
            for h in range(out_ref.shape[0]):
                lanes = pl.ds(h * LANES, LANES)
                copies.append(
                    pltpu.make_async_copy(
                        out_ref.at[h, rows], out_hbm.at[rows, lanes], sems.at[len(copies)]
                    )
                )
                copies[-1].start()
    for copy in copies:
        copy.wait()


VMEM = pl.BlockSpec(memory_space=pltpu.VMEM)
HBM = pl.BlockSpec(memory_space=pltpu.HBM)


def params(mib):
    return pltpu.CompilerParams(vmem_limit_bytes=mib * MIB)


def cost(us):
    return pl.CostEstimate(flops=int(us * 5e8), bytes_accessed=int(us * 2e6), transcendentals=0)


def curve_swap(near, far):
    peers = lax.axis_size("elem")
    up = [(i, (i + 1) % peers) for i in range(peers)]
    near_pairs, far_pairs = up, [(j, i) for i, j in up]
    if peers % 2 == 0:
        near_pairs = [(i, i ^ 1) for i in range(peers)]
        far_pairs = [(i, (i + 1 if i % 2 else i - 1) % peers) for i in range(peers)]
    return lax.ppermute(near, "elem", near_pairs), lax.ppermute(far, "elem", far_pairs)


def group_swap(keep, cross):
    members = lax.axis_size("clus")
    chips = members // 2
    cross = lax.ppermute(cross, "clus", [(i, i ^ 1) for i in range(members)])
    messages = pl.pallas_call(
        merge_kernel,
        in_specs=[VMEM] * 2,
        out_specs=[VMEM] * chips,
        out_shape=[pltpu.VMEM((32, LANES), f32)] * chips,
        compiler_params=params(16),
        name="merge",
    )(keep, cross)
    return [messages[0]] + [
        lax.ppermute(messages[mask], "clus", [(i, i ^ (2 * mask + 1)) for i in range(members)])
        for mask in chip_masks(chips)[1:]
    ]


def on_device(nodal, metric, derivative, interp, face_level, face_target, slot_mortar, vertex_ids):
    elems = nodal.shape[1]
    faces = face_level.shape[0]
    slots = slot_mortar.shape[0]
    blocked = (elems // LANES, nodal.shape[0], LANES)
    total_vertices = NV_DEV * lax.axis_size("elem")
    paired = lax.axis_size("elem") % 2 == 0
    group_slots = slots - 2 * CAP_E
    half_group = pltpu.VMEM((group_slots // 2, LANES), f32)
    nodal, metric, derivative, interp, face_level, face_target, slot_mortar, vertex_ids = (
        pltpu.with_memory_space_constraint(array, pltpu.HBM)
        for array in (
            nodal, metric, derivative, interp, face_level, face_target, slot_mortar, vertex_ids
        )
    )
    maps_shape = pltpu.VMEM((4 * SQ, 3 * SQ), bf16)

    (
        near, far, keep, cross, traces, columns, slot_level, maps,
        level, target, slot_row, interp_in, derivative_in, vertex_in,
    ) = pl.pallas_call(
        functools.partial(send_kernel, total_vertices, paired),
        in_specs=[HBM] * 7,
        out_specs=[VMEM] * 14,
        out_shape=[
            pltpu.VMEM((SQ, CAP_E), f32),
            pltpu.VMEM((SQ, CAP_E), f32),
            half_group,
            half_group,
            pltpu.VMEM((2 * SQ + 16, faces), bf16),
            pltpu.VMEM((faces, LANES), jnp.int32),
            pltpu.VMEM((8, slots), f32),
            maps_shape,
            pltpu.VMEM((1, faces), jnp.int32),
            pltpu.VMEM((1, faces), jnp.int32),
            pltpu.VMEM((1, slots), jnp.int32),
            pltpu.VMEM(interp.shape, f32),
            pltpu.VMEM(derivative.shape, f32),
            pltpu.VMEM(vertex_ids.shape, jnp.int32),
        ],
        scratch_shapes=[
            pltpu.VMEM(blocked, f32),
            pltpu.VMEM((group_slots, LANES), f32),
            pltpu.SemaphoreType.DMA((blocked[0],)),
            pltpu.SemaphoreType.DMA((6,)),
        ],
        compiler_params=params(16),
        name="send",
    )(nodal, face_level, face_target, slot_mortar, interp, derivative, vertex_ids)

    near, far = curve_swap(near, far)
    messages = group_swap(keep, cross)

    mortar, local_answers, equal, back_maps, grad_map, div_map = pl.pallas_call(
        local_kernel,
        in_specs=[VMEM] * 7,
        out_specs=[VMEM] * 6,
        out_shape=[
            pltpu.VMEM((SQ, M_DEV), f32),
            pltpu.VMEM((SQ, slots), f32),
            pltpu.VMEM((slots, slots), bf16),
            maps_shape,
            pltpu.VMEM((2 * SQ, 3 * SQ), bf16),
            pltpu.VMEM((SQ, 6 * SQ), bf16),
        ],
        compiler_params=params(16),
        cost_estimate=cost(3),
        name="local",
    )(traces, maps, level, columns, slot_row, interp_in, derivative_in)

    near, far, keep, cross, incoming, sums = pl.pallas_call(
        functools.partial(answer_kernel, paired),
        in_specs=[VMEM] * (4 + len(messages)),
        out_specs=[VMEM] * 6,
        out_shape=[
            pltpu.VMEM((SQ + 8, CAP_E), f32),
            pltpu.VMEM((SQ + 8, CAP_E), f32),
            half_group,
            half_group,
            pltpu.VMEM((SQ, slots), f32),
            pltpu.VMEM((16, LANES), f32),
        ],
        scratch_shapes=[pltpu.VMEM((group_slots, LANES), f32)],
        compiler_params=params(16),
        name="answer",
    )(near, far, equal, local_answers, *messages)

    near, far = curve_swap(near, far)
    messages = group_swap(keep, cross)

    result, remote, low_ids, high_ids = pl.pallas_call(
        functools.partial(gather_kernel, total_vertices),
        in_specs=[HBM, HBM] + [VMEM] * 9,
        out_specs=[VMEM] * 4,
        out_shape=[
            pltpu.VMEM(blocked, f32),
            pltpu.VMEM((slots, faces), bf16),
            pltpu.VMEM((2 * HALF, 8 * elems), bf16),
            pltpu.VMEM((8, elems), jnp.int32),
        ],
        scratch_shapes=[
            pltpu.VMEM(blocked, f32),
            pltpu.VMEM(metric.shape, bf16),
            pltpu.VMEM(nodal.shape, f32),
            pltpu.VMEM(nodal.shape, f32),
            pltpu.SemaphoreType.DMA((blocked[0],)),
            pltpu.SemaphoreType.DMA,
        ],
        compiler_params=params(16),
        cost_estimate=cost(3),
        name="gather",
    )(
        nodal, metric, mortar, incoming, slot_row, target, level, back_maps,
        grad_map, div_map, vertex_in,
    )

    return pl.pallas_call(
        functools.partial(final_kernel, paired),
        in_specs=[VMEM] * (9 + len(messages)),
        out_specs=HBM,
        out_shape=jax.ShapeDtypeStruct(nodal.shape, f32),
        scratch_shapes=[
            pltpu.VMEM(blocked, f32),
            pltpu.VMEM((group_slots, LANES), f32),
            pltpu.SemaphoreType.DMA((POINTS // 2 * blocked[0],)),
        ],
        compiler_params=params(16),
        name="final",
    )(
        near, far, slot_level, back_maps, remote, sums, high_ids, low_ids, result, *messages
    )


def solution(mesh):
    in_specs = (
        P(None, ("elem", "clus")),
        P(None, None, ("elem", "clus")),
        P(),
        P(),
        P(("elem", "clus")),
        P(("elem", "clus")),
        P(("elem", "clus")),
        P(None, ("elem", "clus")),
    )
    out_specs = P(None, ("elem", "clus"))
    return jax.shard_map(
        on_device, mesh=mesh, in_specs=in_specs, out_specs=out_specs, check_vma=False
    )
```

```python
import functools

import jax
import jax.numpy as jnp
from jax import lax
from jax.experimental import pallas as pl
from jax.experimental.pallas import tpu as pltpu
from jax.sharding import PartitionSpec as P

POINTS = 8
SQ = POINTS * POINTS
CAP_E = 128
CAP_C = 16
M_DEV = 512
NV_DEV = 256
HALF = 64
LANES = 128
MIB = 1 << 20

f32 = jnp.float32
bf16 = jnp.bfloat16
highest = lax.Precision.HIGHEST


def split(x):
    hi = x.astype(bf16)
    lo = (x - hi.astype(f32)).astype(bf16)
    return hi, lo


def stack3(x, axis=0):
    hi, lo = split(x)
    return jnp.concatenate([hi, lo, hi], axis=axis)


def stack2(x):
    hi, lo = split(x)
    return jnp.concatenate([hi, lo], axis=0)


def mm(a, b):
    return lax.dot_general(a, b, (((1,), (0,)), ((), ())), preferred_element_type=f32)


def mm_nt(a, b):
    return lax.dot_general(a, b, (((1,), (1,)), ((), ())), preferred_element_type=f32)


def iota(shape, dim):
    return lax.broadcasted_iota(jnp.int32, shape, dim)


def expand(matrix, copies):
    width = SQ * copies
    lane = iota((POINTS, width), 1) % SQ
    row = iota((POINTS, width), 0)
    to_first = (lane // POINTS == row).astype(f32)
    to_second = (lane % POINTS == row).astype(f32)
    first = jnp.dot(matrix, to_first, precision=highest, preferred_element_type=f32)
    second = jnp.dot(matrix, to_second, precision=highest, preferred_element_type=f32)
    first = jnp.broadcast_to(first[:, None, :], (POINTS, POINTS, width)).reshape(SQ, width)
    second = jnp.concatenate([second] * POINTS, axis=0)
    return first, second


def hi_hi_lo(matrix):
    hi = matrix.astype(bf16).astype(f32)
    lane = iota(matrix.shape, 1)
    return jnp.where(lane < 2 * SQ, hi, matrix - hi).astype(bf16)


def kron_four(low, high):
    low_first, low_second = expand(low, 3)
    high_first, high_second = expand(high, 3)
    maps = [
        low_first * low_second,
        low_first * high_second,
        high_first * low_second,
        high_first * high_second,
    ]
    return hi_hi_lo(jnp.concatenate(maps, axis=0))


def load_rows(ref, rows):
    return jnp.concatenate([ref[h, rows, :] for h in range(ref.shape[0])], axis=1)


def load_comb(ref, j):
    return jnp.concatenate([load_rows(ref, pl.ds(a * SQ + j * 8, 8)) for a in range(8)], axis=0)


def store_rows(ref, rows, value):
    for h in range(ref.shape[0]):
        ref[h, rows, :] = value[:, h * LANES : (h + 1) * LANES]


def add_rows(ref, rows, value):
    for h in range(ref.shape[0]):
        ref[h, rows, :] += value[:, h * LANES : (h + 1) * LANES]


def lane_copies(hbm, blocks, sems):
    return [
        pltpu.make_async_copy(hbm.at[:, pl.ds(h * LANES, LANES)], blocks.at[h], sems.at[h])
        for h in range(blocks.shape[0])
    ]


def pick_level(plain, mapped, level):
    out = plain
    for number in range(1, 5):
        out = jnp.where(level == number, mapped[(number - 1) * SQ : number * SQ], out)
    return out


def one_hot_rows(ids, first, count):
    return (iota((count, ids.shape[1]), 0) + first == ids).astype(f32).astype(bf16)


def columns_of(row):
    return jnp.broadcast_to(row, (LANES, row.shape[1])).T


def one_hot_lanes(columns, first, count):
    lane = iota((columns.shape[0], LANES), 1) + first
    blocks = [columns == lane + start for start in range(0, count, LANES)]
    return jnp.concatenate([block.astype(f32).astype(bf16) for block in blocks], axis=1)


def window_ids(vertex_ids, elem_index, total):
    shifted = vertex_ids - elem_index * NV_DEV
    window = jnp.where(shifted < 0, shifted + total, shifted)
    return window // HALF, window % HALF


def low_one_hot(low_id):
    parts = []
    for corner in range(8):
        hot = one_hot_rows(low_id[corner : corner + 1], 0, HALF)
        parts.append(jnp.concatenate([jnp.zeros_like(hot), hot], axis=0))
    return jnp.concatenate(parts, axis=1)


def corner_row(corner):
    last = POINTS - 1
    return corner // 4 * last * SQ + corner // 2 % 2 * last * POINTS + corner % 2 * last


def up_goes_near(paired):
    return lax.axis_index("elem") % 2 == 0 if paired else lax.axis_index("elem") >= 0


def up_came_near(paired):
    return lax.axis_index("elem") % 2 == 1 if paired else lax.axis_index("elem") >= 0


def swap_if(flag, first, second):
    return jnp.where(flag, first, second), jnp.where(flag, second, first)


def member_rows(mask):
    member = lax.axis_index("clus")
    same = jnp.bitwise_xor(member, 2 * mask + (mask > 0))
    other = jnp.bitwise_xor(same, 1)
    return pl.ds(pl.multiple_of(same * 16, 16), 16), pl.ds(pl.multiple_of(other * 16, 16), 16)


def chip_masks(chips):
    return [0] + list(range(chips - 1, 0, -1))


def part_group(group_ref, keep_ref, cross_ref):
    for mask in range(group_ref.shape[0] // 32):
        same, other = member_rows(mask)
        keep_ref[mask * 16 : mask * 16 + 16, :] = group_ref[same, :]
        cross_ref[mask * 16 : mask * 16 + 16, :] = group_ref[other, :]


def join_group(message_refs, group_ref):
    for mask, message_ref in zip(chip_masks(len(message_refs)), message_refs):
        same, other = member_rows(mask)
        group_ref[same, :] = message_ref[0:16, :]
        group_ref[other, :] = message_ref[16:32, :]


def merge_kernel(keep_ref, cross_ref, *message_refs):
    upper = iota((16, LANES), 1) >= HALF
    sums = jnp.where(upper, keep_ref[0:16, :] + cross_ref[0:16, :], 0.0)
    for mask, message_ref in enumerate(message_refs):
        block = keep_ref[mask * 16 : mask * 16 + 16, :]
        message_ref[0:16, :] = jnp.where(upper, sums, block)
        message_ref[16:32, :] = cross_ref[mask * 16 : mask * 16 + 16, :]


def send_kernel(
    total_vertices,
    paired,
    nodal_hbm,
    level_hbm,
    target_hbm,
    slot_hbm,
    interp_hbm,
    derivative_hbm,
    vertex_hbm,
    near_ref,
    far_ref,
    keep_ref,
    cross_ref,
    traces_ref,
    columns_ref,
    slot_level_ref,
    maps_ref,
    level_ref,
    target_ref,
    slot_mortar_ref,
    interp_ref,
    derivative_ref,
    vertex_ref,
    nodal_ref,
    group_ref,
    nodal_sems,
    sems,
):
    target_copy = pltpu.make_async_copy(target_hbm, target_ref.at[0], sems.at[0])
    level_copy = pltpu.make_async_copy(level_hbm, level_ref.at[0], sems.at[1])
    interp_copy = pltpu.make_async_copy(interp_hbm, interp_ref, sems.at[2])
    vertex_copy = pltpu.make_async_copy(vertex_hbm, vertex_ref, sems.at[3])
    slot_copy = pltpu.make_async_copy(slot_hbm, slot_mortar_ref.at[0], sems.at[4])
    derivative_copy = pltpu.make_async_copy(derivative_hbm, derivative_ref, sems.at[5])
    nodal_copies = lane_copies(nodal_hbm, nodal_ref, nodal_sems)
    target_copy.start()
    interp_copy.start()
    for copy in nodal_copies:
        copy.start()
    for copy in (level_copy, vertex_copy, slot_copy, derivative_copy):
        copy.start()
    slots = slot_level_ref.shape[1]
    elems = nodal_hbm.shape[1]
    target_copy.wait()
    columns = columns_of(target_ref[...])
    columns_ref[...] = columns
    remote = one_hot_lanes(columns, M_DEV, -(-slots // 256) * 256)
    interp_copy.wait()
    maps = kron_four(interp_ref[0], interp_ref[1])
    maps_ref[...] = maps
    vertex_copy.wait()
    high_id, low_id = window_ids(vertex_ref[...], lax.axis_index("elem"), total_vertices)
    low_hot = low_one_hot(low_id)

    for copy in nodal_copies:
        copy.wait()
    level_copy.wait()
    level = level_ref[...]
    faces = [
        load_rows(nodal_ref, pl.ds(0, SQ)),
        load_rows(nodal_ref, pl.ds(7 * SQ, SQ)),
        load_comb(nodal_ref, 0),
        load_comb(nodal_ref, 7),
        load_rows(nodal_ref, pl.ds(0, SQ, stride=8)),
        load_rows(nodal_ref, pl.ds(7, SQ, stride=8)),
    ]
    trace = jnp.concatenate(faces, axis=1)
    hi, lo = split(trace)
    traces_ref[0:SQ, :] = hi
    traces_ref[SQ : 2 * SQ, :] = lo
    traces_ref[2 * SQ :, :] = jnp.broadcast_to(level, (16, level.shape[1])).astype(f32).astype(bf16)

    picked = mm(traces_ref[...], remote)[:, 0:slots]
    plain = picked[0:SQ] + picked[SQ : 2 * SQ]
    slot_level = picked[2 * SQ : 2 * SQ + 8]
    slot_level_ref[...] = slot_level
    sent = pick_level(plain, mm(maps, stack3(plain)), slot_level[0:1])

    row = iota((16, elems), 0)
    row_high = row % 4 + 4 * (row // 8)
    is_count = row // 4 % 2 == 1
    weighted = []
    for corner in range(8):
        value = load_rows(nodal_ref, pl.ds(corner_row(corner), 1))
        value_hi = value.astype(bf16).astype(f32)
        value_lo = value - value_hi
        mine = high_id[corner : corner + 1] == row_high
        first = jnp.where(mine, jnp.where(is_count, 1.0, value_hi), 0.0)
        second = jnp.where(mine & ~is_count, value_lo, 0.0)
        weighted.append(jnp.concatenate([first, second], axis=0).astype(bf16))
    sums = mm_nt(jnp.concatenate(weighted, axis=1), low_hot)
    sums = sums[0:16] + sums[16:32]
    group = sent[:, 2 * CAP_E :]
    group_ref[...] = jnp.concatenate([group, jnp.zeros_like(group)], axis=0).T
    part_group(group_ref, keep_ref, cross_ref)
    keep_ref[0:16, :] += sums
    cross_ref[0:16, :] += sums
    near_ref[...], far_ref[...] = swap_if(
        up_goes_near(paired), sent[:, CAP_E : 2 * CAP_E], sent[:, 0:CAP_E]
    )
    slot_copy.wait()
    derivative_copy.wait()


def stiffness_maps(matrix):
    row = iota((SQ, 3 * SQ), 0)
    lane = iota((SQ, 3 * SQ), 1) % SQ
    first, second = expand(matrix, 3)
    outer = jnp.where(row % 8 == lane % 8, first, 0.0)
    inner = jnp.where(row // 8 == lane // 8, second, 0.0)
    return hi_hi_lo(outer), hi_hi_lo(inner)


def local_kernel(
    nodal_hbm,
    metric_hbm,
    traces_ref,
    maps_ref,
    level_ref,
    columns_ref,
    slot_mortar_ref,
    interp_ref,
    derivative_ref,
    mortar_ref,
    answers_ref,
    equal_ref,
    back_maps_ref,
    grad_map_ref,
    div_map_ref,
    nodal_ref,
    metric_ref,
    nodal_sems,
    sem,
):
    nodal_copies = lane_copies(nodal_hbm, nodal_ref, nodal_sems)
    metric_copy = pltpu.make_async_copy(metric_hbm, metric_ref, sem)
    for copy in nodal_copies:
        copy.start()
    metric_copy.start()
    back_maps_ref[...] = kron_four(interp_ref[0].T, interp_ref[1].T)
    slot_row = slot_mortar_ref[...]
    equal_ref[...] = (columns_of(slot_row)[:, 0:1] == slot_row).astype(f32).astype(bf16)
    hi = traces_ref[0:SQ, :]
    lo = traces_ref[SQ : 2 * SQ, :]
    plain = hi.astype(f32) + lo.astype(f32)
    mapped = mm(maps_ref[...], jnp.concatenate([hi, lo, hi], axis=0))
    projected = pick_level(plain, mapped, level_ref[...])
    mortar = mm(stack2(projected), one_hot_lanes(columns_ref[...], 0, M_DEV))
    mortar = mortar[0:SQ] + mortar[SQ:]
    mortar_ref[...] = mortar
    answers = mm(stack2(mortar), one_hot_rows(slot_row, 0, M_DEV))
    answers_ref[...] = answers[0:SQ] + answers[SQ:]
    outer, inner = stiffness_maps(derivative_ref[...])
    outer_t, inner_t = stiffness_maps(derivative_ref[...].T)
    grad_map_ref[0:SQ, :] = outer
    grad_map_ref[SQ:, :] = inner
    div_map_ref[...] = jnp.concatenate([outer_t, inner_t], axis=1)
    for copy in nodal_copies:
        copy.wait()
    metric_copy.wait()


def first_direction(nodal_ref, metric_ref, outer, outer_t, stiff_ref, by_row):
    for i in range(8):
        by_row[i * SQ : (i + 1) * SQ, :] = metric_ref[i * SQ : (i + 1) * SQ, :].astype(f32)
    grads = [mm(outer, stack3(load_comb(nodal_ref, j))) for j in range(8)]
    weighted = []
    for j in range(8):
        factor = [by_row[i * SQ + j * 8 : i * SQ + j * 8 + 8, :] for i in range(8)]
        weighted.append(stack3(grads[j] * jnp.concatenate(factor, axis=0)))
    for j in range(8):
        out = mm(outer_t, weighted[j])
        for i in range(8):
            stiff_ref[i * SQ + j * 8 : i * SQ + j * 8 + 8, :] = out[i * 8 : i * 8 + 8]


def other_directions(nodal_ref, metric_ref, grad_map, div_map, stiff_ref, result_ref):
    slabs = [pl.ds(i * SQ, SQ) for i in range(8)]
    grads = [mm(grad_map, stack3(load_rows(nodal_ref, slab))) for slab in slabs]
    weighted = []
    for slab, grad in zip(slabs, grads):
        second = stack3(grad[0:SQ] * metric_ref[0, slab, :].astype(f32))
        third = stack3(grad[SQ:] * metric_ref[1, slab, :].astype(f32))
        weighted.append(jnp.concatenate([second, third], axis=0))
    for slab, part in zip(slabs, weighted):
        store_rows(result_ref, slab, stiff_ref[slab, :] + mm(div_map, part))


def answer_kernel(
    paired,
    near_in_ref,
    far_in_ref,
    equal_ref,
    local_answers_ref,
    *refs,
):
    *message_refs, near_ref, far_ref, keep_ref, cross_ref, incoming_ref, sums_ref, group_ref = refs
    join_group(message_refs, group_ref)
    from_up, from_down = swap_if(
        up_came_near(paired), near_in_ref[...], far_in_ref[...]
    )
    incoming = jnp.concatenate([from_up, from_down, group_ref[...].T[0:SQ]], axis=1)
    incoming_ref[...] = incoming
    added = mm(stack2(incoming), equal_ref[...])
    answers = local_answers_ref[...] + added[0:SQ] + added[SQ:]
    group = answers[:, 2 * CAP_E :]
    group_ref[...] = jnp.concatenate([group, jnp.zeros_like(group)], axis=0).T
    part_group(group_ref, keep_ref, cross_ref)
    sums = message_refs[0][0:16, :]
    for message_ref in message_refs[1:]:
        sums = sums + message_ref[0:16, :]
    sums_ref[...] = sums
    down = jnp.concatenate([answers[:, 0:CAP_E], sums[0:8]], axis=0)
    up = jnp.concatenate([answers[:, CAP_E : 2 * CAP_E], sums[8:16]], axis=0)
    near_ref[...], far_ref[...] = swap_if(up_goes_near(paired), up, down)


def gather_kernel(
    total_vertices,
    nodal_ref,
    metric_ref,
    mortar_ref,
    incoming_ref,
    slot_mortar_ref,
    target_ref,
    level_ref,
    back_maps_ref,
    grad_map_ref,
    div_map_ref,
    vertex_ref,
    result_ref,
    remote_ref,
    low_ids_ref,
    high_ids_ref,
    stiff_ref,
    by_row,
):
    slot_hot = one_hot_lanes(columns_of(slot_mortar_ref[...]), 0, M_DEV)
    added = mm(stack2(incoming_ref[...]), slot_hot)
    mortar = mortar_ref[...] + added[0:SQ] + added[SQ:]
    target = target_ref[...]
    picked = mm(stack2(mortar), one_hot_rows(target, 0, M_DEV))
    picked = picked[0:SQ] + picked[SQ:]
    back = pick_level(picked, mm(back_maps_ref[...], stack3(picked)), level_ref[...])
    remote_ref[...] = one_hot_rows(target, M_DEV, remote_ref.shape[0])
    high_id, low_id = window_ids(vertex_ref[...], lax.axis_index("elem"), total_vertices)
    high_ids_ref[...] = high_id
    low_ids_ref[...] = low_one_hot(low_id)
    first_direction(nodal_ref, metric_ref.at[0], grad_map_ref[0:SQ, :], div_map_ref[:, 0:3 * SQ], stiff_ref, by_row)
    other_directions(
        nodal_ref, metric_ref.at[1:3], grad_map_ref[...], div_map_ref[...], stiff_ref, result_ref
    )
    add_faces(result_ref, back)


def add_faces(ref, back):
    elems = ref.shape[0] * LANES
    parts = [back[:, f * elems : (f + 1) * elems] for f in range(6)]
    add_rows(ref, pl.ds(0, SQ), parts[0])
    add_rows(ref, pl.ds(7 * SQ, SQ), parts[1])
    for a in range(8):
        add_rows(ref, pl.ds(a * SQ, 8), parts[2][a * 8 : a * 8 + 8])
        add_rows(ref, pl.ds(a * SQ + 56, 8), parts[3][a * 8 : a * 8 + 8])
    add_rows(ref, pl.ds(0, SQ, stride=8), parts[4])
    add_rows(ref, pl.ds(7, SQ, stride=8), parts[5])


def final_kernel(
    paired,
    near_in_ref,
    far_in_ref,
    slot_level_ref,
    maps_ref,
    remote_ref,
    sums_ref,
    high_ids_ref,
    low_ids_ref,
    result_ref,
    *refs,
):
    *message_refs, out_hbm, out_ref, group_ref, sems = refs
    join_group(message_refs, group_ref)
    from_up, from_down = swap_if(
        up_came_near(paired), near_in_ref[...], far_in_ref[...]
    )
    arrived = jnp.concatenate([from_up[0:SQ], from_down[0:SQ], group_ref[...].T[0:SQ]], axis=1)
    slot_back = pick_level(arrived, mm(maps_ref[...], stack3(arrived)), slot_level_ref[0:1, :])
    back = mm(stack2(slot_back), remote_ref[...])
    back = back[0:SQ] + back[SQ:]

    first = sums_ref[0:8, :] + from_up[SQ:]
    second = sums_ref[8:16, :] + from_down[SQ:]
    totals = jnp.concatenate([first[0:4], second[0:4]], axis=0)
    counts = jnp.concatenate([first[4:8], second[4:8]], axis=0)
    coarse = jnp.where(iota(totals.shape, 1) < HALF, 0.0, totals / (1.0 + counts))
    coarse_hi = coarse.astype(bf16).astype(f32)
    table = jnp.concatenate([coarse_hi, coarse - coarse_hi], axis=0).astype(bf16)
    found = mm(table, low_ids_ref[...])
    found = found[0:8] + found[8:16]
    high_id = high_ids_ref[...]

    elems = out_hbm.shape[1]
    row = iota((8, elems), 0)
    fixes = []
    for corner in range(8):
        mine = row == high_id[corner : corner + 1]
        fix = jnp.where(mine, found[:, corner * elems : (corner + 1) * elems], 0.0)
        fixes.append(jnp.sum(fix, axis=0, keepdims=True))
    parts = [back[:, f * elems : (f + 1) * elems] for f in range(6)]
    copies = []
    for i in range(POINTS):
        rows = slice(i * POINTS, (i + 1) * POINTS)
        slab = load_rows(result_ref, pl.ds(i * SQ, SQ))
        if i in (0, POINTS - 1):
            slab = slab + parts[min(i, 1)]
        pieces = [slab[0:8] + parts[2][rows], slab[8:56], slab[56:64] + parts[3][rows]]
        store_rows(out_ref, pl.ds(i * SQ, SQ), jnp.concatenate(pieces, axis=0))
        add_rows(out_ref, pl.ds(i * SQ, 8, stride=8), parts[4][rows])
        add_rows(out_ref, pl.ds(i * SQ + 7, 8, stride=8), parts[5][rows])
        for corner in range(8):
            if corner_row(corner) // SQ == i:
                add_rows(out_ref, pl.ds(corner_row(corner), 1), fixes[corner])
        if i % 2:
            rows = pl.ds((i - 1) * SQ, 2 * SQ)
            for h in range(out_ref.shape[0]):
                lanes = pl.ds(h * LANES, LANES)
                copies.append(
                    pltpu.make_async_copy(
                        out_ref.at[h, rows], out_hbm.at[rows, lanes], sems.at[len(copies)]
                    )
                )
                copies[-1].start()
    for copy in copies:
        copy.wait()


VMEM = pl.BlockSpec(memory_space=pltpu.VMEM)
HBM = pl.BlockSpec(memory_space=pltpu.HBM)


def params(mib):
    return pltpu.CompilerParams(vmem_limit_bytes=mib * MIB)


def cost(us):
    return pl.CostEstimate(flops=int(us * 5e8), bytes_accessed=int(us * 2e6), transcendentals=0)


def curve_swap(near, far):
    peers = lax.axis_size("elem")
    up = [(i, (i + 1) % peers) for i in range(peers)]
    near_pairs, far_pairs = up, [(j, i) for i, j in up]
    if peers % 2 == 0:
        near_pairs = [(i, i ^ 1) for i in range(peers)]
        far_pairs = [(i, (i + 1 if i % 2 else i - 1) % peers) for i in range(peers)]
    return lax.ppermute(near, "elem", near_pairs), lax.ppermute(far, "elem", far_pairs)


def group_swap(keep, cross):
    members = lax.axis_size("clus")
    chips = members // 2
    cross = lax.ppermute(cross, "clus", [(i, i ^ 1) for i in range(members)])
    messages = pl.pallas_call(
        merge_kernel,
        in_specs=[VMEM] * 2,
        out_specs=[VMEM] * chips,
        out_shape=[pltpu.VMEM((32, LANES), f32)] * chips,
        compiler_params=params(16),
        name="merge",
    )(keep, cross)
    return [messages[0]] + [
        lax.ppermute(messages[mask], "clus", [(i, i ^ (2 * mask + 1)) for i in range(members)])
        for mask in chip_masks(chips)[1:]
    ]


def on_device(nodal, metric, derivative, interp, face_level, face_target, slot_mortar, vertex_ids):
    elems = nodal.shape[1]
    faces = face_level.shape[0]
    slots = slot_mortar.shape[0]
    blocked = (elems // LANES, nodal.shape[0], LANES)
    total_vertices = NV_DEV * lax.axis_size("elem")
    paired = lax.axis_size("elem") % 2 == 0
    group_slots = slots - 2 * CAP_E
    half_group = pltpu.VMEM((group_slots // 2, LANES), f32)
    nodal, metric, derivative, interp, face_level, face_target, slot_mortar, vertex_ids = (
        pltpu.with_memory_space_constraint(array, pltpu.HBM)
        for array in (
            nodal, metric, derivative, interp, face_level, face_target, slot_mortar, vertex_ids
        )
    )
    maps_shape = pltpu.VMEM((4 * SQ, 3 * SQ), bf16)

    (
        near, far, keep, cross, traces, columns, slot_level, maps,
        level, target, slot_row, interp_in, derivative_in, vertex_in,
    ) = pl.pallas_call(
        functools.partial(send_kernel, total_vertices, paired),
        in_specs=[HBM] * 7,
        out_specs=[VMEM] * 14,
        out_shape=[
            pltpu.VMEM((SQ, CAP_E), f32),
            pltpu.VMEM((SQ, CAP_E), f32),
            half_group,
            half_group,
            pltpu.VMEM((2 * SQ + 16, faces), bf16),
            pltpu.VMEM((faces, LANES), jnp.int32),
            pltpu.VMEM((8, slots), f32),
            maps_shape,
            pltpu.VMEM((1, faces), jnp.int32),
            pltpu.VMEM((1, faces), jnp.int32),
            pltpu.VMEM((1, slots), jnp.int32),
            pltpu.VMEM(interp.shape, f32),
            pltpu.VMEM(derivative.shape, f32),
            pltpu.VMEM(vertex_ids.shape, jnp.int32),
        ],
        scratch_shapes=[
            pltpu.VMEM(blocked, f32),
            pltpu.VMEM((group_slots, LANES), f32),
            pltpu.SemaphoreType.DMA((blocked[0],)),
            pltpu.SemaphoreType.DMA((6,)),
        ],
        compiler_params=params(16),
        name="send",
    )(nodal, face_level, face_target, slot_mortar, interp, derivative, vertex_ids)

    near, far = curve_swap(near, far)
    messages = group_swap(keep, cross)

    mortar, local_answers, equal, back_maps, grad_map, div_map, nodal_in, metric_in = pl.pallas_call(
        local_kernel,
        in_specs=[HBM, HBM] + [VMEM] * 7,
        out_specs=[VMEM] * 8,
        out_shape=[
            pltpu.VMEM((SQ, M_DEV), f32),
            pltpu.VMEM((SQ, slots), f32),
            pltpu.VMEM((slots, slots), bf16),
            maps_shape,
            pltpu.VMEM((2 * SQ, 3 * SQ), bf16),
            pltpu.VMEM((SQ, 6 * SQ), bf16),
            pltpu.VMEM(blocked, f32),
            pltpu.VMEM(metric.shape, bf16),
        ],
        scratch_shapes=[pltpu.SemaphoreType.DMA((blocked[0],)), pltpu.SemaphoreType.DMA],
        compiler_params=params(16),
        cost_estimate=cost(3),
        name="local",
    )(nodal, metric, traces, maps, level, columns, slot_row, interp_in, derivative_in)

    near, far, keep, cross, incoming, sums = pl.pallas_call(
        functools.partial(answer_kernel, paired),
        in_specs=[VMEM] * (4 + len(messages)),
        out_specs=[VMEM] * 6,
        out_shape=[
            pltpu.VMEM((SQ + 8, CAP_E), f32),
            pltpu.VMEM((SQ + 8, CAP_E), f32),
            half_group,
            half_group,
            pltpu.VMEM((SQ, slots), f32),
            pltpu.VMEM((16, LANES), f32),
        ],
        scratch_shapes=[pltpu.VMEM((group_slots, LANES), f32)],
        compiler_params=params(16),
        name="answer",
    )(near, far, equal, local_answers, *messages)

    near, far = curve_swap(near, far)
    messages = group_swap(keep, cross)

    result, remote, low_ids, high_ids = pl.pallas_call(
        functools.partial(gather_kernel, total_vertices),
        in_specs=[VMEM] * 11,
        out_specs=[VMEM] * 4,
        out_shape=[
            pltpu.VMEM(blocked, f32),
            pltpu.VMEM((slots, faces), bf16),
            pltpu.VMEM((2 * HALF, 8 * elems), bf16),
            pltpu.VMEM((8, elems), jnp.int32),
        ],
        scratch_shapes=[
            pltpu.VMEM(nodal.shape, f32),
            pltpu.VMEM(nodal.shape, f32),
        ],
        compiler_params=params(16),
        cost_estimate=cost(3),
        name="gather",
    )(
        nodal_in, metric_in, mortar, incoming, slot_row, target, level, back_maps,
        grad_map, div_map, vertex_in,
    )

    return pl.pallas_call(
        functools.partial(final_kernel, paired),
        in_specs=[VMEM] * (9 + len(messages)),
        out_specs=HBM,
        out_shape=jax.ShapeDtypeStruct(nodal.shape, f32),
        scratch_shapes=[
            pltpu.VMEM(blocked, f32),
            pltpu.VMEM((group_slots, LANES), f32),
            pltpu.SemaphoreType.DMA((POINTS // 2 * blocked[0],)),
        ],
        compiler_params=params(16),
        name="final",
    )(
        near, far, slot_level, back_maps, remote, sums, high_ids, low_ids, result, *messages
    )


def solution(mesh):
    in_specs = (
        P(None, ("elem", "clus")),
        P(None, None, ("elem", "clus")),
        P(),
        P(),
        P(("elem", "clus")),
        P(("elem", "clus")),
        P(("elem", "clus")),
        P(None, ("elem", "clus")),
    )
    out_specs = P(None, ("elem", "clus"))
    return jax.shard_map(
        on_device, mesh=mesh, in_specs=in_specs, out_specs=out_specs, check_vma=False
    )
```

```python
import functools

import jax
import jax.numpy as jnp
from jax import lax
from jax.experimental import pallas as pl
from jax.experimental.pallas import tpu as pltpu
from jax.sharding import PartitionSpec as P

POINTS = 8
SQ = POINTS * POINTS
CAP_E = 128
CAP_C = 16
M_DEV = 512
NV_DEV = 256
HALF = 64
LANES = 128
MIB = 1 << 20

f32 = jnp.float32
bf16 = jnp.bfloat16
highest = lax.Precision.HIGHEST


def split(x):
    hi = x.astype(bf16)
    lo = (x - hi.astype(f32)).astype(bf16)
    return hi, lo


def stack3(x, axis=0):
    hi, lo = split(x)
    return jnp.concatenate([hi, lo, hi], axis=axis)


def stack2(x):
    hi, lo = split(x)
    return jnp.concatenate([hi, lo], axis=0)


def mm(a, b):
    return lax.dot_general(a, b, (((1,), (0,)), ((), ())), preferred_element_type=f32)


def mm_nt(a, b):
    return lax.dot_general(a, b, (((1,), (1,)), ((), ())), preferred_element_type=f32)


def iota(shape, dim):
    return lax.broadcasted_iota(jnp.int32, shape, dim)


def expand(matrix, copies):
    width = SQ * copies
    lane = iota((POINTS, width), 1) % SQ
    row = iota((POINTS, width), 0)
    to_first = (lane // POINTS == row).astype(f32)
    to_second = (lane % POINTS == row).astype(f32)
    first = jnp.dot(matrix, to_first, precision=highest, preferred_element_type=f32)
    second = jnp.dot(matrix, to_second, precision=highest, preferred_element_type=f32)
    first = jnp.broadcast_to(first[:, None, :], (POINTS, POINTS, width)).reshape(SQ, width)
    second = jnp.concatenate([second] * POINTS, axis=0)
    return first, second


def hi_hi_lo(matrix):
    hi = matrix.astype(bf16).astype(f32)
    lane = iota(matrix.shape, 1)
    return jnp.where(lane < 2 * SQ, hi, matrix - hi).astype(bf16)


def kron_four(low, high):
    low_first, low_second = expand(low, 3)
    high_first, high_second = expand(high, 3)
    maps = [
        low_first * low_second,
        low_first * high_second,
        high_first * low_second,
        high_first * high_second,
    ]
    return hi_hi_lo(jnp.concatenate(maps, axis=0))


def load_rows(ref, rows):
    return jnp.concatenate([ref[h, rows, :] for h in range(ref.shape[0])], axis=1)


def load_comb(ref, j):
    return jnp.concatenate([load_rows(ref, pl.ds(a * SQ + j * 8, 8)) for a in range(8)], axis=0)


def store_rows(ref, rows, value):
    for h in range(ref.shape[0]):
        ref[h, rows, :] = value[:, h * LANES : (h + 1) * LANES]


def add_rows(ref, rows, value):
    for h in range(ref.shape[0]):
        ref[h, rows, :] += value[:, h * LANES : (h + 1) * LANES]


def lane_copies(hbm, blocks, sems):
    return [
        pltpu.make_async_copy(hbm.at[:, pl.ds(h * LANES, LANES)], blocks.at[h], sems.at[h])
        for h in range(blocks.shape[0])
    ]


def pick_level(plain, mapped, level):
    out = plain
    for number in range(1, 5):
        out = jnp.where(level == number, mapped[(number - 1) * SQ : number * SQ], out)
    return out


def one_hot_rows(ids, first, count):
    return (iota((count, ids.shape[1]), 0) + first == ids).astype(f32).astype(bf16)


def columns_of(row):
    return jnp.broadcast_to(row, (LANES, row.shape[1])).T


def one_hot_lanes(columns, first, count):
    lane = iota((columns.shape[0], LANES), 1) + first
    blocks = [columns == lane + start for start in range(0, count, LANES)]
    return jnp.concatenate([block.astype(f32).astype(bf16) for block in blocks], axis=1)


def window_ids(vertex_ids, elem_index, total):
    shifted = vertex_ids - elem_index * NV_DEV
    window = jnp.where(shifted < 0, shifted + total, shifted)
    return window // HALF, window % HALF


def low_one_hot(low_id):
    parts = []
    for corner in range(8):
        hot = one_hot_rows(low_id[corner : corner + 1], 0, HALF)
        parts.append(jnp.concatenate([jnp.zeros_like(hot), hot], axis=0))
    return jnp.concatenate(parts, axis=1)


def corner_row(corner):
    last = POINTS - 1
    return corner // 4 * last * SQ + corner // 2 % 2 * last * POINTS + corner % 2 * last


def up_goes_near(paired):
    return lax.axis_index("elem") % 2 == 0 if paired else lax.axis_index("elem") >= 0


def up_came_near(paired):
    return lax.axis_index("elem") % 2 == 1 if paired else lax.axis_index("elem") >= 0


def swap_if(flag, first, second):
    return jnp.where(flag, first, second), jnp.where(flag, second, first)


def member_rows(mask):
    member = lax.axis_index("clus")
    same = jnp.bitwise_xor(member, 2 * mask + (mask > 0))
    other = jnp.bitwise_xor(same, 1)
    return pl.ds(pl.multiple_of(same * 16, 16), 16), pl.ds(pl.multiple_of(other * 16, 16), 16)


def chip_masks(chips):
    return [0] + list(range(chips - 1, 0, -1))


def part_group(group_ref, keep_ref, cross_ref):
    for mask in range(group_ref.shape[0] // 32):
        same, other = member_rows(mask)
        keep_ref[mask * 16 : mask * 16 + 16, :] = group_ref[same, :]
        cross_ref[mask * 16 : mask * 16 + 16, :] = group_ref[other, :]


def join_group(message_refs, group_ref):
    for mask, message_ref in zip(chip_masks(len(message_refs)), message_refs):
        same, other = member_rows(mask)
        group_ref[same, :] = message_ref[0:16, :]
        group_ref[other, :] = message_ref[16:32, :]


def merge_kernel(keep_ref, cross_ref, *message_refs):
    upper = iota((16, LANES), 1) >= HALF
    sums = jnp.where(upper, keep_ref[0:16, :] + cross_ref[0:16, :], 0.0)
    for mask, message_ref in enumerate(message_refs):
        block = keep_ref[mask * 16 : mask * 16 + 16, :]
        message_ref[0:16, :] = jnp.where(upper, sums, block)
        message_ref[16:32, :] = cross_ref[mask * 16 : mask * 16 + 16, :]


def send_kernel(
    total_vertices,
    paired,
    nodal_hbm,
    level_hbm,
    target_hbm,
    slot_hbm,
    interp_hbm,
    derivative_hbm,
    vertex_hbm,
    near_ref,
    far_ref,
    keep_ref,
    cross_ref,
    traces_ref,
    columns_ref,
    slot_level_ref,
    maps_ref,
    level_ref,
    target_ref,
    slot_mortar_ref,
    interp_ref,
    derivative_ref,
    vertex_ref,
    nodal_ref,
    group_ref,
    nodal_sems,
    sems,
):
    target_copy = pltpu.make_async_copy(target_hbm, target_ref.at[0], sems.at[0])
    level_copy = pltpu.make_async_copy(level_hbm, level_ref.at[0], sems.at[1])
    interp_copy = pltpu.make_async_copy(interp_hbm, interp_ref, sems.at[2])
    vertex_copy = pltpu.make_async_copy(vertex_hbm, vertex_ref, sems.at[3])
    slot_copy = pltpu.make_async_copy(slot_hbm, slot_mortar_ref.at[0], sems.at[4])
    derivative_copy = pltpu.make_async_copy(derivative_hbm, derivative_ref, sems.at[5])
    nodal_copies = lane_copies(nodal_hbm, nodal_ref, nodal_sems)
    target_copy.start()
    interp_copy.start()
    for copy in nodal_copies:
        copy.start()
    for copy in (level_copy, vertex_copy, slot_copy, derivative_copy):
        copy.start()
    slots = slot_level_ref.shape[1]
    elems = nodal_hbm.shape[1]
    interp_copy.wait()
    maps = kron_four(interp_ref[0], interp_ref[1])
    maps_ref[...] = maps
    target_copy.wait()
    columns = columns_of(target_ref[...])
    columns_ref[...] = columns
    remote = one_hot_lanes(columns, M_DEV, slots)
    vertex_copy.wait()
    high_id, low_id = window_ids(vertex_ref[...], lax.axis_index("elem"), total_vertices)
    low_hot = low_one_hot(low_id)

    for copy in nodal_copies:
        copy.wait()
    level_copy.wait()
    level = level_ref[...]
    faces = [
        load_rows(nodal_ref, pl.ds(0, SQ)),
        load_rows(nodal_ref, pl.ds(7 * SQ, SQ)),
        load_comb(nodal_ref, 0),
        load_comb(nodal_ref, 7),
        load_rows(nodal_ref, pl.ds(0, SQ, stride=8)),
        load_rows(nodal_ref, pl.ds(7, SQ, stride=8)),
    ]
    trace = jnp.concatenate(faces, axis=1)
    hi, lo = split(trace)
    level_rows = jnp.broadcast_to(level, (16, level.shape[1])).astype(f32).astype(bf16)

    traces = jnp.concatenate([hi, lo, level_rows], axis=0)
    traces_ref[...] = traces
    picked = mm(traces, remote)[:, 0:slots]
    plain = picked[0:SQ] + picked[SQ : 2 * SQ]
    slot_level = picked[2 * SQ : 2 * SQ + 8]
    slot_level_ref[...] = slot_level
    sent = pick_level(plain, mm(maps, stack3(plain)), slot_level[0:1])

    row = iota((16, elems), 0)
    row_high = row % 4 + 4 * (row // 8)
    is_count = row // 4 % 2 == 1
    weighted = []
    for corner in range(8):
        value = load_rows(nodal_ref, pl.ds(corner_row(corner), 1))
        value_hi = value.astype(bf16).astype(f32)
        value_lo = value - value_hi
        mine = high_id[corner : corner + 1] == row_high
        first = jnp.where(mine, jnp.where(is_count, 1.0, value_hi), 0.0)
        second = jnp.where(mine & ~is_count, value_lo, 0.0)
        weighted.append(jnp.concatenate([first, second], axis=0).astype(bf16))
    sums = mm_nt(jnp.concatenate(weighted, axis=1), low_hot)
    sums = sums[0:16] + sums[16:32]
    group = sent[:, 2 * CAP_E :]
    group_ref[...] = jnp.concatenate([group, jnp.zeros_like(group)], axis=0).T
    part_group(group_ref, keep_ref, cross_ref)
    keep_ref[0:16, :] += sums
    cross_ref[0:16, :] += sums
    near_ref[...], far_ref[...] = swap_if(
        up_goes_near(paired), sent[:, CAP_E : 2 * CAP_E], sent[:, 0:CAP_E]
    )
    slot_copy.wait()
    derivative_copy.wait()


def stiffness_maps(matrix):
    row = iota((SQ, 3 * SQ), 0)
    lane = iota((SQ, 3 * SQ), 1) % SQ
    first, second = expand(matrix, 3)
    outer = jnp.where(row % 8 == lane % 8, first, 0.0)
    inner = jnp.where(row // 8 == lane // 8, second, 0.0)
    return hi_hi_lo(outer), hi_hi_lo(inner)


def local_kernel(
    nodal_hbm,
    metric_hbm,
    traces_ref,
    maps_ref,
    level_ref,
    columns_ref,
    slot_mortar_ref,
    interp_ref,
    derivative_ref,
    mortar_ref,
    answers_ref,
    equal_ref,
    back_maps_ref,
    grad_map_ref,
    div_map_ref,
    nodal_ref,
    metric_ref,
    nodal_sems,
    sem,
):
    nodal_copies = lane_copies(nodal_hbm, nodal_ref, nodal_sems)
    metric_copy = pltpu.make_async_copy(metric_hbm, metric_ref, sem)
    for copy in nodal_copies:
        copy.start()
    metric_copy.start()
    back_maps_ref[...] = kron_four(interp_ref[0].T, interp_ref[1].T)
    slot_row = slot_mortar_ref[...]
    equal_ref[...] = (columns_of(slot_row)[:, 0:1] == slot_row).astype(f32).astype(bf16)
    hi = traces_ref[0:SQ, :]
    lo = traces_ref[SQ : 2 * SQ, :]
    plain = hi.astype(f32) + lo.astype(f32)
    mapped = mm(maps_ref[...], jnp.concatenate([hi, lo, hi], axis=0))
    projected = pick_level(plain, mapped, level_ref[...])
    mortar = mm(stack2(projected), one_hot_lanes(columns_ref[...], 0, M_DEV))
    mortar = mortar[0:SQ] + mortar[SQ:]
    mortar_ref[...] = mortar
    answers = mm(stack2(mortar), one_hot_rows(slot_row, 0, M_DEV))
    answers_ref[...] = answers[0:SQ] + answers[SQ:]
    outer, inner = stiffness_maps(derivative_ref[...])
    outer_t, inner_t = stiffness_maps(derivative_ref[...].T)
    grad_map_ref[0:SQ, :] = outer
    grad_map_ref[SQ:, :] = inner
    div_map_ref[...] = jnp.concatenate([outer_t, inner_t], axis=1)
    for copy in nodal_copies:
        copy.wait()
    metric_copy.wait()


def first_direction(nodal_ref, metric_ref, outer, outer_t, stiff_ref, by_row):
    for i in range(8):
        by_row[i * SQ : (i + 1) * SQ, :] = metric_ref[i * SQ : (i + 1) * SQ, :].astype(f32)
    grads = [mm(outer, stack3(load_comb(nodal_ref, j))) for j in range(8)]
    weighted = []
    for j in range(8):
        factor = [by_row[i * SQ + j * 8 : i * SQ + j * 8 + 8, :] for i in range(8)]
        weighted.append(stack3(grads[j] * jnp.concatenate(factor, axis=0)))
    for j in range(8):
        out = mm(outer_t, weighted[j])
        for i in range(8):
            stiff_ref[i * SQ + j * 8 : i * SQ + j * 8 + 8, :] = out[i * 8 : i * 8 + 8]


def other_directions(nodal_ref, metric_ref, grad_map, div_map, stiff_ref, result_ref):
    slabs = [pl.ds(i * SQ, SQ) for i in range(8)]
    grads = [mm(grad_map, stack3(load_rows(nodal_ref, slab))) for slab in slabs]
    weighted = []
    for slab, grad in zip(slabs, grads):
        second = stack3(grad[0:SQ] * metric_ref[0, slab, :].astype(f32))
        third = stack3(grad[SQ:] * metric_ref[1, slab, :].astype(f32))
        weighted.append(jnp.concatenate([second, third], axis=0))
    for slab, part in zip(slabs, weighted):
        store_rows(result_ref, slab, stiff_ref[slab, :] + mm(div_map, part))


def answer_kernel(
    paired,
    near_in_ref,
    far_in_ref,
    equal_ref,
    local_answers_ref,
    *refs,
):
    *message_refs, near_ref, far_ref, keep_ref, cross_ref, incoming_ref, sums_ref, group_ref = refs
    join_group(message_refs, group_ref)
    from_up, from_down = swap_if(
        up_came_near(paired), near_in_ref[...], far_in_ref[...]
    )
    incoming = jnp.concatenate([from_up, from_down, group_ref[...].T[0:SQ]], axis=1)
    incoming_ref[...] = incoming
    added = mm(stack2(incoming), equal_ref[...])
    answers = local_answers_ref[...] + added[0:SQ] + added[SQ:]
    group = answers[:, 2 * CAP_E :]
    group_ref[...] = jnp.concatenate([group, jnp.zeros_like(group)], axis=0).T
    part_group(group_ref, keep_ref, cross_ref)
    sums = message_refs[0][0:16, :]
    for message_ref in message_refs[1:]:
        sums = sums + message_ref[0:16, :]
    sums_ref[...] = sums
    down = jnp.concatenate([answers[:, 0:CAP_E], sums[0:8]], axis=0)
    up = jnp.concatenate([answers[:, CAP_E : 2 * CAP_E], sums[8:16]], axis=0)
    near_ref[...], far_ref[...] = swap_if(up_goes_near(paired), up, down)


def gather_kernel(
    total_vertices,
    nodal_ref,
    metric_ref,
    mortar_ref,
    incoming_ref,
    slot_mortar_ref,
    target_ref,
    level_ref,
    back_maps_ref,
    grad_map_ref,
    div_map_ref,
    vertex_ref,
    result_ref,
    remote_ref,
    low_ids_ref,
    high_ids_ref,
    stiff_ref,
    by_row,
):
    first_direction(nodal_ref, metric_ref.at[0], grad_map_ref[0:SQ, :], div_map_ref[:, 0:3 * SQ], stiff_ref, by_row)
    other_directions(
        nodal_ref, metric_ref.at[1:3], grad_map_ref[...], div_map_ref[...], stiff_ref, result_ref
    )
    slot_hot = one_hot_lanes(columns_of(slot_mortar_ref[...]), 0, M_DEV)
    added = mm(stack2(incoming_ref[...]), slot_hot)
    mortar = mortar_ref[...] + added[0:SQ] + added[SQ:]
    target = target_ref[...]
    picked = mm(stack2(mortar), one_hot_rows(target, 0, M_DEV))
    picked = picked[0:SQ] + picked[SQ:]
    back = pick_level(picked, mm(back_maps_ref[...], stack3(picked)), level_ref[...])
    remote_ref[...] = one_hot_rows(target, M_DEV, remote_ref.shape[0])
    high_id, low_id = window_ids(vertex_ref[...], lax.axis_index("elem"), total_vertices)
    high_ids_ref[...] = high_id
    low_ids_ref[...] = low_one_hot(low_id)
    add_faces(result_ref, back)


def add_faces(ref, back):
    elems = ref.shape[0] * LANES
    parts = [back[:, f * elems : (f + 1) * elems] for f in range(6)]
    add_rows(ref, pl.ds(0, SQ), parts[0])
    add_rows(ref, pl.ds(7 * SQ, SQ), parts[1])
    for a in range(8):
        add_rows(ref, pl.ds(a * SQ, 8), parts[2][a * 8 : a * 8 + 8])
        add_rows(ref, pl.ds(a * SQ + 56, 8), parts[3][a * 8 : a * 8 + 8])
    add_rows(ref, pl.ds(0, SQ, stride=8), parts[4])
    add_rows(ref, pl.ds(7, SQ, stride=8), parts[5])


def final_kernel(
    paired,
    near_in_ref,
    far_in_ref,
    slot_level_ref,
    maps_ref,
    remote_ref,
    sums_ref,
    high_ids_ref,
    low_ids_ref,
    result_ref,
    *refs,
):
    *message_refs, out_hbm, out_ref, group_ref, sems = refs
    join_group(message_refs, group_ref)
    from_up, from_down = swap_if(
        up_came_near(paired), near_in_ref[...], far_in_ref[...]
    )
    arrived = jnp.concatenate([from_up[0:SQ], from_down[0:SQ], group_ref[...].T[0:SQ]], axis=1)
    slot_back = pick_level(arrived, mm(maps_ref[...], stack3(arrived)), slot_level_ref[0:1, :])
    back = mm(stack2(slot_back), remote_ref[...])
    back = back[0:SQ] + back[SQ:]

    first = sums_ref[0:8, :] + from_up[SQ:]
    second = sums_ref[8:16, :] + from_down[SQ:]
    totals = jnp.concatenate([first[0:4], second[0:4]], axis=0)
    counts = jnp.concatenate([first[4:8], second[4:8]], axis=0)
    coarse = jnp.where(iota(totals.shape, 1) < HALF, 0.0, totals / (1.0 + counts))
    coarse_hi = coarse.astype(bf16).astype(f32)
    table = jnp.concatenate([coarse_hi, coarse - coarse_hi], axis=0).astype(bf16)
    found = mm(table, low_ids_ref[...])
    found = found[0:8] + found[8:16]
    high_id = high_ids_ref[...]

    elems = out_hbm.shape[1]
    row = iota((8, elems), 0)
    fixes = []
    for corner in range(8):
        mine = row == high_id[corner : corner + 1]
        fix = jnp.where(mine, found[:, corner * elems : (corner + 1) * elems], 0.0)
        fixes.append(jnp.sum(fix, axis=0, keepdims=True))
    parts = [back[:, f * elems : (f + 1) * elems] for f in range(6)]
    copies = []
    for i in range(POINTS):
        rows = slice(i * POINTS, (i + 1) * POINTS)
        slab = load_rows(result_ref, pl.ds(i * SQ, SQ))
        if i in (0, POINTS - 1):
            slab = slab + parts[min(i, 1)]
        pieces = [slab[0:8] + parts[2][rows], slab[8:56], slab[56:64] + parts[3][rows]]
        store_rows(out_ref, pl.ds(i * SQ, SQ), jnp.concatenate(pieces, axis=0))
        add_rows(out_ref, pl.ds(i * SQ, 8, stride=8), parts[4][rows])
        add_rows(out_ref, pl.ds(i * SQ + 7, 8, stride=8), parts[5][rows])
        for corner in range(8):
            if corner_row(corner) // SQ == i:
                add_rows(out_ref, pl.ds(corner_row(corner), 1), fixes[corner])
        if i % 2:
            rows = pl.ds((i - 1) * SQ, 2 * SQ)
            for h in range(out_ref.shape[0]):
                lanes = pl.ds(h * LANES, LANES)
                copies.append(
                    pltpu.make_async_copy(
                        out_ref.at[h, rows], out_hbm.at[rows, lanes], sems.at[len(copies)]
                    )
                )
                copies[-1].start()
    for copy in copies:
        copy.wait()


VMEM = pl.BlockSpec(memory_space=pltpu.VMEM)
HBM = pl.BlockSpec(memory_space=pltpu.HBM)


def params(mib):
    return pltpu.CompilerParams(vmem_limit_bytes=mib * MIB)


def cost(us):
    return pl.CostEstimate(flops=int(us * 5e8), bytes_accessed=int(us * 2e6), transcendentals=0)


def curve_swap(near, far):
    peers = lax.axis_size("elem")
    up = [(i, (i + 1) % peers) for i in range(peers)]
    near_pairs, far_pairs = up, [(j, i) for i, j in up]
    if peers % 2 == 0:
        near_pairs = [(i, i ^ 1) for i in range(peers)]
        far_pairs = [(i, (i + 1 if i % 2 else i - 1) % peers) for i in range(peers)]
    return lax.ppermute(near, "elem", near_pairs), lax.ppermute(far, "elem", far_pairs)


def group_swap(keep, cross):
    members = lax.axis_size("clus")
    chips = members // 2
    cross = lax.ppermute(cross, "clus", [(i, i ^ 1) for i in range(members)])
    messages = pl.pallas_call(
        merge_kernel,
        in_specs=[VMEM] * 2,
        out_specs=[VMEM] * chips,
        out_shape=[pltpu.VMEM((32, LANES), f32)] * chips,
        compiler_params=params(16),
        name="merge",
    )(keep, cross)
    return [messages[0]] + [
        lax.ppermute(messages[mask], "clus", [(i, i ^ (2 * mask + 1)) for i in range(members)])
        for mask in chip_masks(chips)[1:]
    ]


def on_device(nodal, metric, derivative, interp, face_level, face_target, slot_mortar, vertex_ids):
    elems = nodal.shape[1]
    faces = face_level.shape[0]
    slots = slot_mortar.shape[0]
    blocked = (elems // LANES, nodal.shape[0], LANES)
    total_vertices = NV_DEV * lax.axis_size("elem")
    paired = lax.axis_size("elem") % 2 == 0
    group_slots = slots - 2 * CAP_E
    half_group = pltpu.VMEM((group_slots // 2, LANES), f32)
    nodal, metric, derivative, interp, face_level, face_target, slot_mortar, vertex_ids = (
        pltpu.with_memory_space_constraint(array, pltpu.HBM)
        for array in (
            nodal, metric, derivative, interp, face_level, face_target, slot_mortar, vertex_ids
        )
    )
    maps_shape = pltpu.VMEM((4 * SQ, 3 * SQ), bf16)

    (
        near, far, keep, cross, traces, columns, slot_level, maps,
        level, target, slot_row, interp_in, derivative_in, vertex_in,
    ) = pl.pallas_call(
        functools.partial(send_kernel, total_vertices, paired),
        in_specs=[HBM] * 7,
        out_specs=[VMEM] * 14,
        out_shape=[
            pltpu.VMEM((SQ, CAP_E), f32),
            pltpu.VMEM((SQ, CAP_E), f32),
            half_group,
            half_group,
            pltpu.VMEM((2 * SQ + 16, faces), bf16),
            pltpu.VMEM((faces, LANES), jnp.int32),
            pltpu.VMEM((8, slots), f32),
            maps_shape,
            pltpu.VMEM((1, faces), jnp.int32),
            pltpu.VMEM((1, faces), jnp.int32),
            pltpu.VMEM((1, slots), jnp.int32),
            pltpu.VMEM(interp.shape, f32),
            pltpu.VMEM(derivative.shape, f32),
            pltpu.VMEM(vertex_ids.shape, jnp.int32),
        ],
        scratch_shapes=[
            pltpu.VMEM(blocked, f32),
            pltpu.VMEM((group_slots, LANES), f32),
            pltpu.SemaphoreType.DMA((blocked[0],)),
            pltpu.SemaphoreType.DMA((6,)),
        ],
        compiler_params=params(16),
        name="send",
    )(nodal, face_level, face_target, slot_mortar, interp, derivative, vertex_ids)

    near, far = curve_swap(near, far)
    messages = group_swap(keep, cross)

    mortar, local_answers, equal, back_maps, grad_map, div_map, nodal_in, metric_in = pl.pallas_call(
        local_kernel,
        in_specs=[HBM, HBM] + [VMEM] * 7,
        out_specs=[VMEM] * 8,
        out_shape=[
            pltpu.VMEM((SQ, M_DEV), f32),
            pltpu.VMEM((SQ, slots), f32),
            pltpu.VMEM((slots, slots), bf16),
            maps_shape,
            pltpu.VMEM((2 * SQ, 3 * SQ), bf16),
            pltpu.VMEM((SQ, 6 * SQ), bf16),
            pltpu.VMEM(blocked, f32),
            pltpu.VMEM(metric.shape, bf16),
        ],
        scratch_shapes=[pltpu.SemaphoreType.DMA((blocked[0],)), pltpu.SemaphoreType.DMA],
        compiler_params=params(16),
        cost_estimate=cost(3),
        name="local",
    )(nodal, metric, traces, maps, level, columns, slot_row, interp_in, derivative_in)

    near, far, keep, cross, incoming, sums = pl.pallas_call(
        functools.partial(answer_kernel, paired),
        in_specs=[VMEM] * (4 + len(messages)),
        out_specs=[VMEM] * 6,
        out_shape=[
            pltpu.VMEM((SQ + 8, CAP_E), f32),
            pltpu.VMEM((SQ + 8, CAP_E), f32),
            half_group,
            half_group,
            pltpu.VMEM((SQ, slots), f32),
            pltpu.VMEM((16, LANES), f32),
        ],
        scratch_shapes=[pltpu.VMEM((group_slots, LANES), f32)],
        compiler_params=params(16),
        name="answer",
    )(near, far, equal, local_answers, *messages)

    near, far = curve_swap(near, far)
    messages = group_swap(keep, cross)

    result, remote, low_ids, high_ids = pl.pallas_call(
        functools.partial(gather_kernel, total_vertices),
        in_specs=[VMEM] * 11,
        out_specs=[VMEM] * 4,
        out_shape=[
            pltpu.VMEM(blocked, f32),
            pltpu.VMEM((slots, faces), bf16),
            pltpu.VMEM((2 * HALF, 8 * elems), bf16),
            pltpu.VMEM((8, elems), jnp.int32),
        ],
        scratch_shapes=[
            pltpu.VMEM(nodal.shape, f32),
            pltpu.VMEM(nodal.shape, f32),
        ],
        compiler_params=params(16),
        cost_estimate=cost(3),
        name="gather",
    )(
        nodal_in, metric_in, mortar, incoming, slot_row, target, level, back_maps,
        grad_map, div_map, vertex_in,
    )

    return pl.pallas_call(
        functools.partial(final_kernel, paired),
        in_specs=[VMEM] * (9 + len(messages)),
        out_specs=HBM,
        out_shape=jax.ShapeDtypeStruct(nodal.shape, f32),
        scratch_shapes=[
            pltpu.VMEM(blocked, f32),
            pltpu.VMEM((group_slots, LANES), f32),
            pltpu.SemaphoreType.DMA((POINTS // 2 * blocked[0],)),
        ],
        compiler_params=params(16),
        name="final",
    )(
        near, far, slot_level, back_maps, remote, sums, high_ids, low_ids, result, *messages
    )


def solution(mesh):
    in_specs = (
        P(None, ("elem", "clus")),
        P(None, None, ("elem", "clus")),
        P(),
        P(),
        P(("elem", "clus")),
        P(("elem", "clus")),
        P(("elem", "clus")),
        P(None, ("elem", "clus")),
    )
    out_specs = P(None, ("elem", "clus"))
    return jax.shard_map(
        on_device, mesh=mesh, in_specs=in_specs, out_specs=out_specs, check_vma=False
    )
```

```python
import functools

import jax
import jax.numpy as jnp
from jax import lax
from jax.experimental import pallas as pl
from jax.experimental.pallas import tpu as pltpu
from jax.sharding import PartitionSpec as P

POINTS = 8
SQ = POINTS * POINTS
CAP_E = 128
CAP_C = 16
M_DEV = 512
NV_DEV = 256
HALF = 64
LANES = 128
MIB = 1 << 20

f32 = jnp.float32
bf16 = jnp.bfloat16
highest = lax.Precision.HIGHEST


def split(x):
    hi = x.astype(bf16)
    lo = (x - hi.astype(f32)).astype(bf16)
    return hi, lo


def stack3(x, axis=0):
    hi, lo = split(x)
    return jnp.concatenate([hi, lo, hi], axis=axis)


def stack2(x):
    hi, lo = split(x)
    return jnp.concatenate([hi, lo], axis=0)


def mm(a, b):
    return lax.dot_general(a, b, (((1,), (0,)), ((), ())), preferred_element_type=f32)


def mm_nt(a, b):
    return lax.dot_general(a, b, (((1,), (1,)), ((), ())), preferred_element_type=f32)


def iota(shape, dim):
    return lax.broadcasted_iota(jnp.int32, shape, dim)


def expand(matrix, copies):
    width = SQ * copies
    lane = iota((POINTS, width), 1) % SQ
    row = iota((POINTS, width), 0)
    to_first = (lane // POINTS == row).astype(f32)
    to_second = (lane % POINTS == row).astype(f32)
    first = jnp.dot(matrix, to_first, precision=highest, preferred_element_type=f32)
    second = jnp.dot(matrix, to_second, precision=highest, preferred_element_type=f32)
    first = jnp.broadcast_to(first[:, None, :], (POINTS, POINTS, width)).reshape(SQ, width)
    second = jnp.concatenate([second] * POINTS, axis=0)
    return first, second


def hi_hi_lo(matrix):
    hi = matrix.astype(bf16).astype(f32)
    lane = iota(matrix.shape, 1)
    return jnp.where(lane < 2 * SQ, hi, matrix - hi).astype(bf16)


def kron_four(low, high):
    low_first, low_second = expand(low, 3)
    high_first, high_second = expand(high, 3)
    maps = [
        low_first * low_second,
        low_first * high_second,
        high_first * low_second,
        high_first * high_second,
    ]
    return hi_hi_lo(jnp.concatenate(maps, axis=0))


def load_rows(ref, rows):
    return jnp.concatenate([ref[h, rows, :] for h in range(ref.shape[0])], axis=1)


def load_comb(ref, j):
    return jnp.concatenate([load_rows(ref, pl.ds(a * SQ + j * 8, 8)) for a in range(8)], axis=0)


def store_rows(ref, rows, value):
    for h in range(ref.shape[0]):
        ref[h, rows, :] = value[:, h * LANES : (h + 1) * LANES]


def add_rows(ref, rows, value):
    for h in range(ref.shape[0]):
        ref[h, rows, :] += value[:, h * LANES : (h + 1) * LANES]


def lane_copies(hbm, blocks, sems):
    return [
        pltpu.make_async_copy(hbm.at[:, pl.ds(h * LANES, LANES)], blocks.at[h], sems.at[h])
        for h in range(blocks.shape[0])
    ]


def pick_level(plain, mapped, level):
    out = plain
    for number in range(1, 5):
        out = jnp.where(level == number, mapped[(number - 1) * SQ : number * SQ], out)
    return out


def one_hot_rows(ids, first, count):
    return (iota((count, ids.shape[1]), 0) + first == ids).astype(f32).astype(bf16)


def columns_of(row):
    return jnp.broadcast_to(row, (LANES, row.shape[1])).T


def one_hot_lanes(columns, first, count):
    lane = iota((columns.shape[0], LANES), 1) + first
    blocks = [columns == lane + start for start in range(0, count, LANES)]
    return jnp.concatenate([block.astype(f32).astype(bf16) for block in blocks], axis=1)


def window_ids(vertex_ids, elem_index, total):
    shifted = vertex_ids - elem_index * NV_DEV
    window = jnp.where(shifted < 0, shifted + total, shifted)
    return window // HALF, window % HALF


def low_one_hot(low_id):
    parts = []
    for corner in range(8):
        hot = one_hot_rows(low_id[corner : corner + 1], 0, HALF)
        parts.append(jnp.concatenate([jnp.zeros_like(hot), hot], axis=0))
    return jnp.concatenate(parts, axis=1)


def corner_row(corner):
    last = POINTS - 1
    return corner // 4 * last * SQ + corner // 2 % 2 * last * POINTS + corner % 2 * last


def up_goes_near(paired):
    return lax.axis_index("elem") % 2 == 0 if paired else lax.axis_index("elem") >= 0


def up_came_near(paired):
    return lax.axis_index("elem") % 2 == 1 if paired else lax.axis_index("elem") >= 0


def swap_if(flag, first, second):
    return jnp.where(flag, first, second), jnp.where(flag, second, first)


def member_rows(mask):
    member = lax.axis_index("clus")
    same = jnp.bitwise_xor(member, 2 * mask + (mask > 0))
    other = jnp.bitwise_xor(same, 1)
    return pl.ds(pl.multiple_of(same * 16, 16), 16), pl.ds(pl.multiple_of(other * 16, 16), 16)


def chip_masks(chips):
    return [0, chips - 1] + list(range(1, chips - 1))


def part_group(group_ref, keep_ref, cross_ref):
    for mask in range(group_ref.shape[0] // 32):
        same, other = member_rows(mask)
        keep_ref[mask * 16 : mask * 16 + 16, :] = group_ref[same, :]
        cross_ref[mask * 16 : mask * 16 + 16, :] = group_ref[other, :]


def join_group(message_refs, group_ref):
    for mask, message_ref in zip(chip_masks(len(message_refs)), message_refs):
        same, other = member_rows(mask)
        group_ref[same, :] = message_ref[0:16, :]
        group_ref[other, :] = message_ref[16:32, :]


def merge_kernel(keep_ref, cross_ref, *message_refs):
    upper = iota((16, LANES), 1) >= HALF
    sums = jnp.where(upper, keep_ref[0:16, :] + cross_ref[0:16, :], 0.0)
    for mask, message_ref in enumerate(message_refs):
        block = keep_ref[mask * 16 : mask * 16 + 16, :]
        message_ref[0:16, :] = jnp.where(upper, sums, block)
        message_ref[16:32, :] = cross_ref[mask * 16 : mask * 16 + 16, :]


def send_kernel(
    total_vertices,
    paired,
    nodal_hbm,
    level_hbm,
    target_hbm,
    slot_hbm,
    interp_hbm,
    derivative_hbm,
    vertex_hbm,
    near_ref,
    far_ref,
    keep_ref,
    cross_ref,
    traces_ref,
    columns_ref,
    slot_level_ref,
    maps_ref,
    level_ref,
    target_ref,
    slot_mortar_ref,
    interp_ref,
    derivative_ref,
    vertex_ref,
    nodal_ref,
    group_ref,
    nodal_sems,
    sems,
):
    target_copy = pltpu.make_async_copy(target_hbm, target_ref.at[0], sems.at[0])
    level_copy = pltpu.make_async_copy(level_hbm, level_ref.at[0], sems.at[1])
    interp_copy = pltpu.make_async_copy(interp_hbm, interp_ref, sems.at[2])
    vertex_copy = pltpu.make_async_copy(vertex_hbm, vertex_ref, sems.at[3])
    slot_copy = pltpu.make_async_copy(slot_hbm, slot_mortar_ref.at[0], sems.at[4])
    derivative_copy = pltpu.make_async_copy(derivative_hbm, derivative_ref, sems.at[5])
    nodal_copies = lane_copies(nodal_hbm, nodal_ref, nodal_sems)
    target_copy.start()
    interp_copy.start()
    for copy in nodal_copies:
        copy.start()
    for copy in (level_copy, vertex_copy, slot_copy, derivative_copy):
        copy.start()
    slots = slot_level_ref.shape[1]
    elems = nodal_hbm.shape[1]
    interp_copy.wait()
    maps = kron_four(interp_ref[0], interp_ref[1])
    maps_ref[...] = maps
    target_copy.wait()
    columns = columns_of(target_ref[...])
    columns_ref[...] = columns
    remote = one_hot_lanes(columns, M_DEV, slots)
    vertex_copy.wait()
    high_id, low_id = window_ids(vertex_ref[...], lax.axis_index("elem"), total_vertices)
    low_hot = low_one_hot(low_id)

    for copy in nodal_copies:
        copy.wait()
    level_copy.wait()
    level = level_ref[...]
    faces = [
        load_rows(nodal_ref, pl.ds(0, SQ)),
        load_rows(nodal_ref, pl.ds(7 * SQ, SQ)),
        load_comb(nodal_ref, 0),
        load_comb(nodal_ref, 7),
        load_rows(nodal_ref, pl.ds(0, SQ, stride=8)),
        load_rows(nodal_ref, pl.ds(7, SQ, stride=8)),
    ]
    trace = jnp.concatenate(faces, axis=1)
    hi, lo = split(trace)
    level_rows = jnp.broadcast_to(level, (16, level.shape[1])).astype(f32).astype(bf16)

    traces = jnp.concatenate([hi, lo, level_rows], axis=0)
    traces_ref[...] = traces
    picked = mm(traces, remote)[:, 0:slots]
    plain = picked[0:SQ] + picked[SQ : 2 * SQ]
    slot_level = picked[2 * SQ : 2 * SQ + 8]
    slot_level_ref[...] = slot_level
    sent = pick_level(plain, mm(maps, stack3(plain)), slot_level[0:1])

    row = iota((16, elems), 0)
    row_high = row % 4 + 4 * (row // 8)
    is_count = row // 4 % 2 == 1
    weighted = []
    for corner in range(8):
        value = load_rows(nodal_ref, pl.ds(corner_row(corner), 1))
        value_hi = value.astype(bf16).astype(f32)
        value_lo = value - value_hi
        mine = high_id[corner : corner + 1] == row_high
        first = jnp.where(mine, jnp.where(is_count, 1.0, value_hi), 0.0)
        second = jnp.where(mine & ~is_count, value_lo, 0.0)
        weighted.append(jnp.concatenate([first, second], axis=0).astype(bf16))
    sums = mm_nt(jnp.concatenate(weighted, axis=1), low_hot)
    sums = sums[0:16] + sums[16:32]
    group = sent[:, 2 * CAP_E :]
    group_ref[...] = jnp.concatenate([group, jnp.zeros_like(group)], axis=0).T
    part_group(group_ref, keep_ref, cross_ref)
    keep_ref[0:16, :] += sums
    cross_ref[0:16, :] += sums
    near_ref[...], far_ref[...] = swap_if(
        up_goes_near(paired), sent[:, CAP_E : 2 * CAP_E], sent[:, 0:CAP_E]
    )
    slot_copy.wait()
    derivative_copy.wait()


def stiffness_maps(matrix):
    row = iota((SQ, 3 * SQ), 0)
    lane = iota((SQ, 3 * SQ), 1) % SQ
    first, second = expand(matrix, 3)
    outer = jnp.where(row % 8 == lane % 8, first, 0.0)
    inner = jnp.where(row // 8 == lane // 8, second, 0.0)
    return hi_hi_lo(outer), hi_hi_lo(inner)


def local_kernel(
    nodal_hbm,
    metric_hbm,
    traces_ref,
    maps_ref,
    level_ref,
    columns_ref,
    slot_mortar_ref,
    interp_ref,
    derivative_ref,
    mortar_ref,
    answers_ref,
    equal_ref,
    back_maps_ref,
    grad_map_ref,
    div_map_ref,
    nodal_ref,
    metric_ref,
    nodal_sems,
    sem,
):
    nodal_copies = lane_copies(nodal_hbm, nodal_ref, nodal_sems)
    metric_copy = pltpu.make_async_copy(metric_hbm, metric_ref, sem)
    for copy in nodal_copies:
        copy.start()
    metric_copy.start()
    back_maps_ref[...] = kron_four(interp_ref[0].T, interp_ref[1].T)
    slot_row = slot_mortar_ref[...]
    equal_ref[...] = (columns_of(slot_row)[:, 0:1] == slot_row).astype(f32).astype(bf16)
    hi = traces_ref[0:SQ, :]
    lo = traces_ref[SQ : 2 * SQ, :]
    plain = hi.astype(f32) + lo.astype(f32)
    mapped = mm(maps_ref[...], jnp.concatenate([hi, lo, hi], axis=0))
    projected = pick_level(plain, mapped, level_ref[...])
    mortar = mm(stack2(projected), one_hot_lanes(columns_ref[...], 0, M_DEV))
    mortar = mortar[0:SQ] + mortar[SQ:]
    mortar_ref[...] = mortar
    answers = mm(stack2(mortar), one_hot_rows(slot_row, 0, M_DEV))
    answers_ref[...] = answers[0:SQ] + answers[SQ:]
    outer, inner = stiffness_maps(derivative_ref[...])
    outer_t, inner_t = stiffness_maps(derivative_ref[...].T)
    grad_map_ref[0:SQ, :] = outer
    grad_map_ref[SQ:, :] = inner
    div_map_ref[...] = jnp.concatenate([outer_t, inner_t], axis=1)
    for copy in nodal_copies:
        copy.wait()
    metric_copy.wait()


def first_direction(nodal_ref, metric_ref, outer, outer_t, stiff_ref, by_row):
    for i in range(8):
        by_row[i * SQ : (i + 1) * SQ, :] = metric_ref[i * SQ : (i + 1) * SQ, :].astype(f32)
    grads = [mm(outer, stack3(load_comb(nodal_ref, j))) for j in range(8)]
    weighted = []
    for j in range(8):
        factor = [by_row[i * SQ + j * 8 : i * SQ + j * 8 + 8, :] for i in range(8)]
        weighted.append(stack3(grads[j] * jnp.concatenate(factor, axis=0)))
    for j in range(8):
        out = mm(outer_t, weighted[j])
        for i in range(8):
            stiff_ref[i * SQ + j * 8 : i * SQ + j * 8 + 8, :] = out[i * 8 : i * 8 + 8]


def other_directions(nodal_ref, metric_ref, grad_map, div_map, stiff_ref, result_ref):
    slabs = [pl.ds(i * SQ, SQ) for i in range(8)]
    grads = [mm(grad_map, stack3(load_rows(nodal_ref, slab))) for slab in slabs]
    weighted = []
    for slab, grad in zip(slabs, grads):
        second = stack3(grad[0:SQ] * metric_ref[0, slab, :].astype(f32))
        third = stack3(grad[SQ:] * metric_ref[1, slab, :].astype(f32))
        weighted.append(jnp.concatenate([second, third], axis=0))
    for slab, part in zip(slabs, weighted):
        store_rows(result_ref, slab, stiff_ref[slab, :] + mm(div_map, part))


def answer_kernel(
    paired,
    near_in_ref,
    far_in_ref,
    equal_ref,
    local_answers_ref,
    *refs,
):
    *message_refs, near_ref, far_ref, keep_ref, cross_ref, incoming_ref, sums_ref, group_ref = refs
    join_group(message_refs, group_ref)
    from_up, from_down = swap_if(
        up_came_near(paired), near_in_ref[...], far_in_ref[...]
    )
    incoming = jnp.concatenate([from_up, from_down, group_ref[...].T[0:SQ]], axis=1)
    incoming_ref[...] = incoming
    added = mm(stack2(incoming), equal_ref[...])
    answers = local_answers_ref[...] + added[0:SQ] + added[SQ:]
    group = answers[:, 2 * CAP_E :]
    group_ref[...] = jnp.concatenate([group, jnp.zeros_like(group)], axis=0).T
    part_group(group_ref, keep_ref, cross_ref)
    sums = message_refs[0][0:16, :]
    for message_ref in message_refs[1:]:
        sums = sums + message_ref[0:16, :]
    sums_ref[...] = sums
    down = jnp.concatenate([answers[:, 0:CAP_E], sums[0:8]], axis=0)
    up = jnp.concatenate([answers[:, CAP_E : 2 * CAP_E], sums[8:16]], axis=0)
    near_ref[...], far_ref[...] = swap_if(up_goes_near(paired), up, down)


def gather_kernel(
    total_vertices,
    nodal_ref,
    metric_ref,
    mortar_ref,
    incoming_ref,
    slot_mortar_ref,
    target_ref,
    level_ref,
    back_maps_ref,
    grad_map_ref,
    div_map_ref,
    vertex_ref,
    result_ref,
    remote_ref,
    low_ids_ref,
    high_ids_ref,
    stiff_ref,
    by_row,
):
    first_direction(nodal_ref, metric_ref.at[0], grad_map_ref[0:SQ, :], div_map_ref[:, 0:3 * SQ], stiff_ref, by_row)
    other_directions(
        nodal_ref, metric_ref.at[1:3], grad_map_ref[...], div_map_ref[...], stiff_ref, result_ref
    )
    slot_hot = one_hot_lanes(columns_of(slot_mortar_ref[...]), 0, M_DEV)
    added = mm(stack2(incoming_ref[...]), slot_hot)
    mortar = mortar_ref[...] + added[0:SQ] + added[SQ:]
    target = target_ref[...]
    picked = mm(stack2(mortar), one_hot_rows(target, 0, M_DEV))
    picked = picked[0:SQ] + picked[SQ:]
    back = pick_level(picked, mm(back_maps_ref[...], stack3(picked)), level_ref[...])
    remote_ref[...] = one_hot_rows(target, M_DEV, remote_ref.shape[0])
    high_id, low_id = window_ids(vertex_ref[...], lax.axis_index("elem"), total_vertices)
    high_ids_ref[...] = high_id
    low_ids_ref[...] = low_one_hot(low_id)
    add_faces(result_ref, back)


def add_faces(ref, back):
    elems = ref.shape[0] * LANES
    parts = [back[:, f * elems : (f + 1) * elems] for f in range(6)]
    add_rows(ref, pl.ds(0, SQ), parts[0])
    add_rows(ref, pl.ds(7 * SQ, SQ), parts[1])
    for a in range(8):
        add_rows(ref, pl.ds(a * SQ, 8), parts[2][a * 8 : a * 8 + 8])
        add_rows(ref, pl.ds(a * SQ + 56, 8), parts[3][a * 8 : a * 8 + 8])
    add_rows(ref, pl.ds(0, SQ, stride=8), parts[4])
    add_rows(ref, pl.ds(7, SQ, stride=8), parts[5])


def final_kernel(
    paired,
    near_in_ref,
    far_in_ref,
    slot_level_ref,
    maps_ref,
    remote_ref,
    sums_ref,
    high_ids_ref,
    low_ids_ref,
    result_ref,
    *refs,
):
    *message_refs, out_hbm, out_ref, group_ref, sems = refs
    join_group(message_refs, group_ref)
    from_up, from_down = swap_if(
        up_came_near(paired), near_in_ref[...], far_in_ref[...]
    )
    arrived = jnp.concatenate([from_up[0:SQ], from_down[0:SQ], group_ref[...].T[0:SQ]], axis=1)
    slot_back = pick_level(arrived, mm(maps_ref[...], stack3(arrived)), slot_level_ref[0:1, :])
    back = mm(stack2(slot_back), remote_ref[...])
    back = back[0:SQ] + back[SQ:]

    first = sums_ref[0:8, :] + from_up[SQ:]
    second = sums_ref[8:16, :] + from_down[SQ:]
    totals = jnp.concatenate([first[0:4], second[0:4]], axis=0)
    counts = jnp.concatenate([first[4:8], second[4:8]], axis=0)
    coarse = jnp.where(iota(totals.shape, 1) < HALF, 0.0, totals / (1.0 + counts))
    coarse_hi = coarse.astype(bf16).astype(f32)
    table = jnp.concatenate([coarse_hi, coarse - coarse_hi], axis=0).astype(bf16)
    found = mm(table, low_ids_ref[...])
    found = found[0:8] + found[8:16]
    high_id = high_ids_ref[...]

    elems = out_hbm.shape[1]
    row = iota((8, elems), 0)
    fixes = []
    for corner in range(8):
        mine = row == high_id[corner : corner + 1]
        fix = jnp.where(mine, found[:, corner * elems : (corner + 1) * elems], 0.0)
        fixes.append(jnp.sum(fix, axis=0, keepdims=True))
    parts = [back[:, f * elems : (f + 1) * elems] for f in range(6)]
    copies = []
    for i in range(POINTS):
        rows = slice(i * POINTS, (i + 1) * POINTS)
        slab = load_rows(result_ref, pl.ds(i * SQ, SQ))
        if i in (0, POINTS - 1):
            slab = slab + parts[min(i, 1)]
        pieces = [slab[0:8] + parts[2][rows], slab[8:56], slab[56:64] + parts[3][rows]]
        store_rows(out_ref, pl.ds(i * SQ, SQ), jnp.concatenate(pieces, axis=0))
        add_rows(out_ref, pl.ds(i * SQ, 8, stride=8), parts[4][rows])
        add_rows(out_ref, pl.ds(i * SQ + 7, 8, stride=8), parts[5][rows])
        for corner in range(8):
            if corner_row(corner) // SQ == i:
                add_rows(out_ref, pl.ds(corner_row(corner), 1), fixes[corner])
        if i % 2:
            rows = pl.ds((i - 1) * SQ, 2 * SQ)
            for h in range(out_ref.shape[0]):
                lanes = pl.ds(h * LANES, LANES)
                copies.append(
                    pltpu.make_async_copy(
                        out_ref.at[h, rows], out_hbm.at[rows, lanes], sems.at[len(copies)]
                    )
                )
                copies[-1].start()
    for copy in copies:
        copy.wait()


VMEM = pl.BlockSpec(memory_space=pltpu.VMEM)
HBM = pl.BlockSpec(memory_space=pltpu.HBM)


def params(mib):
    return pltpu.CompilerParams(vmem_limit_bytes=mib * MIB)


def cost(us):
    return pl.CostEstimate(flops=int(us * 5e8), bytes_accessed=int(us * 2e6), transcendentals=0)


def curve_swap(near, far):
    peers = lax.axis_size("elem")
    up = [(i, (i + 1) % peers) for i in range(peers)]
    near_pairs, far_pairs = up, [(j, i) for i, j in up]
    if peers % 2 == 0:
        near_pairs = [(i, i ^ 1) for i in range(peers)]
        far_pairs = [(i, (i + 1 if i % 2 else i - 1) % peers) for i in range(peers)]
    return lax.ppermute(near, "elem", near_pairs), lax.ppermute(far, "elem", far_pairs)


def group_swap(keep, cross):
    members = lax.axis_size("clus")
    chips = members // 2
    cross = lax.ppermute(cross, "clus", [(i, i ^ 1) for i in range(members)])
    messages = pl.pallas_call(
        merge_kernel,
        in_specs=[VMEM] * 2,
        out_specs=[VMEM] * chips,
        out_shape=[pltpu.VMEM((32, LANES), f32)] * chips,
        compiler_params=params(16),
        name="merge",
    )(keep, cross)
    return [messages[0]] + [
        lax.ppermute(messages[mask], "clus", [(i, i ^ (2 * mask + 1)) for i in range(members)])
        for mask in chip_masks(chips)[1:]
    ]


def on_device(nodal, metric, derivative, interp, face_level, face_target, slot_mortar, vertex_ids):
    elems = nodal.shape[1]
    faces = face_level.shape[0]
    slots = slot_mortar.shape[0]
    blocked = (elems // LANES, nodal.shape[0], LANES)
    total_vertices = NV_DEV * lax.axis_size("elem")
    paired = lax.axis_size("elem") % 2 == 0
    group_slots = slots - 2 * CAP_E
    half_group = pltpu.VMEM((group_slots // 2, LANES), f32)
    nodal, metric, derivative, interp, face_level, face_target, slot_mortar, vertex_ids = (
        pltpu.with_memory_space_constraint(array, pltpu.HBM)
        for array in (
            nodal, metric, derivative, interp, face_level, face_target, slot_mortar, vertex_ids
        )
    )
    maps_shape = pltpu.VMEM((4 * SQ, 3 * SQ), bf16)

    (
        near, far, keep, cross, traces, columns, slot_level, maps,
        level, target, slot_row, interp_in, derivative_in, vertex_in,
    ) = pl.pallas_call(
        functools.partial(send_kernel, total_vertices, paired),
        in_specs=[HBM] * 7,
        out_specs=[VMEM] * 14,
        out_shape=[
            pltpu.VMEM((SQ, CAP_E), f32),
            pltpu.VMEM((SQ, CAP_E), f32),
            half_group,
            half_group,
            pltpu.VMEM((2 * SQ + 16, faces), bf16),
            pltpu.VMEM((faces, LANES), jnp.int32),
            pltpu.VMEM((8, slots), f32),
            maps_shape,
            pltpu.VMEM((1, faces), jnp.int32),
            pltpu.VMEM((1, faces), jnp.int32),
            pltpu.VMEM((1, slots), jnp.int32),
            pltpu.VMEM(interp.shape, f32),
            pltpu.VMEM(derivative.shape, f32),
            pltpu.VMEM(vertex_ids.shape, jnp.int32),
        ],
        scratch_shapes=[
            pltpu.VMEM(blocked, f32),
            pltpu.VMEM((group_slots, LANES), f32),
            pltpu.SemaphoreType.DMA((blocked[0],)),
            pltpu.SemaphoreType.DMA((6,)),
        ],
        compiler_params=params(16),
        name="send",
    )(nodal, face_level, face_target, slot_mortar, interp, derivative, vertex_ids)

    near, far = curve_swap(near, far)
    messages = group_swap(keep, cross)

    mortar, local_answers, equal, back_maps, grad_map, div_map, nodal_in, metric_in = pl.pallas_call(
        local_kernel,
        in_specs=[HBM, HBM] + [VMEM] * 7,
        out_specs=[VMEM] * 8,
        out_shape=[
            pltpu.VMEM((SQ, M_DEV), f32),
            pltpu.VMEM((SQ, slots), f32),
            pltpu.VMEM((slots, slots), bf16),
            maps_shape,
            pltpu.VMEM((2 * SQ, 3 * SQ), bf16),
            pltpu.VMEM((SQ, 6 * SQ), bf16),
            pltpu.VMEM(blocked, f32),
            pltpu.VMEM(metric.shape, bf16),
        ],
        scratch_shapes=[pltpu.SemaphoreType.DMA((blocked[0],)), pltpu.SemaphoreType.DMA],
        compiler_params=params(16),
        cost_estimate=cost(3),
        name="local",
    )(nodal, metric, traces, maps, level, columns, slot_row, interp_in, derivative_in)

    near, far, keep, cross, incoming, sums = pl.pallas_call(
        functools.partial(answer_kernel, paired),
        in_specs=[VMEM] * (4 + len(messages)),
        out_specs=[VMEM] * 6,
        out_shape=[
            pltpu.VMEM((SQ + 8, CAP_E), f32),
            pltpu.VMEM((SQ + 8, CAP_E), f32),
            half_group,
            half_group,
            pltpu.VMEM((SQ, slots), f32),
            pltpu.VMEM((16, LANES), f32),
        ],
        scratch_shapes=[pltpu.VMEM((group_slots, LANES), f32)],
        compiler_params=params(16),
        name="answer",
    )(near, far, equal, local_answers, *messages)

    near, far = curve_swap(near, far)
    messages = group_swap(keep, cross)

    result, remote, low_ids, high_ids = pl.pallas_call(
        functools.partial(gather_kernel, total_vertices),
        in_specs=[VMEM] * 11,
        out_specs=[VMEM] * 4,
        out_shape=[
            pltpu.VMEM(blocked, f32),
            pltpu.VMEM((slots, faces), bf16),
            pltpu.VMEM((2 * HALF, 8 * elems), bf16),
            pltpu.VMEM((8, elems), jnp.int32),
        ],
        scratch_shapes=[
            pltpu.VMEM(nodal.shape, f32),
            pltpu.VMEM(nodal.shape, f32),
        ],
        compiler_params=params(16),
        cost_estimate=cost(3),
        name="gather",
    )(
        nodal_in, metric_in, mortar, incoming, slot_row, target, level, back_maps,
        grad_map, div_map, vertex_in,
    )

    return pl.pallas_call(
        functools.partial(final_kernel, paired),
        in_specs=[VMEM] * (9 + len(messages)),
        out_specs=HBM,
        out_shape=jax.ShapeDtypeStruct(nodal.shape, f32),
        scratch_shapes=[
            pltpu.VMEM(blocked, f32),
            pltpu.VMEM((group_slots, LANES), f32),
            pltpu.SemaphoreType.DMA((POINTS // 2 * blocked[0],)),
        ],
        compiler_params=params(16),
        name="final",
    )(
        near, far, slot_level, back_maps, remote, sums, high_ids, low_ids, result, *messages
    )


def solution(mesh):
    in_specs = (
        P(None, ("elem", "clus")),
        P(None, None, ("elem", "clus")),
        P(),
        P(),
        P(("elem", "clus")),
        P(("elem", "clus")),
        P(("elem", "clus")),
        P(None, ("elem", "clus")),
    )
    out_specs = P(None, ("elem", "clus"))
    return jax.shard_map(
        on_device, mesh=mesh, in_specs=in_specs, out_specs=out_specs, check_vma=False
    )
```
